128 devices in a mesh: band: 16 (over y, z), shard: 8 (over x, core).
Axes of the slice: x: 4, y: 4, z: 4, core: 2. Of those that a mesh axis runs over, the one named last changes fastest.
Arguments:
- grid_input: bfloat16 [1024, 512, 474], P('band', 'shard'), may hold values from -6 to 6
- w_stem: bfloat16 [9, 474, 512], replicated, may hold values from -0.09375 to 0.09375
- b_stem: float32 [512], replicated, may hold values from -3 to 3
- w_edge: bfloat16 [512, 512], replicated, may hold values from -0.25 to 0.25
- w_node: bfloat16 [512, 512], replicated, may hold values from -0.25 to 0.25
- src_index: int32 [128, 128, 16], P(('band', 'shard')), may hold values from 0 to 1023
- dst_index: int32 [128, 128, 16], P(('band', 'shard')), may hold values from 0 to 319
- counts: int32 [128, 128], P(('band', 'shard')), may hold values from 0 to 16, as said below
- mesh_cotangent: bfloat16 [40960, 512], P(('band', 'shard')), may hold values from -0.119628906 to 0.119628906
Outputs:
- mesh_out: bfloat16 [40960, 512], P(('band', 'shard'))
- grad_stem: float32 [9, 474, 512], replicated
- grad_bias: float32 [512], replicated
- grad_edge: float32 [512, 512], replicated
- grad_node: float32 [512, 512], replicated
The draws below stay inside these ranges and needn't reach their ends.
Inputs may be any that keep to these rules, and one draw needn't show every extreme that they name: counts[q, r] of the 16 slots of each block are used; 16 is reached, and some destination owner receives 16 from every sender.
All inputs are finite; a program needn't handle non-finite values.
Results may differ from the reference program's by a relative error of at most 0.0066.
Values may be sent and summed in bfloat16 or wider, within the bound.
No kernel may reach another device: no remote copies, remote signals or barrier semaphores. Data moves between devices by JAX's collectives and lax.ppermute only.
A program may use at most 128 MiB of HBM per device.

```python
import jax
import jax.numpy as jnp
from jax import lax

C = 474
L = 512
ROWS_DEV = 64
COLS_DEV = 64
CAP = 16
MESH_DEV = 320
NLAT = 1024
NLON = 512
POINTS_DEV = 1024
DEVICES_ALL = 128
MESH = 40960
N_BAND = 16
N_SHARD = 8


def draw_counts(key, part):
    key = jax.random.fold_in(key, 11)
    device_count = N_BAND * N_SHARD
    first_key, second_key, third_key = jax.random.split(key, 3)
    ceiling = jax.random.randint(first_key, (1, device_count), CAP // 2, CAP + 1)
    filled = jax.random.randint(second_key, (device_count, device_count), ceiling // 2, ceiling + 1)
    full_owner = jax.random.randint(third_key, (), 0, device_count)
    owners = jnp.arange(device_count, dtype=jnp.int32)[None, :]
    filled = jnp.where(owners == full_owner, CAP, filled)
    return filled.astype(jnp.int32)


def plant(entries, key, least, top_value):
    index_at = [jax.random.randint(jax.random.fold_in(key, axis), (), 0, length) for axis, length in enumerate(entries.shape)]
    main_axis = entries.shape.index(max(entries.shape))
    next_to = index_at[:main_axis] + [(index_at[main_axis] + 1) % entries.shape[main_axis]] + index_at[main_axis + 1:]
    return entries.at[tuple(index_at)].set(least).at[tuple(next_to)].set(top_value)


def shard_levels(key, extent, pieces, low, high):
    def one(position, parts):
        heights = jax.random.uniform(jax.random.fold_in(jax.random.fold_in(key, 6), position), (parts,), jnp.float32, low / len(pieces), high / len(pieces))
        return jnp.repeat(jnp.exp(heights), extent[position] // parts).reshape((-1,) + (1,) * (len(extent) - position - 1))

    gain = one(*pieces[0])
    for cut in pieces[1:]:
        gain = gain * one(*cut)
    return gain


def normal_values(rng, extent, width, bound, shards=(), held_as=jnp.bfloat16):
    entries = width * jax.random.normal(rng, extent, jnp.float32)
    if shards:
        entries = entries * shard_levels(rng, extent, shards, -0.22, 0.18)
    return jnp.clip(entries, -bound, bound).astype(held_as)


def setup_inputs(seed: int = 0) -> dict:
    seeds = jax.random.split(jax.random.key(seed), 10)
    grid_input = normal_values(seeds[0], (NLAT, NLON, C), 1.0, 6.0, ((0, 16), (1, 8)))
    w_stem = normal_values(seeds[1], (9, C, L), (9 * C) ** -0.5, 0.09375)
    b_stem = normal_values(seeds[2], (L,), 0.5, 3.0, (), jnp.float32)
    w_edge = normal_values(seeds[3], (L, L), L ** -0.5, 0.25)
    w_node = normal_values(seeds[4], (L, L), L ** -0.5, 0.25)
    src_index = plant(jax.random.randint(seeds[5], (DEVICES_ALL, DEVICES_ALL, CAP), 0, POINTS_DEV), jax.random.fold_in(seeds[5], 1), 0, POINTS_DEV - 1).astype(jnp.int32)
    dst_index = plant(jax.random.randint(seeds[6], (DEVICES_ALL, DEVICES_ALL, CAP), 0, MESH_DEV), jax.random.fold_in(seeds[6], 1), 0, MESH_DEV - 1).astype(jnp.int32)
    counts = draw_counts(jax.random.fold_in(seeds[9], 71), 0)
    mesh_cotangent = normal_values(seeds[8], (MESH, L), 0.02, 0.119628906, ((0, 128),))
    return {"grid_input": grid_input, "w_stem": w_stem, "b_stem": b_stem, "w_edge": w_edge, "w_node": w_node, "src_index": src_index, "dst_index": dst_index, "counts": counts, "mesh_cotangent": mesh_cotangent}


def silu_grad(values):
    sigmoid = jax.nn.sigmoid(values)
    return sigmoid * (1.0 + values * (1.0 - sigmoid))

def reference(grid_input, w_stem, b_stem, w_edge, w_node, src_index, dst_index, counts, mesh_cotangent):
    lat_count, lon_count, channels = grid_input.shape
    latent_width = w_edge.shape[0]
    device_count = N_BAND * N_SHARD
    half_rows = ROWS_DEV // 2
    half_cols = COLS_DEV // 2
    points = half_rows * half_cols
    slot_count = src_index.shape[2]
    widened = jnp.concatenate([grid_input[:, -1:, :], grid_input], axis=1)
    extended = jnp.concatenate([jnp.zeros((1, lon_count + 1, channels), grid_input.dtype), widened], axis=0)
    tap_list = [extended[row_tap:row_tap + lat_count:2, col_tap:col_tap + lon_count:2, :] for row_tap in range(3) for col_tap in range(3)]
    patches = jnp.concatenate(tap_list, axis=2).reshape(-1, 9 * channels)
    stem_pre = jnp.dot(patches, w_stem.reshape(9 * channels, latent_width), preferred_element_type=jnp.float32) + b_stem
    latent = jax.nn.silu(stem_pre).astype(jnp.bfloat16)
    blocks = latent.reshape(N_BAND, half_rows, N_SHARD, half_cols, latent_width)
    blocks = blocks.transpose(0, 2, 1, 3, 4).reshape(device_count, points, latent_width)
    slot_live = jnp.arange(slot_count, dtype=jnp.int32)[None, None, :] < counts[:, :, None]
    flat_src = src_index.reshape(device_count, device_count * slot_count)
    taken = jax.vmap(lambda block, picks: jnp.take(block, picks, axis=0))(blocks, flat_src)
    taken = taken.reshape(device_count, device_count, slot_count, latent_width)
    rows = jnp.where(slot_live[:, :, :, None], taken, jnp.zeros_like(taken))
    rows_flat = rows.reshape(-1, latent_width)
    edge_pre = jnp.dot(rows_flat, w_edge, preferred_element_type=jnp.float32)
    messages = jax.nn.silu(edge_pre).astype(jnp.bfloat16)
    owner_ids = jnp.arange(device_count, dtype=jnp.int32)[:, None, None] * MESH_DEV + dst_index
    node_ids = owner_ids.transpose(1, 0, 2).reshape(-1)
    aggregate = jnp.zeros((MESH_DEV * device_count, latent_width), jnp.float32).at[node_ids].add(messages.astype(jnp.float32))
    aggregate = aggregate.astype(jnp.bfloat16)
    mesh_out = jnp.dot(aggregate, w_node, preferred_element_type=jnp.float32).astype(jnp.bfloat16)
    grad_agg = jnp.dot(mesh_cotangent, w_node.T, preferred_element_type=jnp.float32).astype(jnp.bfloat16)
    grad_node = jnp.dot(aggregate.T, mesh_cotangent, preferred_element_type=jnp.float32)
    grad_msg = jnp.take(grad_agg, node_ids, axis=0).astype(jnp.float32)
    grad_pre = (grad_msg * silu_grad(edge_pre)).astype(jnp.bfloat16)
    grad_edge = jnp.dot(rows_flat.T, grad_pre, preferred_element_type=jnp.float32)
    grad_rows = jnp.dot(grad_pre, w_edge.T, preferred_element_type=jnp.float32).astype(jnp.bfloat16)
    masked = grad_rows.astype(jnp.float32) * slot_live.reshape(-1, 1).astype(jnp.float32)
    point_ids = (jnp.arange(device_count, dtype=jnp.int32)[:, None, None] * points + src_index).reshape(-1)
    grad_latent = jnp.zeros((device_count * points, latent_width), jnp.float32).at[point_ids].add(masked)
    grad_latent = grad_latent.reshape(N_BAND, N_SHARD, half_rows, half_cols, latent_width)
    grad_latent = grad_latent.transpose(0, 2, 1, 3, 4).reshape(-1, latent_width)
    grad_stemout = (grad_latent * silu_grad(stem_pre)).astype(jnp.bfloat16)
    grad_stem = jnp.dot(patches.T, grad_stemout, preferred_element_type=jnp.float32).reshape(9, channels, latent_width)
    grad_bias = lax.optimization_barrier(jnp.sum(grad_stemout.astype(jnp.float32), axis=0))
    return (mesh_out, grad_stem, grad_bias, grad_edge, grad_node)
```

```python
import jax
import jax.numpy as jnp
from jax import lax
from jax.sharding import Mesh, PartitionSpec as P

CHIPS = ("band", "chip")
PAD = 512


def passed_along(array, axis, by):
    size = lax.axis_size(axis)
    return lax.ppermute(array, axis, [(i, (i + by) % size) for i in range(size)])


def from_behind(array, axis, by):
    size = lax.axis_size(axis)
    pairs = [(i, i + by) for i in range(size) if 0 <= i + by < size]
    return lax.ppermute(array, axis, pairs)


def core_swap(array):
    return lax.ppermute(array, "core", [(0, 1), (1, 0)])


def silu_grad(values):
    sigmoid = jax.nn.sigmoid(values)
    return sigmoid * (1.0 + values * (1.0 - sigmoid))


def inner_dot(first, second):
    return lax.dot_general(
        first, second, (((0,), (0,)), ((), ())), preferred_element_type=jnp.float32
    )


def right_dot(first, second):
    return lax.dot_general(
        first, second, (((1,), (1,)), ((), ())), preferred_element_type=jnp.float32
    )


def phase_taps(row_phase, col_phase):
    return [
        (row_tap, col_tap)
        for row_tap in range(3)
        for col_tap in range(3)
        if row_tap % 2 == row_phase and col_tap % 2 == col_phase
    ]


def shards(
    grid_input, w_stem, b_stem, w_edge, w_node, src_index, dst_index, counts, mesh_cotangent
):
    rows_here, cols_here, channels = grid_input.shape
    latent_width = w_edge.shape[0]
    chips = lax.axis_size("band") * lax.axis_size("chip")
    core = lax.axis_index("core")
    device_count = 2 * chips
    slot_count = src_index.shape[2]
    half_rows = rows_here // 2
    half_cols = cols_here // 2
    half_width = latent_width // 2
    node_total = mesh_cotangent.shape[0]

    dst_pairs = dst_index.reshape(chips, 2, slot_count)
    dst_mine = lax.dynamic_index_in_dim(dst_pairs, core, 1, keepdims=False)
    dst_sent = lax.dynamic_index_in_dim(dst_pairs, 1 - core, 1, keepdims=False)
    dst_other = core_swap(dst_sent)
    grad_agg = right_dot(mesh_cotangent, w_node).astype(jnp.bfloat16)
    grad_agg_other = core_swap(grad_agg)

    west_column = passed_along(grid_input[:, -1:, :], ("chip", "core"), 1)
    widened = jnp.concatenate([west_column, grid_input], axis=1)
    north_row = from_behind(widened[-1:, :, :], "band", 1)
    extended = jnp.concatenate([north_row, widened], axis=0)
    extended = jnp.pad(extended, ((0, 1), (0, 1), (0, 0)))
    phased = extended.reshape(half_rows + 1, 2, half_cols + 1, 2, channels)
    phase_list = []
    for row_phase in range(2):
        for col_phase in range(2):
            phase_list.append((row_phase, col_phase, phased[:, row_phase, :, col_phase, :]))
    stem_pre = jnp.zeros((half_rows, half_cols, latent_width), jnp.float32)
    for row_phase, col_phase, piece in phase_list:
        taps = phase_taps(row_phase, col_phase)
        kernels = jnp.concatenate(
            [w_stem[3 * row_tap + col_tap] for row_tap, col_tap in taps], axis=1
        )
        product = jnp.einsum("ijc,cl->ijl", piece, kernels, preferred_element_type=jnp.float32)
        for order, (row_tap, col_tap) in enumerate(taps):
            row_start = row_tap // 2
            col_start = col_tap // 2
            stem_pre = (
                stem_pre
                + product[
                    row_start : row_start + half_rows,
                    col_start : col_start + half_cols,
                    order * latent_width : (order + 1) * latent_width,
                ]
            )
    stem_pre = (stem_pre + b_stem).reshape(-1, latent_width)
    latent = jax.nn.silu(stem_pre).astype(jnp.bfloat16)
    points = latent.shape[0]
    flat_src = src_index.reshape(device_count, slot_count)
    slot_live = jnp.arange(slot_count, dtype=jnp.int32)[None, :] < counts.reshape(device_count, 1)
    source = jnp.where(slot_live, flat_src, -1).reshape(-1)
    pick = (source[:, None] == jnp.arange(points, dtype=jnp.int32)[None, :]).astype(jnp.bfloat16)
    outgoing = jnp.dot(pick, latent, preferred_element_type=jnp.float32).astype(jnp.bfloat16)
    outgoing = outgoing.reshape(chips, 2 * slot_count, latent_width)
    incoming = lax.all_to_all(outgoing, CHIPS, split_axis=0, concat_axis=0, tiled=True)

    by_owner = incoming.reshape(chips, 2, slot_count, latent_width).transpose(1, 0, 2, 3)
    arrived = by_owner.reshape(2, chips * slot_count, latent_width)
    owner = jnp.arange(2, dtype=jnp.int32)
    is_mine = owner == core
    dst_both = jnp.where(
        is_mine[:, None], dst_mine.reshape(1, -1), dst_other.reshape(1, -1)
    )
    agg_both = jnp.where(is_mine[:, None, None], grad_agg[None], grad_agg_other[None])
    edge_pre = jnp.einsum("jel,lk->jek", arrived, w_edge, preferred_element_type=jnp.float32)
    node_ids = jnp.arange(node_total, dtype=jnp.int32)
    onehot = (node_ids[None, :, None] == dst_both[:, None, :]).astype(jnp.bfloat16)
    grad_msg = jnp.einsum("jne,jnl->jel", onehot, agg_both, preferred_element_type=jnp.float32)
    grad_pre = (grad_msg * silu_grad(edge_pre)).astype(jnp.bfloat16)
    grad_rows = jnp.einsum("jek,lk->jel", grad_pre, w_edge, preferred_element_type=jnp.float32)
    grad_rows = grad_rows.astype(jnp.bfloat16).reshape(2, chips, slot_count, latent_width)
    grad_rows = grad_rows.transpose(1, 0, 2, 3).reshape(chips, 2 * slot_count, latent_width)
    returned = lax.all_to_all(grad_rows, CHIPS, split_axis=0, concat_axis=0, tiled=True)
    returned = returned.reshape(-1, latent_width)

    messages = jax.nn.silu(edge_pre).astype(jnp.bfloat16)
    partial = jnp.einsum("jne,jel->jnl", onehot, messages, preferred_element_type=jnp.float32)
    partial_mine = lax.dynamic_index_in_dim(partial, core, 0, keepdims=False)
    partial_sent = lax.dynamic_index_in_dim(partial, 1 - core, 0, keepdims=False)
    aggregate = (partial_mine + core_swap(partial_sent)).astype(jnp.bfloat16)
    mesh_out = jnp.dot(aggregate, w_node, preferred_element_type=jnp.float32).astype(jnp.bfloat16)
    grad_node = inner_dot(aggregate, mesh_cotangent)
    grad_edge = inner_dot(arrived.reshape(-1, latent_width), grad_pre.reshape(-1, latent_width))

    source_pick = jnp.arange(points, dtype=jnp.int32)[:, None] == source[None, :]
    grad_latent = jnp.dot(
        source_pick.astype(jnp.bfloat16), returned, preferred_element_type=jnp.float32
    )
    grad_stemout = (grad_latent * silu_grad(stem_pre)).astype(jnp.bfloat16)
    grad_grid = grad_stemout.reshape(half_rows, half_cols, latent_width)
    tap_grads = {}
    for row_phase, col_phase, piece in phase_list:
        taps = phase_taps(row_phase, col_phase)
        placed = [
            jnp.pad(
                grad_grid,
                ((row_tap // 2, 1 - row_tap // 2), (col_tap // 2, 1 - col_tap // 2), (0, 0)),
            )
            for row_tap, col_tap in taps
        ]
        stacked = jnp.concatenate(placed, axis=2)
        contracted = jnp.einsum("ijc,ijl->cl", piece, stacked, preferred_element_type=jnp.float32)
        for order, (row_tap, col_tap) in enumerate(taps):
            tap_grads[3 * row_tap + col_tap] = contracted[
                :, order * latent_width : (order + 1) * latent_width
            ]
    local_bias = jnp.sum(grad_stemout.astype(jnp.float32), axis=0, keepdims=True)
    gap = jnp.zeros((PAD - channels - 1, latent_width), jnp.float32)
    blocks = []
    for number in range(9):
        blocks += [tap_grads[number], local_bias if number == 0 else jnp.zeros_like(local_bias), gap]
    blocks += [grad_edge, grad_node]
    local = jnp.concatenate(blocks, axis=0).astype(jnp.bfloat16)
    total_rows = local.shape[0]

    halves = [local[:, :half_width], local[:, half_width:]]
    sent = jnp.where(core == 0, halves[1], halves[0])
    kept = jnp.where(core == 0, halves[0], halves[1])
    chip_sum = (kept.astype(jnp.float32) + core_swap(sent).astype(jnp.float32)).astype(jnp.bfloat16)
    chunk = total_rows // chips
    pieces = lax.all_to_all(
        chip_sum.reshape(chips, chunk, half_width), CHIPS, split_axis=0, concat_axis=0, tiled=True
    )
    summed = jnp.sum(pieces.astype(jnp.float32), axis=0).astype(jnp.bfloat16)
    spread = jnp.broadcast_to(summed[None], (chips, chunk, half_width))
    gathered = lax.all_to_all(spread, CHIPS, split_axis=0, concat_axis=0, tiled=True)
    gathered = gathered.reshape(total_rows, half_width)
    gathered_other = core_swap(gathered)
    left = jnp.where(core == 0, gathered, gathered_other)
    right = jnp.where(core == 0, gathered_other, gathered)
    whole = jnp.concatenate([left, right], axis=1).astype(jnp.float32)
    stem_part = whole[: 9 * PAD].reshape(9, PAD, latent_width)
    return (
        mesh_out,
        stem_part[:, :channels],
        stem_part[0, channels],
        whole[9 * PAD : 9 * PAD + latent_width],
        whole[9 * PAD + latent_width :],
    )


def solution(mesh):
    bands, columns = mesh.devices.shape
    fine = Mesh(mesh.devices.reshape(bands, columns // 2, 2), ("band", "chip", "core"))
    every = ("band", "chip", "core")
    in_specs = (
        P("band", ("chip", "core"), None),
        P(),
        P(),
        P(),
        P(),
        P(every, None, None),
        P(every, None, None),
        P(every, None),
        P(every, None),
    )
    out_specs = (P(every, None), P(), P(), P(), P())
    return jax.shard_map(shards, mesh=fine, in_specs=in_specs, out_specs=out_specs, check_vma=False)
```

```python
import functools

import jax
import jax.numpy as jnp
from jax import lax
from jax.experimental import pallas as pl
from jax.experimental.pallas import tpu as pltpu
from jax.sharding import Mesh, PartitionSpec as P

CHIPS = ("band", "chip")
EVERY = ("band", "chip", "core")
TAPS = 9
VMEM_LIMIT = 52 * 1024 * 1024


def f32_dot(first, second):
    return jnp.dot(first, second, preferred_element_type=jnp.float32)


def inner_dot(first, second):
    return lax.dot_general(
        first, second, (((0,), (0,)), ((), ())), preferred_element_type=jnp.float32
    )


def right_dot(first, second):
    return lax.dot_general(
        first, second, (((1,), (1,)), ((), ())), preferred_element_type=jnp.float32
    )


def core_swap(array):
    return lax.ppermute(array, "core", [(0, 1), (1, 0)])


def whole(memory=pltpu.VMEM):
    return pl.BlockSpec(memory_space=memory)


def params(**more):
    return pltpu.CompilerParams(vmem_limit_bytes=VMEM_LIMIT, **more)


def column_picker(image_rows, cols, parts):
    half = cols // 2
    shape = (3 * image_rows * half, image_rows * cols)
    out = lax.broadcasted_iota(jnp.int32, shape, 0)
    inside = lax.broadcasted_iota(jnp.int32, shape, 1)
    per_tap = image_rows * half
    tap = out // per_tap
    rest = out - tap * per_tap
    line = rest // half
    col = 2 * (rest - line * half) + tap - 1
    if parts == 2:
        pairs = image_rows // 2
        parity = line // pairs
        line = 2 * (line - parity * pairs) + parity
    hit = (col >= 0) & (inside == line * cols + col)
    return jnp.where(hit, 1.0, 0.0).astype(jnp.bfloat16)


def stem_kernel(
    grid_hbm, west_ref, north_ref, corner_ref, picker_ref, north_picker_ref, w_hbm, bias_ref,
    source_ref, even_hbm, odd_hbm, slope_ref, out_ref,
    grid, weights, even, odd, latent, in_sems, w_sem, out_sems,
):
    rows, cols, channels = grid.shape
    half_rows, half_cols = rows // 2, cols // 2
    width = even.shape[-1]
    chunks = in_sems.shape[0]
    per_chunk = rows // chunks

    def load(chunk):
        part = pl.ds(chunk * per_chunk, per_chunk)
        return pltpu.make_async_copy(grid_hbm.at[part], grid.at[part], in_sems.at[chunk])

    for chunk in range(chunks):
        load(chunk).start()
    w_copy = pltpu.make_async_copy(w_hbm, weights, w_sem)
    w_copy.start()

    tail = width - 128
    even[:, :, :, tail:] = jnp.zeros((3, half_rows, half_cols, 128), jnp.bfloat16)
    odd[:, :, :, tail:] = jnp.zeros((3, half_rows + 1, half_cols, 128), jnp.bfloat16)
    picker = picker_ref[...]
    north = f32_dot(north_picker_ref[...], north_ref[0]).astype(jnp.bfloat16)
    for tap in range(3):
        odd[tap, 0, :, :channels] = north[tap * half_cols : (tap + 1) * half_cols]

    for chunk in range(chunks):
        load(chunk).wait()

        @pl.loop(chunk * per_chunk // 4, (chunk + 1) * per_chunk // 4)
        def _(group):
            block = grid[pl.ds(4 * group, 4)].reshape(4 * cols, channels)
            picked = f32_dot(picker, block).astype(jnp.bfloat16)
            picked = picked.reshape(3, 2, 2, half_cols, channels)
            for tap in range(3):
                even[tap, pl.ds(2 * group, 2), :, :channels] = picked[tap, 0]
                odd[tap, pl.ds(2 * group + 1, 2), :, :channels] = picked[tap, 1]

    def patch(target, first, count, column):
        old = target[0, first : first + count, 0:16, :channels].astype(jnp.float32)
        line = lax.broadcasted_iota(jnp.int32, old.shape, 1)
        new = jnp.where(line == 0, column.astype(jnp.float32), old)
        target[0, first : first + count, 0:16, :channels] = new.astype(jnp.bfloat16)

    patch(even, 0, half_rows, west_ref[:, 0])
    patch(odd, 1, half_rows, west_ref[:, 1])
    patch(odd, 0, 1, corner_ref[...])
    even_copy = pltpu.make_async_copy(even, even_hbm, out_sems.at[0])
    odd_copy = pltpu.make_async_copy(odd, odd_hbm, out_sems.at[1])
    even_copy.start()
    odd_copy.start()

    w_copy.wait()
    tile_rows = 8
    tile = tile_rows * half_cols

    @pl.loop(0, half_rows // tile_rows)
    def _(step):
        first = step * tile_rows
        pieces = []
        for row_tap in range(3):
            for col_tap in range(3):
                if row_tap == 1:
                    piece = even[col_tap, pl.ds(first, tile_rows)]
                else:
                    piece = odd[col_tap, pl.ds(first + row_tap // 2, tile_rows)]
                pieces.append(piece.reshape(tile, width))
        pre = f32_dot(jnp.concatenate(pieces, axis=1), weights[...]) + bias_ref[...]
        sigmoid = jax.nn.sigmoid(pre)
        here = pl.ds(pl.multiple_of(step * tile, tile), tile)
        slope_ref[here] = sigmoid * (1.0 + pre * (1.0 - sigmoid))
        latent[here] = (pre * sigmoid).astype(jnp.bfloat16)

    points = latent.shape[0]
    slots = out_ref.shape[0]

    @pl.loop(0, slots // 256)
    def _(step):
        here = pl.ds(pl.multiple_of(step * 256, 256), 256)
        point = lax.broadcasted_iota(jnp.int32, (256, points), 1)
        pick = jnp.where(point == source_ref[here], 1.0, 0.0).astype(jnp.bfloat16)
        out_ref[here] = f32_dot(pick, latent[...]).astype(jnp.bfloat16)

    even_copy.wait()
    odd_copy.wait()


def flip_kernel(channels, even_ref, odd_ref, out_ref):
    number = pl.program_id(0)
    row_tap = number // 3
    col_tap = number % 3
    half_rows, half_cols, width = even_ref.shape[1:]

    def write(values):
        flipped = values.reshape(half_rows * half_cols, width).T
        line = lax.broadcasted_iota(jnp.int32, flipped.shape, 0)
        ones = (line == channels) & (number == 0)
        out_ref[0] = jnp.where(ones, 1.0, flipped.astype(jnp.float32)).astype(jnp.bfloat16)

    @pl.when(row_tap == 1)
    def _():
        write(even_ref[col_tap])

    @pl.when(row_tap != 1)
    def _():
        write(odd_ref[col_tap, pl.ds(row_tap // 2, half_rows)])


def edge_kernel(rows_ref, w_ref, dst_ref, agg_ref, back_ref, message_ref, grad_ref):
    nodes = agg_ref.shape[0]
    tile = rows_ref.shape[0]
    weights = w_ref[...]
    pre = f32_dot(rows_ref[...], weights)
    node = lax.broadcasted_iota(jnp.int32, (tile, nodes), 1)
    pick = jnp.where(node == dst_ref[...], 1.0, 0.0).astype(jnp.bfloat16)
    grad_msg = f32_dot(pick, agg_ref[...])
    sigmoid = jax.nn.sigmoid(pre)
    message_ref[...] = (pre * sigmoid).astype(jnp.bfloat16)
    grad_pre = (grad_msg * (sigmoid * (1.0 + pre * (1.0 - sigmoid)))).astype(jnp.bfloat16)
    grad_ref[...] = grad_pre
    back_ref[...] = right_dot(grad_pre, weights).astype(jnp.bfloat16)


def sent_kernel(
    half_ref, patches_ref, small_ref, returned_ref, source_ref, slope_ref, out_ref, stemout_ref
):
    number = pl.program_id(0)
    points, width = stemout_ref.shape
    slots = returned_ref.shape[0]
    half_width = out_ref.shape[-1]

    @pl.when(number == 0)
    def _():
        @pl.loop(0, points // 256)
        def _(step):
            first = pl.multiple_of(step * 256, 256)
            here = pl.ds(first, 256)
            point = lax.broadcasted_iota(jnp.int32, (256, slots), 0) + first
            pick = jnp.where(point == source_ref[...], 1.0, 0.0).astype(jnp.bfloat16)
            grad_latent = f32_dot(pick, returned_ref[...])
            stemout_ref[here] = (grad_latent * slope_ref[here]).astype(jnp.bfloat16)

    columns = pl.ds(pl.multiple_of(half_ref[0] * half_width, half_width), half_width)

    @pl.when(number < TAPS)
    def _():
        out_ref[0] = f32_dot(patches_ref[0], stemout_ref[:, columns]).astype(out_ref.dtype)

    @pl.when(number >= TAPS)
    def _():
        out_ref[0] = small_ref[0, :, columns].astype(out_ref.dtype)


def kept_kernel(half_ref, patches_ref, small_ref, stemout_ref, out_ref):
    number = pl.program_id(0)
    half_width = out_ref.shape[-1]
    columns = pl.ds(pl.multiple_of(half_ref[0] * half_width, half_width), half_width)

    @pl.when(number < TAPS)
    def _():
        out_ref[0] = f32_dot(patches_ref[0], stemout_ref[:, columns])

    @pl.when(number >= TAPS)
    def _():
        out_ref[0] = small_ref[0, :, columns]


def final_kernel(core_ref, mine_ref, other_ref, stem_ref, bias_ref, edge_ref, node_ref):
    number = pl.program_id(0)
    channels = stem_ref.shape[1]
    half_width = mine_ref.shape[-1]
    mine = mine_ref[0].astype(jnp.float32)
    other = other_ref[0].astype(jnp.float32)
    first = core_ref[0] == 0
    left = jnp.where(first, mine, other)
    right = jnp.where(first, other, mine)

    @pl.when(number < TAPS)
    def _():
        stem_ref[0, :, :half_width] = left[:channels]
        stem_ref[0, :, half_width:] = right[:channels]

    @pl.when(number == 0)
    def _():
        bias_ref[:, :half_width] = left[channels : channels + 1]
        bias_ref[:, half_width:] = right[channels : channels + 1]

    @pl.when(number == TAPS)
    def _():
        edge_ref[:, :half_width] = left
        edge_ref[:, half_width:] = right

    @pl.when(number == TAPS + 1)
    def _():
        node_ref[:, :half_width] = left
        node_ref[:, half_width:] = right


def shards(
    grid_input, w_stem, b_stem, w_edge, w_node, src_index, dst_index, counts, mesh_cotangent
):
    rows_here, cols_here, channels = grid_input.shape
    width = w_edge.shape[0]
    bands = lax.axis_size("band")
    columns = lax.axis_size("chip") * 2
    chips = bands * lax.axis_size("chip")
    core = lax.axis_index("core")
    device_count = 2 * chips
    slot_count = src_index.shape[2]
    slots = device_count * slot_count
    half_rows = rows_here // 2
    half_cols = cols_here // 2
    points = half_rows * half_cols
    half_width = width // 2
    node_total = mesh_cotangent.shape[0]
    bf16, f32 = jnp.bfloat16, jnp.float32

    west = lax.ppermute(
        grid_input[:, -1:, :], ("chip", "core"), [(i, (i + 1) % columns) for i in range(columns)]
    )
    north = lax.ppermute(grid_input[-1:], "band", [(i, i + 1) for i in range(bands - 1)])
    corner = lax.ppermute(
        grid_input[-1:, -1:],
        EVERY,
        [
            (i * columns + j, (i + 1) * columns + (j + 1) % columns)
            for i in range(bands - 1)
            for j in range(columns)
        ],
    )
    w_flat = jnp.pad(w_stem, ((0, 0), (0, width - channels), (0, 0))).reshape(TAPS * width, width)
    flat_src = src_index.reshape(device_count, slot_count)
    slot_live = jnp.arange(slot_count, dtype=jnp.int32)[None, :] < counts.reshape(device_count, 1)
    source = jnp.where(slot_live, flat_src, -1)

    even, odd, slope, outgoing = pl.pallas_call(
        stem_kernel,
        out_shape=(
            jax.ShapeDtypeStruct((3, half_rows, half_cols, width), bf16),
            jax.ShapeDtypeStruct((3, half_rows + 1, half_cols, width), bf16),
            jax.ShapeDtypeStruct((points, width), f32),
            jax.ShapeDtypeStruct((slots, width), bf16),
        ),
        in_specs=[
            whole(pl.ANY), whole(), whole(), whole(), whole(), whole(), whole(pl.ANY), whole(), whole(),
        ],
        out_specs=(whole(pl.ANY), whole(pl.ANY), whole(), whole()),
        scratch_shapes=[
            pltpu.VMEM((rows_here, cols_here, channels), bf16),
            pltpu.VMEM((TAPS * width, width), bf16),
            pltpu.VMEM((3, half_rows, half_cols, width), bf16),
            pltpu.VMEM((3, half_rows + 1, half_cols, width), bf16),
            pltpu.VMEM((points, width), bf16),
            pltpu.SemaphoreType.DMA((4,)),
            pltpu.SemaphoreType.DMA,
            pltpu.SemaphoreType.DMA((2,)),
        ],
        compiler_params=params(),
        name="stem",
    )(
        grid_input,
        west.reshape(half_rows, 2, 1, channels),
        north,
        corner,
        column_picker(4, cols_here, 2),
        column_picker(1, cols_here, 1),
        w_flat,
        b_stem.reshape(1, width),
        source.reshape(slots, 1),
    )

    incoming = lax.all_to_all(
        outgoing.reshape(device_count, slot_count, width), EVERY, split_axis=0, concat_axis=0, tiled=True
    )
    arrived = incoming.reshape(slots, width)

    patches = pl.pallas_call(
        functools.partial(flip_kernel, channels),
        grid=(TAPS,),
        out_shape=jax.ShapeDtypeStruct((TAPS, width, points), bf16),
        in_specs=[
            pl.BlockSpec((3, half_rows, half_cols, width), lambda t: (0, 0, 0, 0)),
            pl.BlockSpec((3, half_rows + 1, half_cols, width), lambda t: (0, 0, 0, 0)),
        ],
        out_specs=pl.BlockSpec((1, width, points), lambda t: (t, 0, 0)),
        compiler_params=params(),
        cost_estimate=pl.CostEstimate(flops=0, bytes_accessed=16 * 1024 * 1024, transcendentals=0),
        name="flip",
    )(even, odd)
    grad_agg = right_dot(mesh_cotangent, w_node).astype(bf16)
    dst_flat = dst_index.reshape(slots)

    tile = 256
    by_tile = pl.BlockSpec((tile, width), lambda i: (i, 0))
    back, messages, grad_pre = pl.pallas_call(
        edge_kernel,
        grid=(slots // tile,),
        out_shape=(jax.ShapeDtypeStruct((slots, width), bf16),) * 3,
        in_specs=[
            by_tile,
            pl.BlockSpec((width, width), lambda i: (0, 0)),
            pl.BlockSpec((tile, 1), lambda i: (i, 0)),
            pl.BlockSpec((node_total, width), lambda i: (0, 0)),
        ],
        out_specs=(by_tile,) * 3,
        compiler_params=params(),
        name="edge",
    )(arrived, w_edge, dst_flat.reshape(slots, 1), grad_agg)

    returned = lax.all_to_all(
        back.reshape(device_count, slot_count, width), EVERY, split_axis=0, concat_axis=0, tiled=True
    ).reshape(slots, width)

    node_ids = jnp.arange(node_total, dtype=jnp.int32)
    onehot = (node_ids[:, None] == dst_flat[None, :]).astype(bf16)
    aggregate = f32_dot(onehot, messages).astype(bf16)
    mesh_out = f32_dot(aggregate, w_node).astype(bf16)
    grad_node = inner_dot(aggregate, mesh_cotangent)
    grad_edge = inner_dot(arrived, grad_pre)
    small = jnp.stack([grad_edge, grad_node])

    blocks = TAPS + 2
    other_half = (1 - core).reshape(1)
    own_half = core.reshape(1)
    by_tap = pl.BlockSpec((1, width, points), lambda t, h: (jnp.minimum(t, TAPS - 1), 0, 0))
    by_small = pl.BlockSpec((1, width, width), lambda t, h: (jnp.maximum(t - TAPS, 0), 0, 0))
    by_block = pl.BlockSpec((1, width, half_width), lambda t, h: (t, 0, 0))
    fixed = lambda shape: pl.BlockSpec(shape, lambda t, h: (0,) * len(shape))
    sent, stemout = pl.pallas_call(
        sent_kernel,
        out_shape=(
            jax.ShapeDtypeStruct((blocks, width, half_width), bf16),
            jax.ShapeDtypeStruct((points, width), bf16),
        ),
        grid_spec=pltpu.PrefetchScalarGridSpec(
            num_scalar_prefetch=1,
            grid=(blocks,),
            in_specs=[
                by_tap, by_small, fixed((slots, width)), fixed((1, slots)), fixed((points, width)),
            ],
            out_specs=(by_block, fixed((points, width))),
        ),
        compiler_params=params(),
        name="sent_half",
    )(other_half, patches, small, returned, source.reshape(1, slots), slope)
    received = core_swap(sent)
    kept = pl.pallas_call(
        kept_kernel,
        out_shape=jax.ShapeDtypeStruct((blocks, width, half_width), f32),
        grid_spec=pltpu.PrefetchScalarGridSpec(
            num_scalar_prefetch=1,
            grid=(blocks,),
            in_specs=[by_tap, by_small, fixed((points, width))],
            out_specs=by_block,
        ),
        compiler_params=params(),
        cost_estimate=pl.CostEstimate(
            flops=2 * TAPS * width * points * half_width,
            bytes_accessed=20 * 1024 * 1024,
            transcendentals=0,
        ),
        name="kept_half",
    )(own_half, patches, small, stemout)

    chip_sum = (kept + received.astype(f32)).astype(bf16)
    chunk = blocks * width // chips
    pieces = lax.all_to_all(
        chip_sum.reshape(chips, chunk, half_width), CHIPS, split_axis=0, concat_axis=0, tiled=True
    )
    summed = jnp.sum(pieces.astype(f32), axis=0).astype(bf16)
    spread = jnp.broadcast_to(summed[None], (chips, chunk, half_width))
    gathered = lax.all_to_all(spread, CHIPS, split_axis=0, concat_axis=0, tiled=True)
    mine = gathered.reshape(blocks, width, half_width)
    other = core_swap(mine)

    grad_stem, grad_bias, out_edge, out_node = pl.pallas_call(
        final_kernel,
        out_shape=(
            jax.ShapeDtypeStruct((TAPS, channels, width), f32),
            jax.ShapeDtypeStruct((1, width), f32),
            jax.ShapeDtypeStruct((width, width), f32),
            jax.ShapeDtypeStruct((width, width), f32),
        ),
        grid_spec=pltpu.PrefetchScalarGridSpec(
            num_scalar_prefetch=1,
            grid=(blocks,),
            in_specs=[by_block, by_block],
            out_specs=(
                pl.BlockSpec((1, channels, width), lambda t, h: (jnp.minimum(t, TAPS - 1), 0, 0)),
                fixed((1, width)),
                fixed((width, width)),
                fixed((width, width)),
            ),
        ),
        compiler_params=params(),
        name="final",
    )(own_half, mine, other)
    return (mesh_out, grad_stem, grad_bias.reshape(width), out_edge, out_node)


def solution(mesh):
    bands, columns = mesh.devices.shape
    fine = Mesh(mesh.devices.reshape(bands, columns // 2, 2), EVERY)
    in_specs = (
        P("band", ("chip", "core"), None),
        P(),
        P(),
        P(),
        P(),
        P(EVERY, None, None),
        P(EVERY, None, None),
        P(EVERY, None),
        P(EVERY, None),
    )
    out_specs = (P(EVERY, None), P(), P(), P(), P())
    return jax.shard_map(shards, mesh=fine, in_specs=in_specs, out_specs=out_specs, check_vma=False)
```

```python
import functools

import jax
import jax.numpy as jnp
from jax import lax
from jax.experimental import pallas as pl
from jax.experimental.pallas import tpu as pltpu
from jax.sharding import Mesh, PartitionSpec as P

CHIPS = ("band", "chip")
EVERY = ("band", "chip", "core")
TAPS = 9
MIB = 1024 * 1024
TILE = 256


def f32_dot(first, second):
    return jnp.dot(first, second, preferred_element_type=jnp.float32)


def inner_dot(first, second):
    return lax.dot_general(
        first, second, (((0,), (0,)), ((), ())), preferred_element_type=jnp.float32
    )


def right_dot(first, second):
    return lax.dot_general(
        first, second, (((1,), (1,)), ((), ())), preferred_element_type=jnp.float32
    )


def core_swap(array):
    return lax.ppermute(array, "core", [(0, 1), (1, 0)])


def whole(memory=pltpu.VMEM):
    return pl.BlockSpec(memory_space=memory)


def params(mib):
    return pltpu.CompilerParams(vmem_limit_bytes=mib * MIB)


def cost(flops, moved):
    return pl.CostEstimate(flops=int(flops), bytes_accessed=int(moved), transcendentals=0)


def rows_at(number, size=TILE):
    return pl.ds(number * size, size)


def column_picker(image_rows, cols, parts):
    half = cols // 2
    shape = (3 * image_rows * half, image_rows * cols)
    out = lax.broadcasted_iota(jnp.int32, shape, 0)
    inside = lax.broadcasted_iota(jnp.int32, shape, 1)
    per_tap = image_rows * half
    tap = out // per_tap
    rest = out - tap * per_tap
    line = rest // half
    col = 2 * (rest - line * half) + tap - 1
    if parts == 2:
        pairs = image_rows // 2
        parity = line // pairs
        line = 2 * (line - parity * pairs) + parity
    hit = (col >= 0) & (inside == line * cols + col)
    return jnp.where(hit, 1.0, 0.0).astype(jnp.bfloat16)


def stem_kernel(
    west_ref, north_ref, corner_ref, picker_ref, north_picker_ref, bias_ref, source_ref,
    grid_hbm, w_hbm, even_hbm, odd_hbm, slope_hbm, out_hbm,
    grid, raw, weights, even, odd, latent, slope, out, in_sems, w_sems, out_sems, slope_sems, row_sems,
):
    rows, cols, channels = grid.shape
    half_rows, half_cols = rows // 2, cols // 2
    width = even.shape[-1]
    chunks = in_sems.shape[0]
    per_chunk = rows // chunks
    bf16 = jnp.bfloat16

    loads = [
        pltpu.make_async_copy(
            grid_hbm.at[rows_at(chunk, per_chunk)], grid.at[rows_at(chunk, per_chunk)], in_sems.at[chunk]
        )
        for chunk in range(chunks)
    ]
    w_loads = [
        pltpu.make_async_copy(w_hbm.at[tap], raw.at[tap], w_sems.at[tap]) for tap in range(TAPS)
    ]
    for copy in loads + w_loads:
        copy.start()

    tail = width - 128
    even[:, :, :, tail:] = jnp.zeros((3, half_rows, half_cols, 128), bf16)
    odd[:, :, :, tail:] = jnp.zeros((3, half_rows + 1, half_cols, 128), bf16)
    gap = channels // 16 * 16
    for tap in range(TAPS):
        weights[tap * width + gap : (tap + 1) * width] = jnp.zeros((width - gap, width), bf16)
    picker = picker_ref[...]
    north = f32_dot(north_picker_ref[...], north_ref[0]).astype(bf16)
    for tap in range(3):
        odd[tap, 0, :, :channels] = north[tap * half_cols : (tap + 1) * half_cols]

    for chunk in range(chunks):
        loads[chunk].wait()
        for group in range(chunk * per_chunk // 4, (chunk + 1) * per_chunk // 4):
            block = grid[4 * group : 4 * group + 4].reshape(4 * cols, channels)
            picked = f32_dot(picker, block).astype(bf16).reshape(3, 2, 2, half_cols, channels)
            for tap in range(3):
                even[tap, 2 * group : 2 * group + 2, :, :channels] = picked[tap, 0]
                odd[tap, 2 * group + 1 : 2 * group + 3, :, :channels] = picked[tap, 1]

    def patch(target, first, count, column):
        old = target[0, first : first + count, 0:16, :channels].astype(jnp.float32)
        line = lax.broadcasted_iota(jnp.int32, old.shape, 1)
        new = jnp.where(line == 0, column.astype(jnp.float32), old)
        target[0, first : first + count, 0:16, :channels] = new.astype(bf16)

    patch(even, 0, half_rows, west_ref[:, 0])
    patch(odd, 1, half_rows, west_ref[:, 1])
    patch(odd, 0, 1, corner_ref[...])
    phase_copies = [
        pltpu.make_async_copy(even, even_hbm, out_sems.at[0]),
        pltpu.make_async_copy(odd, odd_hbm, out_sems.at[1]),
    ]
    for tap in range(TAPS):
        w_loads[tap].wait()
        weights[tap * width : tap * width + channels] = raw[tap]
    for copy in phase_copies:
        copy.start()

    tile_rows = TILE // half_cols
    slope_copies = []
    for step in range(half_rows // tile_rows):
        pieces = []
        for row_tap in range(3):
            for col_tap in range(3):
                first = step * tile_rows + (row_tap // 2)
                held = even if row_tap == 1 else odd
                pieces.append(held[col_tap, first : first + tile_rows].reshape(TILE, width))
        pre = f32_dot(jnp.concatenate(pieces, axis=1), weights[...]) + bias_ref[...]
        sigmoid = jax.nn.sigmoid(pre)
        here = rows_at(step)
        slope[here] = sigmoid * (1.0 + pre * (1.0 - sigmoid))
        latent[here] = (pre * sigmoid).astype(bf16)
        copy = pltpu.make_async_copy(slope.at[here], slope_hbm.at[here], slope_sems.at[step])
        copy.start()
        slope_copies.append(copy)

    points = latent.shape[0]
    row_copies = []
    for step in range(out.shape[0] // TILE):
        here = rows_at(step)
        point = lax.broadcasted_iota(jnp.int32, (TILE, points), 1)
        pick = jnp.where(point == source_ref[here], 1.0, 0.0).astype(bf16)
        out[here] = f32_dot(pick, latent[...]).astype(bf16)
        copy = pltpu.make_async_copy(out.at[here], out_hbm.at[here], row_sems.at[step])
        copy.start()
        row_copies.append(copy)

    for copy in phase_copies + slope_copies + row_copies:
        copy.wait()


def flip_kernel(channels, even_ref, odd_ref, out_ref):
    number = pl.program_id(0)
    row_tap = number // 3
    col_tap = number % 3
    half_rows, half_cols, width = even_ref.shape[1:]

    def write(values):
        flipped = values.reshape(half_rows * half_cols, width).T
        line = lax.broadcasted_iota(jnp.int32, flipped.shape, 0)
        ones = (line == channels) & (number == 0)
        out_ref[0] = jnp.where(ones, 1.0, flipped.astype(jnp.float32)).astype(jnp.bfloat16)

    @pl.when(row_tap == 1)
    def _():
        write(even_ref[col_tap])

    @pl.when(row_tap != 1)
    def _():
        write(odd_ref[col_tap, pl.ds(row_tap // 2, half_rows)])


def edge_kernel(
    w_ref, dst_ref, agg_ref, rows_hbm, back_hbm, message_hbm, grad_hbm,
    rows, back, message, grad, in_sems, back_sems, message_sems, grad_sems,
):
    nodes = agg_ref.shape[0]
    tiles = rows.shape[0] // TILE
    bf16 = jnp.bfloat16
    loads = [
        pltpu.make_async_copy(rows_hbm.at[rows_at(step)], rows.at[rows_at(step)], in_sems.at[step])
        for step in range(tiles)
    ]
    for copy in loads:
        copy.start()
    copies = []
    weights = w_ref[...]
    for step in range(tiles):
        here = rows_at(step)
        node = lax.broadcasted_iota(jnp.int32, (TILE, nodes), 1)
        pick = jnp.where(node == dst_ref[here], 1.0, 0.0).astype(bf16)
        grad_msg = f32_dot(pick, agg_ref[...])
        loads[step].wait()
        pre = f32_dot(rows[here], weights)
        sigmoid = jax.nn.sigmoid(pre)
        message[here] = (pre * sigmoid).astype(bf16)
        grad_pre = (grad_msg * (sigmoid * (1.0 + pre * (1.0 - sigmoid)))).astype(bf16)
        grad[here] = grad_pre
        back[here] = right_dot(grad_pre, weights).astype(bf16)
        for kept, placed, sems in (
            (back, back_hbm, back_sems), (message, message_hbm, message_sems), (grad, grad_hbm, grad_sems),
        ):
            copy = pltpu.make_async_copy(kept.at[here], placed.at[here], sems.at[step])
            copy.start()
            copies.append(copy)
    for copy in copies:
        copy.wait()


def tap_products(columns, stemout_ref, smalls, patches_hbm, out_hbm, patches, out, in_sems, out_sems, ready):
    loads = [
        pltpu.make_async_copy(patches_hbm.at[tap], patches.at[tap], in_sems.at[tap])
        for tap in range(TAPS)
    ]
    for copy in loads:
        copy.start()
    ready()
    copies = [
        pltpu.make_async_copy(out.at[number], out_hbm.at[number], out_sems.at[number])
        for number in range(TAPS + 2)
    ]
    for number, small in enumerate(smalls):
        out[TAPS + number] = small[:, columns].astype(out.dtype)
        copies[TAPS + number].start()
    for tap in range(TAPS):
        loads[tap].wait()
        out[tap] = f32_dot(patches[tap], stemout_ref[:, columns]).astype(out.dtype)
        copies[tap].start()
    for copy in copies:
        copy.wait()


def half_columns(half, half_width):
    return pl.ds(pl.multiple_of(half * half_width, half_width), half_width)


def sent_kernel(
    half_ref, edge_ref, node_ref, returned_ref, source_ref, slope_ref, patches_hbm,
    out_hbm, stemout_ref, patches, out, in_sems, out_sems,
):
    points = stemout_ref.shape[0]
    slots = returned_ref.shape[0]

    def ready():
        for step in range(points // TILE):
            here = rows_at(step)
            point = lax.broadcasted_iota(jnp.int32, (TILE, slots), 0) + step * TILE
            pick = jnp.where(point == source_ref[...], 1.0, 0.0).astype(jnp.bfloat16)
            grad_latent = f32_dot(pick, returned_ref[...])
            stemout_ref[here] = (grad_latent * slope_ref[here]).astype(jnp.bfloat16)

    tap_products(
        half_columns(half_ref[0], out.shape[-1]), stemout_ref, (edge_ref, node_ref),
        patches_hbm, out_hbm, patches, out, in_sems, out_sems, ready,
    )


def kept_kernel(
    half_ref, edge_ref, node_ref, stemout_ref, patches_hbm, out_hbm, patches, out, in_sems, out_sems
):
    tap_products(
        half_columns(half_ref[0], out.shape[-1]), stemout_ref, (edge_ref, node_ref),
        patches_hbm, out_hbm, patches, out, in_sems, out_sems, lambda: None,
    )


def final_kernel(
    half_ref, sums_ref, *refs
):
    stem_hbm, bias_hbm, edge_hbm, node_hbm, stem, bias, square, stem_sems, sems = refs[-9:]
    channels = stem.shape[1]
    columns = half_columns(half_ref[0], stem.shape[-1])
    bias[...] = sums_ref[0, channels : channels + 1].astype(jnp.float32)
    copies = [pltpu.make_async_copy(bias, bias_hbm.at[:, columns], sems.at[0])]
    copies[0].start()
    for tap in range(TAPS):
        stem[tap] = sums_ref[tap, :channels].astype(jnp.float32)
        copies.append(
            pltpu.make_async_copy(stem.at[tap], stem_hbm.at[tap, :, columns], stem_sems.at[tap])
        )
        copies[-1].start()
    for number, placed in enumerate((edge_hbm, node_hbm)):
        square[number] = sums_ref[TAPS + number].astype(jnp.float32)
        copies.append(
            pltpu.make_async_copy(square.at[number], placed.at[:, columns], sems.at[1 + number])
        )
        copies[-1].start()
    for copy in copies:
        copy.wait()


def shards(
    grid_input, w_stem, b_stem, w_edge, w_node, src_index, dst_index, counts, mesh_cotangent
):
    rows_here, cols_here, channels = grid_input.shape
    width = w_edge.shape[0]
    bands = lax.axis_size("band")
    columns = lax.axis_size("chip") * 2
    chips = bands * lax.axis_size("chip")
    core = lax.axis_index("core")
    device_count = 2 * chips
    slot_count = src_index.shape[2]
    slots = device_count * slot_count
    half_rows = rows_here // 2
    half_cols = cols_here // 2
    points = half_rows * half_cols
    half_width = width // 2
    node_total = mesh_cotangent.shape[0]
    bf16, f32 = jnp.bfloat16, jnp.float32

    west = lax.ppermute(
        grid_input[:, -1:, :], ("chip", "core"), [(i, (i + 1) % columns) for i in range(columns)]
    )
    north = lax.ppermute(grid_input[-1:], "band", [(i, i + 1) for i in range(bands - 1)])
    corner = lax.ppermute(
        grid_input[-1:, -1:],
        EVERY,
        [
            (i * columns + j, (i + 1) * columns + (j + 1) % columns)
            for i in range(bands - 1)
            for j in range(columns)
        ],
    )
    flat_src = src_index.reshape(device_count, slot_count)
    slot_live = jnp.arange(slot_count, dtype=jnp.int32)[None, :] < counts.reshape(device_count, 1)
    source = jnp.where(slot_live, flat_src, -1)

    steps = slots // TILE
    even, odd, slope, outgoing = pl.pallas_call(
        stem_kernel,
        out_shape=(
            jax.ShapeDtypeStruct((3, half_rows, half_cols, width), bf16),
            jax.ShapeDtypeStruct((3, half_rows + 1, half_cols, width), bf16),
            jax.ShapeDtypeStruct((points, width), f32),
            jax.ShapeDtypeStruct((slots, width), bf16),
        ),
        in_specs=[whole()] * 7 + [whole(pl.ANY)] * 2,
        out_specs=(whole(pl.ANY),) * 4,
        scratch_shapes=[
            pltpu.VMEM((rows_here, cols_here, channels), bf16),
            pltpu.VMEM((TAPS, channels, width), bf16),
            pltpu.VMEM((TAPS * width, width), bf16),
            pltpu.VMEM((3, half_rows, half_cols, width), bf16),
            pltpu.VMEM((3, half_rows + 1, half_cols, width), bf16),
            pltpu.VMEM((points, width), bf16),
            pltpu.VMEM((points, width), f32),
            pltpu.VMEM((slots, width), bf16),
            pltpu.SemaphoreType.DMA((4,)),
            pltpu.SemaphoreType.DMA((TAPS,)),
            pltpu.SemaphoreType.DMA((2,)),
            pltpu.SemaphoreType.DMA((points // TILE,)),
            pltpu.SemaphoreType.DMA((steps,)),
        ],
        compiler_params=params(40),
        name="stem",
    )(
        west.reshape(half_rows, 2, 1, channels),
        north,
        corner,
        column_picker(4, cols_here, 2),
        column_picker(1, cols_here, 1),
        b_stem.reshape(1, width),
        source.reshape(slots, 1),
        grid_input,
        w_stem,
    )

    incoming = lax.all_to_all(
        outgoing.reshape(device_count, slot_count, width), EVERY, split_axis=0, concat_axis=0, tiled=True
    )
    arrived = incoming.reshape(slots, width)

    patches = pl.pallas_call(
        functools.partial(flip_kernel, channels),
        grid=(TAPS,),
        out_shape=jax.ShapeDtypeStruct((TAPS, width, points), bf16),
        in_specs=[
            pl.BlockSpec((3, half_rows, half_cols, width), lambda t: (0, 0, 0, 0)),
            pl.BlockSpec((3, half_rows + 1, half_cols, width), lambda t: (0, 0, 0, 0)),
        ],
        out_specs=pl.BlockSpec((1, width, points), lambda t: (t, 0, 0)),
        compiler_params=params(24),
        cost_estimate=cost(0, 16 * MIB),
        name="flip",
    )(even, odd)
    grad_agg = right_dot(mesh_cotangent, w_node).astype(bf16)
    dst_flat = dst_index.reshape(slots)

    back, messages, grad_pre = pl.pallas_call(
        edge_kernel,
        out_shape=(jax.ShapeDtypeStruct((slots, width), bf16),) * 3,
        in_specs=[whole()] * 3 + [whole(pl.ANY)],
        out_specs=(whole(pl.ANY),) * 3,
        scratch_shapes=[pltpu.VMEM((slots, width), bf16)] * 4
        + [pltpu.SemaphoreType.DMA((steps,))] * 4,
        compiler_params=params(24),
        name="edge",
    )(w_edge, dst_flat.reshape(slots, 1), grad_agg, arrived)

    returned = lax.all_to_all(
        back.reshape(device_count, slot_count, width), EVERY, split_axis=0, concat_axis=0, tiled=True
    ).reshape(slots, width)

    node_ids = jnp.arange(node_total, dtype=jnp.int32)
    onehot = (node_ids[:, None] == dst_flat[None, :]).astype(bf16)
    aggregate = f32_dot(onehot, messages).astype(bf16)
    mesh_out = f32_dot(aggregate, w_node).astype(bf16)
    grad_node = inner_dot(aggregate, mesh_cotangent)
    grad_edge = inner_dot(arrived, grad_pre)
    mesh_out, grad_edge, grad_node = lax.optimization_barrier((mesh_out, grad_edge, grad_node))

    blocks = TAPS + 2
    other_half = (1 - core).reshape(1)
    own_half = core.reshape(1)
    half_shape = jax.ShapeDtypeStruct((blocks, width, half_width), bf16)
    tap_scratch = [
        pltpu.VMEM((TAPS, width, points), bf16),
        pltpu.VMEM((blocks, width, half_width), bf16),
        pltpu.SemaphoreType.DMA((TAPS,)),
        pltpu.SemaphoreType.DMA((blocks,)),
    ]
    product_flops = 2 * TAPS * width * points * half_width
    sent, stemout = pl.pallas_call(
        sent_kernel,
        out_shape=(half_shape, jax.ShapeDtypeStruct((points, width), bf16)),
        in_specs=[whole(pltpu.SMEM)] + [whole()] * 5 + [whole(pl.ANY)],
        out_specs=(whole(pl.ANY), whole()),
        scratch_shapes=tap_scratch,
        compiler_params=params(32),
        name="sent_half",
    )(other_half, grad_edge, grad_node, returned, source.reshape(1, slots), slope, patches)
    received = core_swap(sent)
    kept = pl.pallas_call(
        kept_kernel,
        out_shape=half_shape,
        in_specs=[whole(pltpu.SMEM)] + [whole()] * 3 + [whole(pl.ANY)],
        out_specs=whole(pl.ANY),
        scratch_shapes=tap_scratch,
        compiler_params=params(28),
        cost_estimate=cost(product_flops, 14 * MIB),
        name="kept_half",
    )(own_half, grad_edge, grad_node, stemout, patches)

    chip_sum = (kept.astype(f32) + received.astype(f32)).astype(bf16)
    chunk = blocks * width // chips
    pieces = lax.all_to_all(
        chip_sum.reshape(chips, chunk, half_width), CHIPS, split_axis=0, concat_axis=0, tiled=True
    )
    summed = jnp.sum(pieces.astype(f32), axis=0).astype(bf16)
    spread = jnp.broadcast_to(summed[None], (chips, chunk, half_width))
    gathered = lax.all_to_all(spread, CHIPS, split_axis=0, concat_axis=0, tiled=True)
    mine = gathered.reshape(blocks, width, half_width)
    other = core_swap(mine)

    out_shape = (
        jax.ShapeDtypeStruct((TAPS, channels, width), f32),
        jax.ShapeDtypeStruct((1, width), f32),
        jax.ShapeDtypeStruct((width, width), f32),
        jax.ShapeDtypeStruct((width, width), f32),
    )

    def final(half, sums, before, name):
        return pl.pallas_call(
            final_kernel,
            out_shape=out_shape,
            in_specs=[whole(pltpu.SMEM), whole()] + [whole(pl.ANY)] * len(before),
            out_specs=(whole(pl.ANY),) * 4,
            scratch_shapes=[
                pltpu.VMEM((TAPS, channels, half_width), f32),
                pltpu.VMEM((1, half_width), f32),
                pltpu.VMEM((2, width, half_width), f32),
                pltpu.SemaphoreType.DMA((TAPS,)),
                pltpu.SemaphoreType.DMA((3,)),
            ],
            input_output_aliases={2 + i: i for i in range(len(before))},
            compiler_params=params(20),
            cost_estimate=cost(0, 9 * MIB),
            name=name,
        )(half, sums, *before)

    first_half = final(own_half, mine, (), "final_mine")
    grad_stem, grad_bias, out_edge, out_node = final(other_half, other, first_half, "final_other")
    return (mesh_out, grad_stem, grad_bias.reshape(width), out_edge, out_node)


def solution(mesh):
    bands, columns = mesh.devices.shape
    fine = Mesh(mesh.devices.reshape(bands, columns // 2, 2), EVERY)
    in_specs = (
        P("band", ("chip", "core"), None),
        P(),
        P(),
        P(),
        P(),
        P(EVERY, None, None),
        P(EVERY, None, None),
        P(EVERY, None),
        P(EVERY, None),
    )
    out_specs = (P(EVERY, None), P(), P(), P(), P())
    return jax.shard_map(shards, mesh=fine, in_specs=in_specs, out_specs=out_specs, check_vma=False)
```

```python
import functools
import itertools

import jax
import jax.numpy as jnp
from jax import lax
from jax.experimental import pallas as pl
from jax.experimental.pallas import tpu as pltpu
from jax.sharding import Mesh, PartitionSpec as P

EVERY = ("band", "chip", "core")
TAPS = 9
LINE = 4
MIB = 1024 * 1024
TILE = 256
AHEAD = 3


def f32_dot(first, second):
    return jnp.dot(first, second, preferred_element_type=jnp.float32)


def inner_dot(first, second):
    return lax.dot_general(
        first, second, (((0,), (0,)), ((), ())), preferred_element_type=jnp.float32
    )


def right_dot(first, second):
    return lax.dot_general(
        first, second, (((1,), (1,)), ((), ())), preferred_element_type=jnp.float32
    )


def core_swap(array):
    return lax.ppermute(array, "core", [(0, 1), (1, 0)])


def device_number(y, z, x, core):
    return ((y * LINE + z) * LINE + x) * 2 + core


def line_pairs(step):
    pairs = []
    for y, z, x in itertools.product(range(LINE), repeat=3):
        pairs.append((device_number(y, z, x, 0), device_number(y, z, (x + step) % LINE, 0)))
        pairs.append((device_number(y, z, x, 1), device_number((y + step) % LINE, z, x, 1)))
    return pairs


def plane_groups():
    planes = []
    for fixed in range(LINE):
        rest = list(itertools.product(range(LINE), repeat=2))
        planes.append([device_number(y, z, fixed, 0) for y, z in rest])
        planes.append([device_number(fixed, z, x, 1) for x, z in rest])
    return planes


def whole(memory=pltpu.VMEM):
    return pl.BlockSpec(memory_space=memory)


def params(mib):
    return pltpu.CompilerParams(vmem_limit_bytes=mib * MIB)


def cost(flops, moved):
    return pl.CostEstimate(flops=int(flops), bytes_accessed=int(moved), transcendentals=0)


def rows_at(number, size=TILE):
    return pl.ds(pl.multiple_of(number * size, size), size)


def unrolled(count):
    return pl.loop(0, count, unroll=True)


def column_picker(image_rows, cols, parts):
    half = cols // 2
    shape = (3 * image_rows * half, image_rows * cols)
    out = lax.broadcasted_iota(jnp.int32, shape, 0)
    inside = lax.broadcasted_iota(jnp.int32, shape, 1)
    per_tap = image_rows * half
    tap = out // per_tap
    rest = out - tap * per_tap
    line = rest // half
    col = 2 * (rest - line * half) + tap - 1
    if parts == 2:
        pairs = image_rows // 2
        parity = line // pairs
        line = 2 * (line - parity * pairs) + parity
    hit = (col >= 0) & (inside == line * cols + col)
    return jnp.where(hit, 1.0, 0.0).astype(jnp.bfloat16)


def stem_kernel(
    west_ref, north_ref, corner_ref, picker_ref, north_picker_ref, bias_ref, source_ref,
    grid_hbm, w_hbm, even_hbm, odd_hbm, slope_hbm, out_hbm,
    grid, raw, weights, even, odd, latent, slope, out, in_sems, w_sems, out_sems, slope_sems, row_sems,
):
    rows, cols, channels = grid.shape
    half_rows, half_cols = rows // 2, cols // 2
    width = even.shape[-1]
    chunks = in_sems.shape[0]
    per_chunk = rows // chunks
    bf16 = jnp.bfloat16

    loads = [
        pltpu.make_async_copy(
            grid_hbm.at[rows_at(chunk, per_chunk)], grid.at[rows_at(chunk, per_chunk)], in_sems.at[chunk]
        )
        for chunk in range(chunks)
    ]
    w_loads = [
        pltpu.make_async_copy(w_hbm.at[tap], raw.at[tap], w_sems.at[tap]) for tap in range(TAPS)
    ]
    for copy in loads + w_loads:
        copy.start()

    tail = width - 128
    even[:, :, :, tail:] = jnp.zeros((3, half_rows, half_cols, 128), bf16)
    odd[:, :, :, tail:] = jnp.zeros((3, half_rows + 1, half_cols, 128), bf16)
    gap = channels // 16 * 16
    for tap in range(TAPS):
        weights[tap * width + gap : (tap + 1) * width] = jnp.zeros((width - gap, width), bf16)
    north = f32_dot(north_picker_ref[...], north_ref[0]).astype(bf16)
    for tap in range(3):
        odd[tap, 0, :, :channels] = north[tap * half_cols : (tap + 1) * half_cols]

    for chunk in range(chunks):
        loads[chunk].wait()

        @unrolled(per_chunk // 4)
        def _(step):
            group = chunk * (per_chunk // 4) + step
            block = grid[pl.ds(4 * group, 4)].reshape(4 * cols, channels)
            picked = f32_dot(picker_ref[...], block).astype(bf16)
            picked = picked.reshape(3, 2, 2, half_cols, channels)
            for tap in range(3):
                even[tap, pl.ds(2 * group, 2), :, :channels] = picked[tap, 0]
                odd[tap, pl.ds(2 * group + 1, 2), :, :channels] = picked[tap, 1]

    def patch(target, first, count, column):
        old = target[0, first : first + count, 0:16, :channels].astype(jnp.float32)
        line = lax.broadcasted_iota(jnp.int32, old.shape, 1)
        new = jnp.where(line == 0, column.astype(jnp.float32), old)
        target[0, first : first + count, 0:16, :channels] = new.astype(bf16)

    patch(even, 0, half_rows, west_ref[:, 0])
    patch(odd, 1, half_rows, west_ref[:, 1])
    patch(odd, 0, 1, corner_ref[...])
    phase_copies = [
        pltpu.make_async_copy(even, even_hbm, out_sems.at[0]),
        pltpu.make_async_copy(odd, odd_hbm, out_sems.at[1]),
    ]
    for tap in range(TAPS):
        w_loads[tap].wait()
        weights[tap * width : tap * width + channels] = raw[tap]
    for copy in phase_copies:
        copy.start()

    tile_rows = TILE // half_cols
    points = latent.shape[0]

    def slope_copy(step):
        here = rows_at(step)
        return pltpu.make_async_copy(slope.at[here], slope_hbm.at[here], slope_sems.at[step])

    def row_copy(step):
        here = rows_at(step)
        return pltpu.make_async_copy(out.at[here], out_hbm.at[here], row_sems.at[step])

    @unrolled(points // TILE)
    def _(step):
        pieces = []
        for row_tap in range(3):
            for col_tap in range(3):
                first = step * tile_rows + (row_tap // 2)
                held = even if row_tap == 1 else odd
                pieces.append(held[col_tap, pl.ds(first, tile_rows)].reshape(TILE, width))
        pre = f32_dot(jnp.concatenate(pieces, axis=1), weights[...]) + bias_ref[...]
        sigmoid = jax.nn.sigmoid(pre)
        here = rows_at(step)
        slope[here] = sigmoid * (1.0 + pre * (1.0 - sigmoid))
        latent[here] = (pre * sigmoid).astype(bf16)
        slope_copy(step).start()

    @unrolled(out.shape[0] // TILE)
    def _(step):
        here = rows_at(step)
        point = lax.broadcasted_iota(jnp.int32, (TILE, points), 1)
        pick = jnp.where(point == source_ref[here], 1.0, 0.0).astype(bf16)
        out[here] = f32_dot(pick, latent[...]).astype(bf16)
        row_copy(step).start()

    for copy in phase_copies:
        copy.wait()

    @pl.loop(0, points // TILE)
    def _(step):
        slope_copy(step).wait()

    @pl.loop(0, out.shape[0] // TILE)
    def _(step):
        row_copy(step).wait()


def flip_kernel(channels, even_ref, odd_ref, out_ref):
    number = pl.program_id(0)
    row_tap = number // 3
    col_tap = number % 3
    half_rows, half_cols, width = even_ref.shape[1:]

    def write(values):
        flipped = values.reshape(half_rows * half_cols, width).T
        line = lax.broadcasted_iota(jnp.int32, flipped.shape, 0)
        ones = (line == channels) & (number == 0)
        out_ref[0] = jnp.where(ones, 1.0, flipped.astype(jnp.float32)).astype(jnp.bfloat16)

    @pl.when(row_tap == 1)
    def _():
        write(even_ref[col_tap])

    @pl.when(row_tap != 1)
    def _():
        write(odd_ref[col_tap, pl.ds(row_tap // 2, half_rows)])


def edge_kernel(
    w_ref, flipped_ref, dst_ref, agg_ref, rows_hbm, back_hbm, message_hbm, grad_hbm,
    rows, back, message, grad, in_sems, back_sems, message_sems, grad_sems,
):
    nodes = agg_ref.shape[0]
    tiles = rows.shape[0] // TILE
    bf16 = jnp.bfloat16

    def load(step):
        here = rows_at(step)
        return pltpu.make_async_copy(rows_hbm.at[here], rows.at[here], in_sems.at[step])

    def stores(step):
        here = rows_at(step)
        return [
            pltpu.make_async_copy(kept.at[here], placed.at[here], sems.at[step])
            for kept, placed, sems in (
                (back, back_hbm, back_sems),
                (message, message_hbm, message_sems),
                (grad, grad_hbm, grad_sems),
            )
        ]

    @pl.loop(0, tiles)
    def _(step):
        load(step).start()

    @unrolled(tiles)
    def _(step):
        here = rows_at(step)
        node = lax.broadcasted_iota(jnp.int32, (TILE, nodes), 1)
        pick = jnp.where(node == dst_ref[here], 1.0, 0.0).astype(bf16)
        grad_msg = f32_dot(pick, agg_ref[...])
        load(step).wait()
        pre = f32_dot(rows[here], w_ref[...])
        sigmoid = jax.nn.sigmoid(pre)
        message[here] = (pre * sigmoid).astype(bf16)
        grad_pre = (grad_msg * (sigmoid * (1.0 + pre * (1.0 - sigmoid)))).astype(bf16)
        grad[here] = grad_pre
        back[here] = f32_dot(grad_pre, flipped_ref[...]).astype(bf16)
        for copy in stores(step):
            copy.start()

    @pl.loop(0, tiles)
    def _(step):
        for copy in stores(step):
            copy.wait()


def tap_products(columns, stemout_ref, smalls, patches_hbm, out_hbm, patches, out, in_sems, out_sems, ready):
    quarters, _, depth, half_width = out.shape

    def load(tap):
        return pltpu.make_async_copy(patches_hbm.at[tap], patches.at[tap], in_sems.at[tap])

    def store(number):
        return pltpu.make_async_copy(out.at[:, number], out_hbm.at[:, number], out_sems.at[number])

    def finish(number, values):
        out[:, number] = values.astype(out.dtype).reshape(quarters, depth, half_width)
        store(number).start()

    for tap in range(AHEAD):
        load(tap).start()
    ready()
    for number, small in enumerate(smalls):
        finish(TAPS + number, small[:, columns])
    for tap in range(TAPS):
        load(tap).wait()
        if tap + AHEAD < TAPS:
            load(tap + AHEAD).start()
        finish(tap, f32_dot(patches[tap], stemout_ref[:, columns]))
    for number in range(TAPS + 2):
        store(number).wait()


def half_columns(half, half_width):
    return pl.ds(pl.multiple_of(half * half_width, half_width), half_width)


def sent_kernel(
    half_ref, edge_ref, node_ref, source_ref, returned_hbm, slope_hbm, patches_hbm,
    out_hbm, stemout_ref, returned, slope, patches, out, in_sems, out_sems, returned_sem, slope_sem,
):
    points = stemout_ref.shape[0]
    slots = returned.shape[0]
    returned_copy = pltpu.make_async_copy(returned_hbm, returned, returned_sem)
    slope_copy = pltpu.make_async_copy(slope_hbm, slope, slope_sem)
    returned_copy.start()
    slope_copy.start()

    def ready():
        returned_copy.wait()
        slope_copy.wait()

        @unrolled(points // TILE)
        def _(step):
            here = rows_at(step)
            point = lax.broadcasted_iota(jnp.int32, (TILE, slots), 0) + step * TILE
            pick = jnp.where(point == source_ref[...], 1.0, 0.0).astype(jnp.bfloat16)
            grad_latent = f32_dot(pick, returned[...])
            stemout_ref[here] = (grad_latent * slope[here]).astype(jnp.bfloat16)

    tap_products(
        half_columns(half_ref[0], out.shape[-1]), stemout_ref, (edge_ref, node_ref),
        patches_hbm, out_hbm, patches, out, in_sems, out_sems, ready,
    )


def kept_kernel(
    half_ref, edge_ref, node_ref, stemout_ref, patches_hbm, out_hbm, patches, out, in_sems, out_sems
):
    tap_products(
        half_columns(half_ref[0], out.shape[-1]), stemout_ref, (edge_ref, node_ref),
        patches_hbm, out_hbm, patches, out, in_sems, out_sems, lambda: None,
    )


def line_sum_kernel(
    quarter_ref, one_ref, two_ref, three_ref, kept_hbm, received_hbm, out_ref, kept, received, sems
):
    quarter = quarter_ref[0]
    copies = [
        pltpu.make_async_copy(kept_hbm.at[quarter], kept, sems.at[0]),
        pltpu.make_async_copy(received_hbm.at[quarter], received, sems.at[1]),
    ]
    for copy in copies:
        copy.start()
    for copy in copies:
        copy.wait()
    for piece in range(out_ref.shape[0]):
        here = (slice(None), pl.ds(piece // 2 * 16, 16), pl.ds(piece % 2 * 128, 128))
        total = kept[here].astype(jnp.float32)
        for ref in (received, one_ref, two_ref, three_ref):
            total = total + ref[here].astype(jnp.float32)
        out_ref[piece] = total.astype(out_ref.dtype)


def final_kernel(where_ref, *refs):
    held = refs[:8]
    stem_hbm, bias_ref, edge_hbm, node_hbm, stem, edge, node, stem_sems, sems = refs[8:]
    channels = stem.shape[1]
    depth = 128
    full = channels // depth
    spare = channels - full * depth

    def pieces(block):
        for number, ref in enumerate(held):
            quarter = where_ref[2 * number]
            first_column = where_ref[2 * number + 1] * 256
            for piece in range(ref.shape[0]):
                row, lane = piece // 2 * 16, piece % 2 * 128
                columns = pl.ds(pl.multiple_of(first_column + lane, 128), 128)
                yield quarter, row, columns, ref[piece, block].astype(jnp.float32)

    def place(target, quarter, row, columns, values):
        target[pl.ds(pl.multiple_of(quarter * depth + row, 16), 16), columns] = values

    copies = []
    for tap in range(TAPS):
        for quarter, row, columns, values in pieces(tap):
            if row + 16 <= spare:
                place(stem.at[tap], quarter, row, columns, values)
                continue

            @pl.when(quarter < full)
            def _():
                place(stem.at[tap], quarter, row, columns, values)

            if row < spare:
                @pl.when(quarter == full)
                def _():
                    left = spare - row
                    stem[tap, full * depth + row : channels, columns] = values[:left]
                    if tap == 0:
                        bias_ref[:, columns] = values[left : left + 1]

        copies.append(pltpu.make_async_copy(stem.at[tap], stem_hbm.at[tap], stem_sems.at[tap]))
        copies[-1].start()
    for number, (target, placed) in enumerate(((edge, edge_hbm), (node, node_hbm))):
        for quarter, row, columns, values in pieces(TAPS + number):
            place(target, quarter, row, columns, values)
        copies.append(pltpu.make_async_copy(target, placed, sems.at[number]))
        copies[-1].start()
    for copy in copies:
        copy.wait()


def shards(
    grid_input, w_stem, b_stem, w_edge, w_node, src_index, dst_index, counts, mesh_cotangent
):
    rows_here, cols_here, channels = grid_input.shape
    width = w_edge.shape[0]
    bands = lax.axis_size("band")
    columns = lax.axis_size("chip") * 2
    chips = bands * lax.axis_size("chip")
    core = lax.axis_index("core")
    device_count = 2 * chips
    slot_count = src_index.shape[2]
    slots = device_count * slot_count
    half_rows = rows_here // 2
    half_cols = cols_here // 2
    points = half_rows * half_cols
    half_width = width // 2
    node_total = mesh_cotangent.shape[0]
    bf16, f32 = jnp.bfloat16, jnp.float32

    west = lax.ppermute(
        grid_input[:, -1:, :], ("chip", "core"), [(i, (i + 1) % columns) for i in range(columns)]
    )
    north = lax.ppermute(grid_input[-1:], "band", [(i, i + 1) for i in range(bands - 1)])
    corner = lax.ppermute(
        grid_input[-1:, -1:],
        EVERY,
        [
            (i * columns + j, (i + 1) * columns + (j + 1) % columns)
            for i in range(bands - 1)
            for j in range(columns)
        ],
    )
    flat_src = src_index.reshape(device_count, slot_count)
    slot_live = jnp.arange(slot_count, dtype=jnp.int32)[None, :] < counts.reshape(device_count, 1)
    source = jnp.where(slot_live, flat_src, -1)

    steps = slots // TILE
    even, odd, slope, outgoing = pl.pallas_call(
        stem_kernel,
        out_shape=(
            jax.ShapeDtypeStruct((3, half_rows, half_cols, width), bf16),
            jax.ShapeDtypeStruct((3, half_rows + 1, half_cols, width), bf16),
            jax.ShapeDtypeStruct((points, width), f32),
            jax.ShapeDtypeStruct((slots, width), bf16),
        ),
        in_specs=[whole()] * 7 + [whole(pltpu.HBM)] * 2,
        out_specs=(whole(pltpu.HBM),) * 4,
        scratch_shapes=[
            pltpu.VMEM((rows_here, cols_here, channels), bf16),
            pltpu.VMEM((TAPS, channels, width), bf16),
            pltpu.VMEM((TAPS * width, width), bf16),
            pltpu.VMEM((3, half_rows, half_cols, width), bf16),
            pltpu.VMEM((3, half_rows + 1, half_cols, width), bf16),
            pltpu.VMEM((points, width), bf16),
            pltpu.VMEM((points, width), f32),
            pltpu.VMEM((slots, width), bf16),
            pltpu.SemaphoreType.DMA((4,)),
            pltpu.SemaphoreType.DMA((TAPS,)),
            pltpu.SemaphoreType.DMA((2,)),
            pltpu.SemaphoreType.DMA((points // TILE,)),
            pltpu.SemaphoreType.DMA((steps,)),
        ],
        compiler_params=params(40),
        name="stem",
    )(
        west.reshape(half_rows, 2, 1, channels),
        north,
        corner,
        column_picker(4, cols_here, 2),
        column_picker(1, cols_here, 1),
        b_stem.reshape(1, width),
        source.reshape(slots, 1),
        grid_input,
        w_stem,
    )

    incoming = lax.all_to_all(
        outgoing.reshape(device_count, slot_count, width), EVERY, split_axis=0, concat_axis=0, tiled=True
    )
    arrived = incoming.reshape(slots, width)

    patches = pl.pallas_call(
        functools.partial(flip_kernel, channels),
        grid=(TAPS,),
        out_shape=jax.ShapeDtypeStruct((TAPS, width, points), bf16),
        in_specs=[
            pl.BlockSpec((3, half_rows, half_cols, width), lambda t: (0, 0, 0, 0)),
            pl.BlockSpec((3, half_rows + 1, half_cols, width), lambda t: (0, 0, 0, 0)),
        ],
        out_specs=pl.BlockSpec((1, width, points), lambda t: (t, 0, 0)),
        compiler_params=params(24),
        cost_estimate=cost(0, 16 * MIB),
        name="flip",
    )(even, odd)
    grad_agg = right_dot(mesh_cotangent, w_node).astype(bf16)
    dst_flat = dst_index.reshape(slots)

    back, messages, grad_pre = pl.pallas_call(
        edge_kernel,
        out_shape=(jax.ShapeDtypeStruct((slots, width), bf16),) * 3,
        in_specs=[whole()] * 4 + [whole(pltpu.HBM)],
        out_specs=(whole(pltpu.HBM),) * 3,
        scratch_shapes=[pltpu.VMEM((slots, width), bf16)] * 4
        + [pltpu.SemaphoreType.DMA((steps,))] * 4,
        compiler_params=params(24),
        name="edge",
    )(w_edge, w_edge.T, dst_flat.reshape(slots, 1), grad_agg, arrived)

    returned = lax.all_to_all(
        back.reshape(device_count, slot_count, width), EVERY, split_axis=0, concat_axis=0, tiled=True
    ).reshape(slots, width)

    node_ids = jnp.arange(node_total, dtype=jnp.int32)
    onehot = (node_ids[:, None] == dst_flat[None, :]).astype(bf16)
    aggregate = f32_dot(onehot, messages).astype(bf16)
    mesh_out = f32_dot(aggregate, w_node).astype(bf16)
    grad_node = inner_dot(aggregate, mesh_cotangent)
    grad_edge = inner_dot(arrived, grad_pre)
    mesh_out, grad_edge, grad_node = lax.optimization_barrier((mesh_out, grad_edge, grad_node))

    blocks = TAPS + 2
    other_half = (1 - core).reshape(1)
    own_half = core.reshape(1)
    depth = width // LINE
    half_shape = jax.ShapeDtypeStruct((LINE, blocks, depth, half_width), bf16)
    tap_scratch = [
        pltpu.VMEM((TAPS, width, points), bf16),
        pltpu.VMEM((LINE, blocks, depth, half_width), bf16),
        pltpu.SemaphoreType.DMA((TAPS,)),
        pltpu.SemaphoreType.DMA((blocks,)),
    ]
    product_flops = 2 * TAPS * width * points * half_width
    sent, stemout = pl.pallas_call(
        sent_kernel,
        out_shape=(half_shape, jax.ShapeDtypeStruct((points, width), bf16)),
        in_specs=[whole(pltpu.SMEM)] + [whole()] * 3 + [whole(pltpu.HBM)] * 3,
        out_specs=(whole(pltpu.HBM), whole()),
        scratch_shapes=[pltpu.VMEM((slots, width), bf16), pltpu.VMEM((points, width), f32)]
        + tap_scratch
        + [pltpu.SemaphoreType.DMA] * 2,
        compiler_params=params(32),
        name="sent_half",
    )(other_half, grad_edge, grad_node, source.reshape(1, slots), returned, slope, patches)
    received = core_swap(sent)
    kept = pl.pallas_call(
        kept_kernel,
        out_shape=half_shape,
        in_specs=[whole(pltpu.SMEM)] + [whole()] * 3 + [whole(pltpu.HBM)],
        out_specs=whole(pltpu.HBM),
        scratch_shapes=tap_scratch,
        compiler_params=params(28),
        cost_estimate=cost(product_flops, 14 * MIB),
        name="kept_half",
    )(own_half, grad_edge, grad_node, stemout, patches)

    band, chip = lax.axis_index("band"), lax.axis_index("chip")
    place = jnp.where(core == 0, chip, band // LINE)
    other_place = jnp.where(core == 0, band // LINE, chip)

    def to_send(step):
        number = (place + step) % LINE
        own = lax.dynamic_index_in_dim(kept, number, 0, keepdims=False).astype(f32)
        return (own + lax.dynamic_index_in_dim(received, number, 0, keepdims=False).astype(f32)).astype(bf16)

    steps_out = range(1, LINE)
    arrived_parts = [lax.ppermute(to_send(step), EVERY, line_pairs(step)) for step in steps_out]
    part = (chips // LINE, blocks, 16, 128)
    quarter_scratch = pltpu.VMEM((blocks, depth, half_width), bf16)
    line_sum = pl.pallas_call(
        line_sum_kernel,
        out_shape=jax.ShapeDtypeStruct(part, bf16),
        in_specs=[whole(pltpu.SMEM)] + [whole()] * 3 + [whole(pltpu.HBM)] * 2,
        out_specs=whole(),
        scratch_shapes=[quarter_scratch, quarter_scratch, pltpu.SemaphoreType.DMA((2,))],
        compiler_params=params(16),
        name="line_sum",
    )(place.reshape(1), *arrived_parts, kept, received)
    planes = plane_groups()
    pieces = lax.all_to_all(
        line_sum, EVERY, split_axis=0, concat_axis=0, tiled=True, axis_index_groups=planes
    )
    summed = jnp.sum(pieces.astype(f32), axis=0).astype(bf16)
    mine = lax.all_to_all(
        jnp.broadcast_to(summed[None], part), EVERY, split_axis=0, concat_axis=0, tiled=True,
        axis_index_groups=planes,
    )
    held = [mine] + [lax.ppermute(mine, EVERY, line_pairs(step)) for step in steps_out]
    others = [core_swap(array) for array in held]
    where = [
        jnp.stack([(spot - step) % LINE, half]).astype(jnp.int32)
        for spot, half in ((place, core), (other_place, 1 - core))
        for step in range(LINE)
    ]
    grad_stem, grad_bias, out_edge, out_node = pl.pallas_call(
        final_kernel,
        out_shape=(
            jax.ShapeDtypeStruct((TAPS, channels, width), f32),
            jax.ShapeDtypeStruct((1, width), f32),
            jax.ShapeDtypeStruct((width, width), f32),
            jax.ShapeDtypeStruct((width, width), f32),
        ),
        in_specs=[whole(pltpu.SMEM)] + [whole()] * 8,
        out_specs=(whole(pltpu.HBM), whole(), whole(pltpu.HBM), whole(pltpu.HBM)),
        scratch_shapes=[
            pltpu.VMEM((TAPS, channels, width), f32),
            pltpu.VMEM((width, width), f32),
            pltpu.VMEM((width, width), f32),
            pltpu.SemaphoreType.DMA((TAPS,)),
            pltpu.SemaphoreType.DMA((2,)),
        ],
        compiler_params=params(28),
        name="final",
    )(jnp.concatenate(where), *held, *others)
    return (mesh_out, grad_stem, grad_bias.reshape(width), out_edge, out_node)


def solution(mesh):
    bands, columns = mesh.devices.shape
    fine = Mesh(mesh.devices.reshape(bands, columns // 2, 2), EVERY)
    in_specs = (
        P("band", ("chip", "core"), None),
        P(),
        P(),
        P(),
        P(),
        P(EVERY, None, None),
        P(EVERY, None, None),
        P(EVERY, None),
        P(EVERY, None),
    )
    out_specs = (P(EVERY, None), P(), P(), P(), P())
    return jax.shard_map(shards, mesh=fine, in_specs=in_specs, out_specs=out_specs, check_vma=False)
```

```python
import functools
import itertools

import jax
import jax.numpy as jnp
from jax import lax
from jax.experimental import pallas as pl
from jax.experimental.pallas import tpu as pltpu
from jax.sharding import Mesh, PartitionSpec as P

EVERY = ("band", "chip", "core")
TAPS = 9
LINE = 4
MIB = 1024 * 1024
TILE = 256


def f32_dot(first, second):
    return jnp.dot(first, second, preferred_element_type=jnp.float32)


def inner_dot(first, second):
    return lax.dot_general(
        first, second, (((0,), (0,)), ((), ())), preferred_element_type=jnp.float32
    )


def right_dot(first, second):
    return lax.dot_general(
        first, second, (((1,), (1,)), ((), ())), preferred_element_type=jnp.float32
    )


def core_swap(array):
    return lax.ppermute(array, "core", [(0, 1), (1, 0)])


def device_number(y, z, x, core):
    return ((y * LINE + z) * LINE + x) * 2 + core


def line_pairs(step):
    pairs = []
    for y, z, x in itertools.product(range(LINE), repeat=3):
        pairs.append((device_number(y, z, x, 0), device_number(y, z, (x + step) % LINE, 0)))
        pairs.append((device_number(y, z, x, 1), device_number((y + step) % LINE, z, x, 1)))
    return pairs


def plane_groups():
    planes = []
    for fixed in range(LINE):
        rest = list(itertools.product(range(LINE), repeat=2))
        planes.append([device_number(y, z, fixed, 0) for y, z in rest])
        planes.append([device_number(fixed, z, x, 1) for x, z in rest])
    return planes


def whole(memory=pltpu.VMEM):
    return pl.BlockSpec(memory_space=memory)


def params(mib):
    return pltpu.CompilerParams(vmem_limit_bytes=mib * MIB)


def cost(flops, moved):
    return pl.CostEstimate(flops=int(flops), bytes_accessed=int(moved), transcendentals=0)


def rows_at(number, size=TILE):
    return pl.ds(pl.multiple_of(number * size, size), size)


def unrolled(count):
    return pl.loop(0, count, unroll=True)


def column_picker(image_rows, cols, parts):
    half = cols // 2
    shape = (3 * image_rows * half, image_rows * cols)
    out = lax.broadcasted_iota(jnp.int32, shape, 0)
    inside = lax.broadcasted_iota(jnp.int32, shape, 1)
    per_tap = image_rows * half
    tap = out // per_tap
    rest = out - tap * per_tap
    line = rest // half
    col = 2 * (rest - line * half) + tap - 1
    if parts == 2:
        pairs = image_rows // 2
        parity = line // pairs
        line = 2 * (line - parity * pairs) + parity
    hit = (col >= 0) & (inside == line * cols + col)
    return jnp.where(hit, 1.0, 0.0).astype(jnp.bfloat16)


def stem_kernel(
    west_ref, north_ref, corner_ref, picker_ref, north_picker_ref, bias_ref, source_ref,
    grid_hbm, w_hbm, even_hbm, odd_hbm, slope_hbm, out_hbm,
    grid, raw, weights, even, odd, latent, slope, out, in_sems, w_sems, out_sems, slope_sems, row_sems,
):
    rows, cols, channels = grid.shape
    half_rows, half_cols = rows // 2, cols // 2
    width = even.shape[-1]
    chunks = in_sems.shape[0]
    per_chunk = rows // chunks
    bf16 = jnp.bfloat16

    loads = [
        pltpu.make_async_copy(
            grid_hbm.at[rows_at(chunk, per_chunk)], grid.at[rows_at(chunk, per_chunk)], in_sems.at[chunk]
        )
        for chunk in range(chunks)
    ]
    w_loads = [
        pltpu.make_async_copy(w_hbm.at[tap], raw.at[tap], w_sems.at[tap]) for tap in range(TAPS)
    ]
    for copy in loads + w_loads:
        copy.start()

    tail = width - 128
    even[:, :, :, tail:] = jnp.zeros((3, half_rows, half_cols, 128), bf16)
    odd[:, :, :, tail:] = jnp.zeros((3, half_rows + 1, half_cols, 128), bf16)
    gap = channels // 16 * 16
    for tap in range(TAPS):
        weights[tap * width + gap : (tap + 1) * width] = jnp.zeros((width - gap, width), bf16)
    north = f32_dot(north_picker_ref[...], north_ref[0]).astype(bf16)
    for tap in range(3):
        odd[tap, 0, :, :channels] = north[tap * half_cols : (tap + 1) * half_cols]

    for chunk in range(chunks):
        loads[chunk].wait()

        @unrolled(per_chunk // 4)
        def _(step):
            group = chunk * (per_chunk // 4) + step
            block = grid[pl.ds(4 * group, 4)].reshape(4 * cols, channels)
            picked = f32_dot(picker_ref[...], block).astype(bf16)
            picked = picked.reshape(3, 2, 2, half_cols, channels)
            for tap in range(3):
                even[tap, pl.ds(2 * group, 2), :, :channels] = picked[tap, 0]
                odd[tap, pl.ds(2 * group + 1, 2), :, :channels] = picked[tap, 1]

    def patch(target, first, count, column):
        old = target[0, first : first + count, 0:16, :channels].astype(jnp.float32)
        line = lax.broadcasted_iota(jnp.int32, old.shape, 1)
        new = jnp.where(line == 0, column.astype(jnp.float32), old)
        target[0, first : first + count, 0:16, :channels] = new.astype(bf16)

    patch(even, 0, half_rows, west_ref[:, 0])
    patch(odd, 1, half_rows, west_ref[:, 1])
    patch(odd, 0, 1, corner_ref[...])
    phase_copies = [
        pltpu.make_async_copy(even, even_hbm, out_sems.at[0]),
        pltpu.make_async_copy(odd, odd_hbm, out_sems.at[1]),
    ]
    for tap in range(TAPS):
        w_loads[tap].wait()
        weights[tap * width : tap * width + channels] = raw[tap]
    for copy in phase_copies:
        copy.start()

    tile_rows = TILE // half_cols
    points = latent.shape[0]

    def slope_copy(step):
        here = rows_at(step)
        return pltpu.make_async_copy(slope.at[here], slope_hbm.at[here], slope_sems.at[step])

    def row_copy(step):
        here = rows_at(step)
        return pltpu.make_async_copy(out.at[here], out_hbm.at[here], row_sems.at[step])

    @unrolled(points // TILE)
    def _(step):
        pieces = []
        for row_tap in range(3):
            for col_tap in range(3):
                first = step * tile_rows + (row_tap // 2)
                held = even if row_tap == 1 else odd
                pieces.append(held[col_tap, pl.ds(first, tile_rows)].reshape(TILE, width))
        pre = f32_dot(jnp.concatenate(pieces, axis=1), weights[...]) + bias_ref[...]
        sigmoid = jax.nn.sigmoid(pre)
        here = rows_at(step)
        slope[here] = sigmoid * (1.0 + pre * (1.0 - sigmoid))
        latent[here] = (pre * sigmoid).astype(bf16)
        slope_copy(step).start()

    @unrolled(out.shape[0] // TILE)
    def _(step):
        here = rows_at(step)
        point = lax.broadcasted_iota(jnp.int32, (TILE, points), 1)
        pick = jnp.where(point == source_ref[here], 1.0, 0.0).astype(bf16)
        out[here] = f32_dot(pick, latent[...]).astype(bf16)
        row_copy(step).start()

    for copy in phase_copies:
        copy.wait()

    @pl.loop(0, points // TILE)
    def _(step):
        slope_copy(step).wait()

    @pl.loop(0, out.shape[0] // TILE)
    def _(step):
        row_copy(step).wait()


def flip_kernel(channels, even_ref, odd_ref, out_ref):
    number = pl.program_id(0)
    row_tap = number // 3
    col_tap = number % 3
    half_rows, half_cols, width = even_ref.shape[1:]

    def write(values):
        flipped = values.reshape(half_rows * half_cols, width).T
        line = lax.broadcasted_iota(jnp.int32, flipped.shape, 0)
        ones = (line == channels) & (number == 0)
        out_ref[0] = jnp.where(ones, 1.0, flipped.astype(jnp.float32)).astype(jnp.bfloat16)

    @pl.when(row_tap == 1)
    def _():
        write(even_ref[col_tap])

    @pl.when(row_tap != 1)
    def _():
        write(odd_ref[col_tap, pl.ds(row_tap // 2, half_rows)])


def edge_kernel(side, w_ref, flipped_ref, dst_ref, agg_ref, rows_hbm, *refs):
    outs = 2 if side else 1
    placed, (rows, *kept), (in_sems, out_sems) = refs[:outs], refs[outs : 2 * outs + 1], refs[2 * outs + 1 :]
    nodes = agg_ref.shape[0]
    tiles = in_sems.shape[0]
    tile = rows.shape[0] // tiles
    bf16 = jnp.bfloat16

    def load(step):
        here = rows_at(step, tile)
        return pltpu.make_async_copy(rows_hbm.at[here], rows.at[here], in_sems.at[step])

    def stores(step):
        here = rows_at(step, tile)
        return [
            pltpu.make_async_copy(kept[i].at[here], placed[i].at[here], out_sems.at[i, step])
            for i in range(outs)
        ]

    for step in range(tiles):
        load(step).start()

    @unrolled(tiles)
    def _(step):
        here = rows_at(step, tile)
        node = lax.broadcasted_iota(jnp.int32, (tile, nodes), 1)
        pick = jnp.where(node == dst_ref[here], 1.0, 0.0).astype(bf16)
        grad_msg = f32_dot(pick, agg_ref[...])
        load(step).wait()
        pre = f32_dot(rows[here], w_ref[...])
        sigmoid = jax.nn.sigmoid(pre)
        grad_pre = (grad_msg * (sigmoid * (1.0 + pre * (1.0 - sigmoid)))).astype(bf16)
        if side:
            kept[0][here] = (pre * sigmoid).astype(bf16)
            kept[1][here] = grad_pre
        else:
            kept[0][here] = f32_dot(grad_pre, flipped_ref[...]).astype(bf16)
        for copy in stores(step):
            copy.start()

    for step in range(tiles):
        for copy in stores(step):
            copy.wait()


def quarter_of(spot, step):
    return lax.rem(spot + step + LINE, LINE)


def quarter_kernel(
    step, first, where_ref, source_ref, returned_hbm, slope_hbm, edge_hbm, node_hbm, patches_hbm, *refs
):
    if first:
        sent_hbm, kept_hbm, stemout_hbm = refs[:3]
        returned, slope = refs[3:5]
        refs = refs[5:]
    else:
        stemout_hbm, sent_hbm, kept_hbm = refs[:3]
        refs = refs[3:]
    stemout, patches, smalls, out, patch_sems, small_sems, out_sems, more_sems = refs
    depth, half_width = smalls.shape[2:]
    points, width = stemout.shape
    bf16 = jnp.bfloat16

    parts = []
    for part in range(2):
        quarter = quarter_of(where_ref[3 - part], step)
        rows = pl.ds(pl.multiple_of(quarter * depth, depth), depth)
        half = where_ref[1 - part]
        columns = pl.ds(pl.multiple_of(half * half_width, half_width), half_width)
        parts.append((rows, columns))
    patch_loads = [
        pltpu.make_async_copy(patches_hbm.at[:, parts[part][0]], patches.at[part], patch_sems.at[part])
        for part in range(2)
    ]
    small_loads = [
        pltpu.make_async_copy(
            placed.at[parts[part][0], parts[part][1]], smalls.at[part, number], small_sems.at[part, number]
        )
        for part in range(2)
        for number, placed in enumerate((edge_hbm, node_hbm))
    ]
    if first:
        stemout_store = pltpu.make_async_copy(stemout, stemout_hbm, more_sems.at[0])
        before = [
            pltpu.make_async_copy(returned_hbm, returned, more_sems.at[1]),
            pltpu.make_async_copy(slope_hbm, slope, more_sems.at[2]),
        ]
    else:
        before = [pltpu.make_async_copy(stemout_hbm, stemout, more_sems.at[0])]
    for copy in before + patch_loads + small_loads:
        copy.start()
    for copy in before:
        copy.wait()
    if first:
        slots = returned.shape[0]

        @unrolled(points // TILE)
        def _(step):
            here = rows_at(step)
            point = lax.broadcasted_iota(jnp.int32, (TILE, slots), 0) + step * TILE
            pick = jnp.where(point == source_ref[...], 1.0, 0.0).astype(bf16)
            grad_latent = f32_dot(pick, returned[...])
            stemout[here] = (grad_latent * slope[here]).astype(bf16)

        stemout_store.start()
    for copy in small_loads:
        copy.wait()
    stores = []
    for part, placed in enumerate((sent_hbm, kept_hbm)):
        patch_loads[part].wait()
        block = patches[part].reshape(TAPS * depth, points)
        products = f32_dot(block, stemout[:, parts[part][1]]).astype(bf16)
        out[part, :TAPS] = products.reshape(TAPS, depth, half_width)
        out[part, TAPS:] = smalls[part].astype(bf16)
        stores.append(pltpu.make_async_copy(out.at[part], placed, out_sems.at[part]))
        stores[-1].start()
    for copy in stores:
        copy.wait()
    if first:
        stemout_store.wait()


def line_sum_kernel(kept_ref, received_ref, one_ref, two_ref, three_ref, out_ref):
    for piece in range(out_ref.shape[0]):
        here = (slice(None), pl.ds(piece // 2 * 16, 16), pl.ds(piece % 2 * 128, 128))
        total = kept_ref[here].astype(jnp.float32)
        for ref in (received_ref, one_ref, two_ref, three_ref):
            total = total + ref[here].astype(jnp.float32)
        out_ref[piece] = total.astype(out_ref.dtype)


def final_kernel(step, where_ref, mine_ref, other_ref, *refs):
    stem_hbm, bias_hbm, edge_hbm, node_hbm, blocks, last, bias, stem_sems, small_sems, bias_sems = refs[-10:]
    channels = stem_hbm.shape[1]
    depth, half_width = blocks.shape[2:]
    full = channels // depth
    spare = channels - full * depth
    finish = []
    for part, ref in enumerate((mine_ref, other_ref)):
        quarter = quarter_of(where_ref[2 + part], -step)
        half = where_ref[part]
        rows = pl.ds(pl.multiple_of(quarter * depth, depth), depth)
        columns = pl.ds(pl.multiple_of(half * half_width, half_width), half_width)
        for piece in range(ref.shape[0]):
            row, lane = piece // 2 * 16, piece % 2 * 128
            blocks[part, :, row : row + 16, lane : lane + 128] = ref[piece].astype(jnp.float32)
        whole_copy = pltpu.make_async_copy(
            blocks.at[part, pl.ds(0, TAPS)], stem_hbm.at[:, rows, columns], stem_sems.at[part]
        )
        last_copy = pltpu.make_async_copy(
            last.at[part], stem_hbm.at[:, pl.ds(full * depth, spare), columns], stem_sems.at[part]
        )
        bias_copy = pltpu.make_async_copy(bias.at[part], bias_hbm.at[:, columns], bias_sems.at[part])
        small_copies = [
            pltpu.make_async_copy(
                blocks.at[part, TAPS + number], placed.at[rows, columns], small_sems.at[part, number]
            )
            for number, placed in enumerate((edge_hbm, node_hbm))
        ]

        @pl.when(quarter < full)
        def _():
            whole_copy.start()

        @pl.when(quarter == full)
        def _():
            last[part] = blocks[part, :TAPS, :spare]
            bias[part] = blocks[part, 0, spare : spare + 1]
            last_copy.start()
            bias_copy.start()

        for copy in small_copies:
            copy.start()
        finish.append((quarter, whole_copy, last_copy, bias_copy, small_copies))
    for quarter, whole_copy, last_copy, bias_copy, small_copies in finish:
        @pl.when(quarter < full)
        def _():
            whole_copy.wait()

        @pl.when(quarter == full)
        def _():
            last_copy.wait()
            bias_copy.wait()

        for copy in small_copies:
            copy.wait()


def shards(
    grid_input, w_stem, b_stem, w_edge, w_node, src_index, dst_index, counts, mesh_cotangent
):
    rows_here, cols_here, channels = grid_input.shape
    width = w_edge.shape[0]
    bands = lax.axis_size("band")
    columns = lax.axis_size("chip") * 2
    chips = bands * lax.axis_size("chip")
    core = lax.axis_index("core")
    device_count = 2 * chips
    slot_count = src_index.shape[2]
    slots = device_count * slot_count
    half_rows = rows_here // 2
    half_cols = cols_here // 2
    points = half_rows * half_cols
    half_width = width // 2
    node_total = mesh_cotangent.shape[0]
    bf16, f32 = jnp.bfloat16, jnp.float32

    west = lax.ppermute(
        grid_input[:, -1:, :], ("chip", "core"), [(i, (i + 1) % columns) for i in range(columns)]
    )
    north = lax.ppermute(grid_input[-1:], "band", [(i, i + 1) for i in range(bands - 1)])
    corner = lax.ppermute(
        grid_input[-1:, -1:],
        EVERY,
        [
            (i * columns + j, (i + 1) * columns + (j + 1) % columns)
            for i in range(bands - 1)
            for j in range(columns)
        ],
    )
    flat_src = src_index.reshape(device_count, slot_count)
    slot_live = jnp.arange(slot_count, dtype=jnp.int32)[None, :] < counts.reshape(device_count, 1)
    source = jnp.where(slot_live, flat_src, -1)

    steps = slots // TILE
    even, odd, slope, outgoing = pl.pallas_call(
        stem_kernel,
        out_shape=(
            pltpu.HBM((3, half_rows, half_cols, width), bf16),
            pltpu.HBM((3, half_rows + 1, half_cols, width), bf16),
            pltpu.HBM((points, width), f32),
            pltpu.HBM((slots, width), bf16),
        ),
        in_specs=[whole()] * 7 + [whole(pltpu.HBM)] * 2,
        out_specs=(whole(pltpu.HBM),) * 4,
        scratch_shapes=[
            pltpu.VMEM((rows_here, cols_here, channels), bf16),
            pltpu.VMEM((TAPS, channels, width), bf16),
            pltpu.VMEM((TAPS * width, width), bf16),
            pltpu.VMEM((3, half_rows, half_cols, width), bf16),
            pltpu.VMEM((3, half_rows + 1, half_cols, width), bf16),
            pltpu.VMEM((points, width), bf16),
            pltpu.VMEM((points, width), f32),
            pltpu.VMEM((slots, width), bf16),
            pltpu.SemaphoreType.DMA((4,)),
            pltpu.SemaphoreType.DMA((TAPS,)),
            pltpu.SemaphoreType.DMA((2,)),
            pltpu.SemaphoreType.DMA((points // TILE,)),
            pltpu.SemaphoreType.DMA((steps,)),
        ],
        compiler_params=params(56),
        name="stem",
    )(
        west.reshape(half_rows, 2, 1, channels),
        north,
        corner,
        column_picker(4, cols_here, 2),
        column_picker(1, cols_here, 1),
        b_stem.reshape(1, width),
        source.reshape(slots, 1),
        grid_input,
        w_stem,
    )

    incoming = lax.all_to_all(
        outgoing.reshape(device_count, slot_count, width), EVERY, split_axis=0, concat_axis=0, tiled=True
    )
    arrived = incoming.reshape(slots, width)

    patches = pl.pallas_call(
        functools.partial(flip_kernel, channels),
        grid=(TAPS,),
        out_shape=pltpu.HBM((TAPS, width, points), bf16),
        in_specs=[
            pl.BlockSpec((3, half_rows, half_cols, width), lambda t: (0, 0, 0, 0)),
            pl.BlockSpec((3, half_rows + 1, half_cols, width), lambda t: (0, 0, 0, 0)),
        ],
        out_specs=pl.BlockSpec((1, width, points), lambda t: (t, 0, 0)),
        compiler_params=params(56),
        cost_estimate=cost(0, 16 * MIB),
        name="flip",
    )(even, odd)
    grad_agg = right_dot(mesh_cotangent, w_node).astype(bf16)
    dst_flat = dst_index.reshape(slots)

    dst_column = dst_flat.reshape(slots, 1)
    w_flipped = w_edge.T

    def edge_call(side):
        outs = 2 if side else 1
        return pl.pallas_call(
            functools.partial(edge_kernel, side),
            out_shape=(pltpu.HBM((slots, width), bf16),) * outs,
            in_specs=[whole()] * 4 + [whole(pltpu.HBM)],
            out_specs=(whole(pltpu.HBM),) * outs,
            scratch_shapes=[pltpu.VMEM((slots, width), bf16)] * (1 + outs)
            + [pltpu.SemaphoreType.DMA((2,)), pltpu.SemaphoreType.DMA((outs, 2))],
            compiler_params=params(56),
            cost_estimate=cost(4 * slots * width * width, 8 * MIB),
            name="edge_side" if side else "edge_back",
        )(w_edge, w_flipped, dst_column, grad_agg, arrived)

    (back,) = edge_call(False)

    returned = lax.all_to_all(
        back.reshape(device_count, slot_count, width), EVERY, split_axis=0, concat_axis=0, tiled=True
    ).reshape(slots, width)

    messages, grad_pre = edge_call(True)
    node_ids = jnp.arange(node_total, dtype=jnp.int32)
    onehot = (node_ids[:, None] == dst_flat[None, :]).astype(bf16)
    aggregate = f32_dot(onehot, messages).astype(bf16)
    mesh_out = f32_dot(aggregate, w_node).astype(bf16)
    grad_node = inner_dot(aggregate, mesh_cotangent)
    grad_edge = inner_dot(arrived, grad_pre)
    mesh_out, grad_edge, grad_node = lax.optimization_barrier((mesh_out, grad_edge, grad_node))

    blocks = TAPS + 2
    band, chip = lax.axis_index("band"), lax.axis_index("chip")
    up = band // LINE
    where = jnp.where(
        core == 0, jnp.stack([core, 1 - core, chip, up]), jnp.stack([core, 1 - core, up, chip])
    )
    depth = width // LINE
    quarter_shape = pltpu.HBM((blocks, depth, half_width), bf16)
    stemout_shape = pltpu.HBM((points, width), bf16)
    source_row = source.reshape(1, slots)
    flops = 4 * TAPS * depth * points * half_width

    def quarter_call(step, stemout):
        first = stemout is None
        stemout_spec = whole(pltpu.HBM)
        return pl.pallas_call(
            functools.partial(quarter_kernel, step, first),
            out_shape=(quarter_shape,) * 2 + (stemout_shape,) * first,
            in_specs=[whole(pltpu.SMEM), whole()] + [whole(pltpu.HBM)] * (5 + (not first)),
            out_specs=(whole(pltpu.HBM),) * (2 + first),
            scratch_shapes=[pltpu.VMEM((slots, width), bf16), pltpu.VMEM((points, width), f32)] * first
            + [
                pltpu.VMEM((points, width), bf16),
                pltpu.VMEM((2, TAPS, depth, points), bf16),
                pltpu.VMEM((2, 2, depth, half_width), f32),
                pltpu.VMEM((2, blocks, depth, half_width), bf16),
                pltpu.SemaphoreType.DMA((2,)),
                pltpu.SemaphoreType.DMA((2, 2)),
                pltpu.SemaphoreType.DMA((2,)),
                pltpu.SemaphoreType.DMA((3,)),
            ],
            compiler_params=params(56),
            cost_estimate=cost(flops, 8 * MIB),
            name=f"quarter_{step}",
        )(where, source_row, returned, slope, grad_edge, grad_node, patches, *([] if first else [stemout]))

    order = (2, 1, 3, 0)
    stemout = None
    own, received, arrived_parts = {}, {}, {}
    for step in order:
        results = quarter_call(step, stemout)
        stemout = results[2] if stemout is None else stemout
        own[step] = results[1]
        received[step] = core_swap(results[0])
    for step in order[:-1]:
        chip_sum = (own[step].astype(f32) + received[step].astype(f32)).astype(bf16)
        arrived_parts[step] = lax.ppermute(chip_sum, EVERY, line_pairs(step))
    part = (chips // LINE, blocks, 16, 128)
    line_sum = pl.pallas_call(
        line_sum_kernel,
        out_shape=jax.ShapeDtypeStruct(part, bf16),
        in_specs=[whole()] * 5,
        out_specs=whole(),
        compiler_params=params(16),
        name="line_sum",
    )(own[0], received[0], *arrived_parts.values())
    planes = plane_groups()
    pieces = lax.all_to_all(
        line_sum, EVERY, split_axis=0, concat_axis=0, tiled=True, axis_index_groups=planes
    )
    summed = jnp.sum(pieces.astype(f32), axis=0).astype(bf16)
    mine = lax.all_to_all(
        jnp.broadcast_to(summed[None], part), EVERY, split_axis=0, concat_axis=0, tiled=True,
        axis_index_groups=planes,
    )
    held = {0: mine}
    for step in order[:-1]:
        held[step] = lax.ppermute(mine, EVERY, line_pairs(step))
    out_shape = (
        pltpu.HBM((TAPS, channels, width), f32),
        pltpu.HBM((1, width), f32),
        pltpu.HBM((width, width), f32),
        pltpu.HBM((width, width), f32),
    )
    results = ()
    for step in (0,) + order[:-1]:
        results = pl.pallas_call(
            functools.partial(final_kernel, step),
            out_shape=out_shape,
            in_specs=[whole(pltpu.SMEM)] + [whole()] * 2 + [whole(pltpu.HBM)] * len(results),
            out_specs=(whole(pltpu.HBM),) * 4,
            scratch_shapes=[
                pltpu.VMEM((2, blocks, depth, half_width), f32),
                pltpu.VMEM((2, TAPS, channels % depth, half_width), f32),
                pltpu.VMEM((2, 1, half_width), f32),
                pltpu.SemaphoreType.DMA((2,)),
                pltpu.SemaphoreType.DMA((2, 2)),
                pltpu.SemaphoreType.DMA((2,)),
            ],
            input_output_aliases={3 + i: i for i in range(len(results))},
            compiler_params=params(20),
            cost_estimate=cost(0, 5 * MIB),
            name=f"final_{step}",
        )(where, held[step], core_swap(held[step]), *results)
    grad_stem, grad_bias, out_edge, out_node = results
    return (mesh_out, grad_stem, grad_bias.reshape(width), out_edge, out_node)


def solution(mesh):
    bands, columns = mesh.devices.shape
    fine = Mesh(mesh.devices.reshape(bands, columns // 2, 2), EVERY)
    in_specs = (
        P("band", ("chip", "core"), None),
        P(),
        P(),
        P(),
        P(),
        P(EVERY, None, None),
        P(EVERY, None, None),
        P(EVERY, None),
        P(EVERY, None),
    )
    out_specs = (P(EVERY, None), P(), P(), P(), P())
    return jax.shard_map(shards, mesh=fine, in_specs=in_specs, out_specs=out_specs, check_vma=False)
```

```python
import functools
import itertools

import jax
import jax.numpy as jnp
from jax import lax
from jax.experimental import pallas as pl
from jax.experimental.pallas import tpu as pltpu
from jax.sharding import Mesh, PartitionSpec as P

EVERY = ("band", "chip", "core")
TAPS = 9
LINE = 4
MIB = 1024 * 1024
TILE = 256


def f32_dot(first, second):
    return jnp.dot(first, second, preferred_element_type=jnp.float32)


def inner_dot(first, second):
    return lax.dot_general(
        first, second, (((0,), (0,)), ((), ())), preferred_element_type=jnp.float32
    )


def right_dot(first, second):
    return lax.dot_general(
        first, second, (((1,), (1,)), ((), ())), preferred_element_type=jnp.float32
    )


def core_swap(array):
    return lax.ppermute(array, "core", [(0, 1), (1, 0)])


def device_number(y, z, x, core):
    return ((y * LINE + z) * LINE + x) * 2 + core


def line_pairs(step):
    pairs = []
    for y, z, x in itertools.product(range(LINE), repeat=3):
        pairs.append((device_number(y, z, x, 0), device_number(y, z, (x + step) % LINE, 0)))
        pairs.append((device_number(y, z, x, 1), device_number((y + step) % LINE, z, x, 1)))
    return pairs


def plane_groups():
    planes = []
    for fixed in range(LINE):
        rest = list(itertools.product(range(LINE), repeat=2))
        planes.append([device_number(y, z, fixed, 0) for y, z in rest])
        planes.append([device_number(fixed, z, x, 1) for x, z in rest])
    return planes


def whole(memory=pltpu.VMEM):
    return pl.BlockSpec(memory_space=memory)


def params(mib):
    return pltpu.CompilerParams(vmem_limit_bytes=mib * MIB)


def cost(flops, moved):
    return pl.CostEstimate(flops=int(flops), bytes_accessed=int(moved), transcendentals=0)


def rows_at(number, size=TILE):
    return pl.ds(pl.multiple_of(number * size, size), size)


def unrolled(count):
    return pl.loop(0, count, unroll=True)


def column_picker(image_rows, cols, parts):
    half = cols // 2
    shape = (3 * image_rows * half, image_rows * cols)
    out = lax.broadcasted_iota(jnp.int32, shape, 0)
    inside = lax.broadcasted_iota(jnp.int32, shape, 1)
    per_tap = image_rows * half
    tap = out // per_tap
    rest = out - tap * per_tap
    line = rest // half
    col = 2 * (rest - line * half) + tap - 1
    if parts == 2:
        pairs = image_rows // 2
        parity = line // pairs
        line = 2 * (line - parity * pairs) + parity
    hit = (col >= 0) & (inside == line * cols + col)
    return jnp.where(hit, 1.0, 0.0).astype(jnp.bfloat16)


def stem_kernel(
    west_ref, north_ref, corner_ref, picker_ref, north_picker_ref, bias_ref, source_ref,
    grid_hbm, w_hbm, even_hbm, odd_hbm, slope_hbm, out_hbm,
    grid, raw, weights, even, odd, latent, slope, out, in_sems, w_sems, out_sems, slope_sems, row_sems,
):
    rows, cols, channels = grid.shape
    half_rows, half_cols = rows // 2, cols // 2
    width = even.shape[-1]
    chunks = in_sems.shape[0]
    per_chunk = rows // chunks
    bf16 = jnp.bfloat16

    loads = [
        pltpu.make_async_copy(
            grid_hbm.at[rows_at(chunk, per_chunk)], grid.at[rows_at(chunk, per_chunk)], in_sems.at[chunk]
        )
        for chunk in range(chunks)
    ]
    w_loads = [
        pltpu.make_async_copy(w_hbm.at[tap], raw.at[tap], w_sems.at[tap]) for tap in range(TAPS)
    ]
    for copy in loads:
        copy.start()

    tail = width - 128
    even[:, :, :, tail:] = jnp.zeros((3, half_rows, half_cols, 128), bf16)
    odd[:, :, :, tail:] = jnp.zeros((3, half_rows + 1, half_cols, 128), bf16)
    gap = channels // 16 * 16
    for tap in range(TAPS):
        weights[tap * width + gap : (tap + 1) * width] = jnp.zeros((width - gap, width), bf16)
    north = f32_dot(north_picker_ref[...], north_ref[0]).astype(bf16)
    for tap in range(3):
        odd[tap, 0, :, :channels] = north[tap * half_cols : (tap + 1) * half_cols]

    for chunk in range(chunks):
        loads[chunk].wait()
        if chunk == chunks - 2:
            for copy in w_loads:
                copy.start()

        @unrolled(per_chunk // 4)
        def _(step):
            group = chunk * (per_chunk // 4) + step
            block = grid[pl.ds(4 * group, 4)].reshape(4 * cols, channels)
            picked = f32_dot(picker_ref[...], block).astype(bf16)
            picked = picked.reshape(3, 2, 2, half_cols, channels)
            for tap in range(3):
                even[tap, pl.ds(2 * group, 2), :, :channels] = picked[tap, 0]
                odd[tap, pl.ds(2 * group + 1, 2), :, :channels] = picked[tap, 1]

    def patch(target, first, count, column):
        old = target[0, first : first + count, 0:16, :channels].astype(jnp.float32)
        line = lax.broadcasted_iota(jnp.int32, old.shape, 1)
        new = jnp.where(line == 0, column.astype(jnp.float32), old)
        target[0, first : first + count, 0:16, :channels] = new.astype(bf16)

    patch(even, 0, half_rows, west_ref[:, 0])
    patch(odd, 1, half_rows, west_ref[:, 1])
    patch(odd, 0, 1, corner_ref[...])
    phase_copies = [
        pltpu.make_async_copy(even, even_hbm, out_sems.at[0]),
        pltpu.make_async_copy(odd, odd_hbm, out_sems.at[1]),
    ]
    for tap in range(TAPS):
        w_loads[tap].wait()
        weights[tap * width : tap * width + channels] = raw[tap]
    for copy in phase_copies:
        copy.start()

    tile_rows = TILE // half_cols
    points = latent.shape[0]

    def slope_copy(step):
        here = rows_at(step)
        return pltpu.make_async_copy(slope.at[here], slope_hbm.at[here], slope_sems.at[step])

    def row_copy(step):
        here = rows_at(step)
        return pltpu.make_async_copy(out.at[here], out_hbm.at[here], row_sems.at[step])

    @unrolled(points // TILE)
    def _(step):
        pieces = []
        for row_tap in range(3):
            for col_tap in range(3):
                first = step * tile_rows + (row_tap // 2)
                held = even if row_tap == 1 else odd
                pieces.append(held[col_tap, pl.ds(first, tile_rows)].reshape(TILE, width))
        pre = f32_dot(jnp.concatenate(pieces, axis=1), weights[...]) + bias_ref[...]
        sigmoid = jax.nn.sigmoid(pre)
        here = rows_at(step)
        slope[here] = sigmoid * (1.0 + pre * (1.0 - sigmoid))
        latent[here] = (pre * sigmoid).astype(bf16)
        slope_copy(step).start()

    @unrolled(out.shape[0] // TILE)
    def _(step):
        here = rows_at(step)
        point = lax.broadcasted_iota(jnp.int32, (TILE, points), 1)
        pick = jnp.where(point == source_ref[here], 1.0, 0.0).astype(bf16)
        out[here] = f32_dot(pick, latent[...]).astype(bf16)
        row_copy(step).start()

    for copy in phase_copies:
        copy.wait()

    @pl.loop(0, points // TILE)
    def _(step):
        slope_copy(step).wait()

    @pl.loop(0, out.shape[0] // TILE)
    def _(step):
        row_copy(step).wait()


def flip_kernel(channels, even_ref, odd_ref, out_ref):
    number = pl.program_id(0)
    row_tap = number // 3
    col_tap = number % 3
    half_rows, half_cols, width = even_ref.shape[1:]

    def write(values):
        flipped = values.reshape(half_rows * half_cols, width).T
        line = lax.broadcasted_iota(jnp.int32, flipped.shape, 0)
        ones = (line == channels) & (number == 0)
        out_ref[0] = jnp.where(ones, 1.0, flipped.astype(jnp.float32)).astype(jnp.bfloat16)

    @pl.when(row_tap == 1)
    def _():
        write(even_ref[col_tap])

    @pl.when(row_tap != 1)
    def _():
        write(odd_ref[col_tap, pl.ds(row_tap // 2, half_rows)])


def edge_kernel(side, w_ref, flipped_ref, dst_ref, agg_ref, rows_hbm, *refs):
    outs = 2 if side else 1
    placed, (rows, *kept), (in_sems, out_sems) = refs[:outs], refs[outs : 2 * outs + 1], refs[2 * outs + 1 :]
    nodes = agg_ref.shape[0]
    tiles = in_sems.shape[0]
    tile = rows.shape[0] // tiles
    bf16 = jnp.bfloat16

    def load(step):
        here = rows_at(step, tile)
        return pltpu.make_async_copy(rows_hbm.at[here], rows.at[here], in_sems.at[step])

    def stores(step):
        here = rows_at(step, tile)
        return [
            pltpu.make_async_copy(kept[i].at[here], placed[i].at[here], out_sems.at[i, step])
            for i in range(outs)
        ]

    load(0).start()

    @unrolled(tiles)
    def _(step):
        here = rows_at(step, tile)
        node = lax.broadcasted_iota(jnp.int32, (tile, nodes), 1)
        pick = jnp.where(node == dst_ref[here], 1.0, 0.0).astype(bf16)
        grad_msg = f32_dot(pick, agg_ref[...])
        load(step).wait()

        @pl.when(step + 1 < tiles)
        def _():
            load(step + 1).start()

        pre = f32_dot(rows[here], w_ref[...])
        sigmoid = jax.nn.sigmoid(pre)
        grad_pre = (grad_msg * (sigmoid * (1.0 + pre * (1.0 - sigmoid)))).astype(bf16)
        if side:
            kept[0][here] = (pre * sigmoid).astype(bf16)
            kept[1][here] = grad_pre
        else:
            kept[0][here] = f32_dot(grad_pre, flipped_ref[...]).astype(bf16)
        for copy in stores(step):
            copy.start()

    for step in range(tiles):
        for copy in stores(step):
            copy.wait()


def quarter_of(spot, step):
    return lax.rem(spot + step + LINE, LINE)


def gradients_kernel(
    where_ref, source_ref, returned_hbm, slope_hbm, edge_hbm, node_hbm, patches_hbm,
    sent_line_hbm, sent_own_hbm, kept_line_hbm, kept_own_hbm,
    returned, slope, stemout, patches, smalls, out, before_sems, patch_sems, small_sems, out_sems,
):
    half_width = out.shape[3]
    depth = out.shape[2] // LINE
    points, width = stemout.shape
    slots = returned.shape[0]
    bf16 = jnp.bfloat16
    before = [
        pltpu.make_async_copy(returned_hbm, returned, before_sems.at[0]),
        pltpu.make_async_copy(slope_hbm, slope, before_sems.at[1]),
    ]
    patch_loads = [
        pltpu.make_async_copy(patches_hbm.at[tap], patches.at[tap], patch_sems.at[tap])
        for tap in range(TAPS)
    ]
    small_loads = [
        pltpu.make_async_copy(placed, smalls.at[number], small_sems.at[number])
        for number, placed in enumerate((edge_hbm, node_hbm))
    ]
    placed = ((sent_line_hbm, sent_own_hbm), (kept_line_hbm, kept_own_hbm))

    def stores(part):
        copies = []
        for slot in range(LINE):
            quarter = quarter_of(where_ref[3 - part], slot + 1)
            target = placed[part][0].at[slot] if slot < LINE - 1 else placed[part][1]
            copies.append(
                pltpu.make_async_copy(out.at[part, :, pl.ds(pl.multiple_of(quarter * depth, depth), depth)], target, out_sems.at[part, slot])
            )
        return copies

    def finish(block, part, values):
        out[part, block] = values.astype(bf16)

    def columns(part):
        return pl.ds(pl.multiple_of(where_ref[1 - part] * half_width, half_width), half_width)

    for copy in before:
        copy.start()
    for copy in before:
        copy.wait()
    for copy in patch_loads + small_loads:
        copy.start()

    @unrolled(points // TILE)
    def _(tile):
        here = rows_at(tile)
        point = lax.broadcasted_iota(jnp.int32, (TILE, slots), 0) + tile * TILE
        pick = jnp.where(point == source_ref[...], 1.0, 0.0).astype(bf16)
        grad_latent = f32_dot(pick, returned[...])
        stemout[here] = (grad_latent * slope[here]).astype(bf16)

    for part in range(2):
        for tap in range(TAPS):
            if part == 0 and tap in (0, TAPS // 2):
                for copy in patch_loads[tap : TAPS // 2 if tap == 0 else TAPS]:
                    copy.wait()
            finish(tap, part, f32_dot(patches[tap], stemout[:, columns(part)]))
        for number in range(2):
            if part == 0:
                small_loads[number].wait()
            finish(TAPS + number, part, smalls[number, :, columns(part)])
        for copy in stores(part):
            copy.start()
    for part in range(2):
        for copy in stores(part):
            copy.wait()


def line_sum_kernel(kept_ref, received_ref, one_ref, two_ref, three_ref, out_ref):
    for piece in range(out_ref.shape[0]):
        here = (slice(None), pl.ds(piece // 2 * 16, 16), pl.ds(piece % 2 * 128, 128))
        total = kept_ref[here].astype(jnp.float32)
        for ref in (received_ref, one_ref, two_ref, three_ref):
            total = total + ref[here].astype(jnp.float32)
        out_ref[piece] = total.astype(out_ref.dtype)


def final_kernel(steps, where_ref, *refs):
    held = refs[: 2 * len(steps)]
    stem_hbm, bias_hbm, edge_hbm, node_hbm, blocks, last, bias, stem_sems, small_sems, bias_sems = refs[-10:]
    channels = stem_hbm.shape[1]
    depth, half_width = blocks.shape[2:]
    full = channels // depth
    spare = channels - full * depth
    finish = []
    for index, ref in enumerate(held):
        part = index % 2
        quarter = quarter_of(where_ref[2 + part], -steps[index // 2])
        half = where_ref[part]
        rows = pl.ds(pl.multiple_of(quarter * depth, depth), depth)
        columns = pl.ds(pl.multiple_of(half * half_width, half_width), half_width)
        for piece in range(ref.shape[0]):
            row, lane = piece // 2 * 16, piece % 2 * 128
            blocks[index, :, row : row + 16, lane : lane + 128] = ref[piece].astype(jnp.float32)
        whole_copy = pltpu.make_async_copy(
            blocks.at[index, pl.ds(0, TAPS)], stem_hbm.at[:, rows, columns], stem_sems.at[index]
        )
        last_copy = pltpu.make_async_copy(
            last.at[part], stem_hbm.at[:, pl.ds(full * depth, spare), columns], stem_sems.at[index]
        )
        bias_copy = pltpu.make_async_copy(bias.at[part], bias_hbm.at[:, columns], bias_sems.at[index])
        small_copies = [
            pltpu.make_async_copy(
                blocks.at[index, TAPS + number], placed.at[rows, columns], small_sems.at[index, number]
            )
            for number, placed in enumerate((edge_hbm, node_hbm))
        ]

        @pl.when(quarter < full)
        def _():
            whole_copy.start()

        @pl.when(quarter == full)
        def _():
            last[part] = blocks[index, :TAPS, :spare]
            bias[part] = blocks[index, 0, spare : spare + 1]
            last_copy.start()
            bias_copy.start()

        for copy in small_copies:
            copy.start()
        finish.append((quarter, whole_copy, last_copy, bias_copy, small_copies))
    for quarter, whole_copy, last_copy, bias_copy, small_copies in finish:
        @pl.when(quarter < full)
        def _():
            whole_copy.wait()

        @pl.when(quarter == full)
        def _():
            last_copy.wait()
            bias_copy.wait()

        for copy in small_copies:
            copy.wait()


def shards(
    grid_input, w_stem, b_stem, w_edge, w_node, src_index, dst_index, counts, mesh_cotangent
):
    rows_here, cols_here, channels = grid_input.shape
    width = w_edge.shape[0]
    bands = lax.axis_size("band")
    columns = lax.axis_size("chip") * 2
    chips = bands * lax.axis_size("chip")
    core = lax.axis_index("core")
    device_count = 2 * chips
    slot_count = src_index.shape[2]
    slots = device_count * slot_count
    half_rows = rows_here // 2
    half_cols = cols_here // 2
    points = half_rows * half_cols
    half_width = width // 2
    node_total = mesh_cotangent.shape[0]
    bf16, f32 = jnp.bfloat16, jnp.float32

    west = lax.ppermute(
        grid_input[:, -1:, :], ("chip", "core"), [(i, (i + 1) % columns) for i in range(columns)]
    )
    north = lax.ppermute(grid_input[-1:], "band", [(i, i + 1) for i in range(bands - 1)])
    corner = lax.ppermute(
        grid_input[-1:, -1:],
        EVERY,
        [
            (i * columns + j, (i + 1) * columns + (j + 1) % columns)
            for i in range(bands - 1)
            for j in range(columns)
        ],
    )
    flat_src = src_index.reshape(device_count, slot_count)
    slot_live = jnp.arange(slot_count, dtype=jnp.int32)[None, :] < counts.reshape(device_count, 1)
    source = jnp.where(slot_live, flat_src, -1)

    steps = slots // TILE
    even, odd, slope, outgoing = pl.pallas_call(
        stem_kernel,
        out_shape=(
            pltpu.HBM((3, half_rows, half_cols, width), bf16),
            pltpu.HBM((3, half_rows + 1, half_cols, width), bf16),
            pltpu.HBM((points, width), f32),
            pltpu.HBM((slots, width), bf16),
        ),
        in_specs=[whole()] * 7 + [whole(pltpu.HBM)] * 2,
        out_specs=(whole(pltpu.HBM),) * 4,
        scratch_shapes=[
            pltpu.VMEM((rows_here, cols_here, channels), bf16),
            pltpu.VMEM((TAPS, channels, width), bf16),
            pltpu.VMEM((TAPS * width, width), bf16),
            pltpu.VMEM((3, half_rows, half_cols, width), bf16),
            pltpu.VMEM((3, half_rows + 1, half_cols, width), bf16),
            pltpu.VMEM((points, width), bf16),
            pltpu.VMEM((points, width), f32),
            pltpu.VMEM((slots, width), bf16),
            pltpu.SemaphoreType.DMA((4,)),
            pltpu.SemaphoreType.DMA((TAPS,)),
            pltpu.SemaphoreType.DMA((2,)),
            pltpu.SemaphoreType.DMA((points // TILE,)),
            pltpu.SemaphoreType.DMA((steps,)),
        ],
        compiler_params=params(56),
        name="stem",
    )(
        west.reshape(half_rows, 2, 1, channels),
        north,
        corner,
        column_picker(4, cols_here, 2),
        column_picker(1, cols_here, 1),
        b_stem.reshape(1, width),
        source.reshape(slots, 1),
        grid_input,
        w_stem,
    )

    incoming = lax.all_to_all(
        outgoing.reshape(device_count, slot_count, width), EVERY, split_axis=0, concat_axis=0, tiled=True
    )
    arrived = incoming.reshape(slots, width)

    patches = pl.pallas_call(
        functools.partial(flip_kernel, channels),
        grid=(TAPS,),
        out_shape=pltpu.HBM((TAPS, width, points), bf16),
        in_specs=[
            pl.BlockSpec((3, half_rows, half_cols, width), lambda t: (0, 0, 0, 0)),
            pl.BlockSpec((3, half_rows + 1, half_cols, width), lambda t: (0, 0, 0, 0)),
        ],
        out_specs=pl.BlockSpec((1, width, points), lambda t: (t, 0, 0)),
        compiler_params=params(56),
        cost_estimate=cost(0, 16 * MIB),
        name="flip",
    )(even, odd)
    grad_agg = right_dot(mesh_cotangent, w_node).astype(bf16)
    dst_flat = dst_index.reshape(slots)

    dst_column = dst_flat.reshape(slots, 1)
    w_flipped = w_edge.T

    def edge_call(side):
        outs = 2 if side else 1
        return pl.pallas_call(
            functools.partial(edge_kernel, side),
            out_shape=(pltpu.HBM((slots, width), bf16),) * outs,
            in_specs=[whole()] * 4 + [whole(pltpu.HBM)],
            out_specs=(whole(pltpu.HBM),) * outs,
            scratch_shapes=[pltpu.VMEM((slots, width), bf16)] * (1 + outs)
            + [pltpu.SemaphoreType.DMA((2,)), pltpu.SemaphoreType.DMA((outs, 2))],
            compiler_params=params(40),
            cost_estimate=cost(4 * slots * width * width, 8 * MIB),
            name="edge_side" if side else "edge_back",
        )(w_edge, w_flipped, dst_column, grad_agg, arrived)

    (back,) = edge_call(False)

    returned = lax.all_to_all(
        back.reshape(device_count, slot_count, width), EVERY, split_axis=0, concat_axis=0, tiled=True
    ).reshape(slots, width)

    messages, grad_pre = edge_call(True)
    node_ids = jnp.arange(node_total, dtype=jnp.int32)
    onehot = (node_ids[:, None] == dst_flat[None, :]).astype(bf16)
    aggregate = f32_dot(onehot, messages).astype(bf16)
    mesh_out = f32_dot(aggregate, w_node).astype(bf16)
    grad_node = inner_dot(aggregate, mesh_cotangent).astype(bf16)
    grad_edge = inner_dot(arrived, grad_pre).astype(bf16)
    mesh_out, grad_edge, grad_node = lax.optimization_barrier((mesh_out, grad_edge, grad_node))

    blocks = TAPS + 2
    band, chip = lax.axis_index("band"), lax.axis_index("chip")
    up = band // LINE
    where = jnp.where(
        core == 0, jnp.stack([core, 1 - core, chip, up]), jnp.stack([core, 1 - core, up, chip])
    )
    depth = width // LINE
    source_row = source.reshape(1, slots)
    quarter_shape = (blocks, depth, half_width)
    line_shape = jax.ShapeDtypeStruct((LINE - 1,) + quarter_shape, bf16)
    own_shape = jax.ShapeDtypeStruct(quarter_shape, bf16)
    sent, sent_own, kept, kept_own = pl.pallas_call(
        gradients_kernel,
        out_shape=(line_shape, own_shape) * 2,
        in_specs=[whole(pltpu.SMEM), whole()] + [whole(pltpu.HBM)] * 5,
        out_specs=(whole(pl.ANY),) * 4,
        scratch_shapes=[
            pltpu.VMEM((slots, width), bf16),
            pltpu.VMEM((points, width), f32),
            pltpu.VMEM((points, width), bf16),
            pltpu.VMEM((TAPS, width, points), bf16),
            pltpu.VMEM((2, width, width), bf16),
            pltpu.VMEM((2, blocks, width, half_width), bf16),
            pltpu.SemaphoreType.DMA((2,)),
            pltpu.SemaphoreType.DMA((TAPS,)),
            pltpu.SemaphoreType.DMA((2,)),
            pltpu.SemaphoreType.DMA((2, LINE)),
        ],
        compiler_params=params(51),
        name="gradients",
    )(where, source_row, returned, slope, grad_edge, grad_node, patches)

    steps_out = (1, 2, 3)
    received = core_swap(sent)
    chip_sums = [
        (kept[i].astype(f32) + received[i].astype(f32)).astype(bf16) for i in range(len(steps_out))
    ]
    sent_own, *chip_sums = lax.optimization_barrier((sent_own, *chip_sums))
    arrived_parts = [
        lax.ppermute(chip_sum, EVERY, line_pairs(step)) for step, chip_sum in zip(steps_out, chip_sums)
    ]
    received_own = core_swap(sent_own)
    part = (chips // LINE, blocks, 16, 128)
    line_sum = pl.pallas_call(
        line_sum_kernel,
        out_shape=jax.ShapeDtypeStruct(part, bf16),
        in_specs=[whole()] * 5,
        out_specs=whole(),
        compiler_params=params(16),
        name="line_sum",
    )(kept_own, received_own, *arrived_parts)
    planes = plane_groups()
    pieces = lax.all_to_all(
        line_sum, EVERY, split_axis=0, concat_axis=0, tiled=True, axis_index_groups=planes
    )
    summed = jnp.sum(pieces.astype(f32), axis=0).astype(bf16)
    mine = lax.all_to_all(
        jnp.broadcast_to(summed[None], part), EVERY, split_axis=0, concat_axis=0, tiled=True,
        axis_index_groups=planes,
    )
    held = [lax.ppermute(mine, EVERY, line_pairs(step)) for step in steps_out]
    out_shape = (
        pltpu.HBM((TAPS, channels, width), f32),
        pltpu.HBM((1, width), f32),
        pltpu.HBM((width, width), f32),
        pltpu.HBM((width, width), f32),
    )

    def final(steps, pieces, before):
        count = len(pieces)
        return pl.pallas_call(
            functools.partial(final_kernel, steps),
            out_shape=out_shape,
            in_specs=[whole(pltpu.SMEM)] + [whole()] * count + [whole(pltpu.HBM)] * len(before),
            out_specs=(whole(pltpu.HBM),) * 4,
            scratch_shapes=[
                pltpu.VMEM((count, blocks, depth, half_width), f32),
                pltpu.VMEM((2, TAPS, channels % depth, half_width), f32),
                pltpu.VMEM((2, 1, half_width), f32),
                pltpu.SemaphoreType.DMA((count,)),
                pltpu.SemaphoreType.DMA((count, 2)),
                pltpu.SemaphoreType.DMA((count,)),
            ],
            input_output_aliases={1 + count + i: i for i in range(len(before))},
            compiler_params=params(26),
            cost_estimate=cost(0, 2 * MIB * count),
            name="final_own" if len(before) == 0 else "final_line",
        )(where, *pieces, *before)

    results = final((0,), [mine, core_swap(mine)], ())
    held[0], *results = lax.optimization_barrier((held[0], *results))
    others = [core_swap(held[0]), core_swap(held[1])]
    last, others[0] = lax.optimization_barrier((held[2], others[0]))
    others.append(core_swap(last))
    pieces = [array for pair in zip(held, others) for array in pair]
    results = final(steps_out, pieces, results)
    grad_stem, grad_bias, out_edge, out_node = results
    return (mesh_out, grad_stem, grad_bias.reshape(width), out_edge, out_node)


def solution(mesh):
    bands, columns = mesh.devices.shape
    fine = Mesh(mesh.devices.reshape(bands, columns // 2, 2), EVERY)
    in_specs = (
        P("band", ("chip", "core"), None),
        P(),
        P(),
        P(),
        P(),
        P(EVERY, None, None),
        P(EVERY, None, None),
        P(EVERY, None),
        P(EVERY, None),
    )
    out_specs = (P(EVERY, None), P(), P(), P(), P())
    return jax.shard_map(shards, mesh=fine, in_specs=in_specs, out_specs=out_specs, check_vma=False)
```

```python
import functools
import itertools

import jax
import jax.numpy as jnp
import numpy as np
from jax import lax
from jax.experimental import pallas as pl
from jax.experimental.pallas import tpu as pltpu
from jax.sharding import Mesh, PartitionSpec as P

EVERY = ("band", "chip", "core")
TAPS = 9
LINE = 4
ORDER = (2, 1, 3, 0)
MIB = 1024 * 1024
TILE = 512


def f32_dot(first, second):
    return jnp.dot(first, second, preferred_element_type=jnp.float32)


def inner_dot(first, second):
    return lax.dot_general(
        first, second, (((0,), (0,)), ((), ())), preferred_element_type=jnp.float32
    )


def right_dot(first, second):
    return lax.dot_general(
        first, second, (((1,), (1,)), ((), ())), preferred_element_type=jnp.float32
    )


def core_swap(array):
    return lax.ppermute(array, "core", [(0, 1), (1, 0)])


def device_number(y, z, x, core):
    return ((y * LINE + z) * LINE + x) * 2 + core


def line_pairs(step):
    pairs = []
    for y, z, x in itertools.product(range(LINE), repeat=3):
        pairs.append((device_number(y, z, x, 0), device_number(y, z, (x + step) % LINE, 0)))
        pairs.append((device_number(y, z, x, 1), device_number((y + step) % LINE, z, x, 1)))
    return pairs


def plane_groups():
    planes = []
    for fixed in range(LINE):
        rest = list(itertools.product(range(LINE), repeat=2))
        planes.append([device_number(y, z, fixed, 0) for y, z in rest])
        planes.append([device_number(fixed, z, x, 1) for x, z in rest])
    return planes


def whole(memory=pltpu.VMEM):
    return pl.BlockSpec(memory_space=memory)


def params(mib):
    return pltpu.CompilerParams(vmem_limit_bytes=mib * MIB)


def cost(flops, moved):
    return pl.CostEstimate(flops=int(flops), bytes_accessed=int(moved), transcendentals=0)


def rows_at(number, size=TILE):
    return pl.ds(pl.multiple_of(number * size, size), size)


def unrolled(count):
    return pl.loop(0, count, unroll=True)


def column_picker(image_rows, cols):
    half = cols // 2
    out = np.zeros((3, image_rows, half, image_rows, cols), np.float32)
    lines = [*range(0, image_rows, 2), *range(1, image_rows, 2)]
    for tap, (place, line), j in itertools.product(range(3), enumerate(lines), range(half)):
        if 2 * j + tap >= 1:
            out[tap, place, j, line, 2 * j + tap - 1] = 1.0
    return jnp.asarray(out.reshape(3 * image_rows * half, image_rows * cols), jnp.bfloat16)


def stem_kernel(
    west_ref, north_ref, corner_ref, picker_ref, north_picker_ref, bias_ref, source_ref,
    grid_hbm, w_hbm, even_hbm, odd_hbm, slope_hbm, out_hbm,
    grid, raw, weights, even, odd, latent, slope, out, in_sems, w_sems, out_sems, slope_sems, row_sems,
):
    rows, cols, channels = grid.shape
    half_rows, half_cols = rows // 2, cols // 2
    width = even.shape[-1]
    chunks = in_sems.shape[0]
    per_chunk = rows // chunks
    bf16 = jnp.bfloat16

    loads = [
        pltpu.make_async_copy(
            grid_hbm.at[rows_at(chunk, per_chunk)], grid.at[rows_at(chunk, per_chunk)], in_sems.at[chunk]
        )
        for chunk in range(chunks)
    ]
    w_loads = [
        pltpu.make_async_copy(w_hbm.at[tap], raw.at[tap], w_sems.at[tap]) for tap in range(TAPS)
    ]
    for copy in loads:
        copy.start()

    tail = width - 128
    even[:, :, :, tail:] = jnp.zeros((3, half_rows, half_cols, 128), bf16)
    odd[:, :, :, tail:] = jnp.zeros((3, half_rows + 1, half_cols, 128), bf16)
    gap = channels // 16 * 16
    for tap in range(TAPS):
        weights[tap * width + gap : (tap + 1) * width] = jnp.zeros((width - gap, width), bf16)
    north = f32_dot(north_picker_ref[...], north_ref[0]).astype(bf16)
    for tap in range(3):
        odd[tap, 0, :, :channels] = north[tap * half_cols : (tap + 1) * half_cols]

    for chunk in range(chunks):
        loads[chunk].wait()
        if chunk == chunks - 2:
            for copy in w_loads:
                copy.start()

        @unrolled(per_chunk // 4)
        def _(step):
            group = chunk * (per_chunk // 4) + step
            block = grid[pl.ds(4 * group, 4)].reshape(4 * cols, channels)
            picked = f32_dot(picker_ref[...], block).astype(bf16)
            picked = picked.reshape(3, 2, 2, half_cols, channels)
            for tap in range(3):
                even[tap, pl.ds(2 * group, 2), :, :channels] = picked[tap, 0]
                odd[tap, pl.ds(2 * group + 1, 2), :, :channels] = picked[tap, 1]

    def patch(target, first, count, column):
        old = target[0, first : first + count, 0:16, :channels].astype(jnp.float32)
        line = lax.broadcasted_iota(jnp.int32, old.shape, 1)
        new = jnp.where(line == 0, column.astype(jnp.float32), old)
        target[0, first : first + count, 0:16, :channels] = new.astype(bf16)

    patch(even, 0, half_rows, west_ref[:, 0])
    patch(odd, 1, half_rows, west_ref[:, 1])
    patch(odd, 0, 1, corner_ref[...])
    phase_copies = [
        pltpu.make_async_copy(even, even_hbm, out_sems.at[0]),
        pltpu.make_async_copy(odd, odd_hbm, out_sems.at[1]),
    ]
    for tap in range(TAPS):
        w_loads[tap].wait()
        weights[tap * width : tap * width + channels] = raw[tap]
    for copy in phase_copies:
        copy.start()

    tile_rows = TILE // half_cols
    points = latent.shape[0]

    def slope_copy(step):
        here = rows_at(step)
        return pltpu.make_async_copy(slope.at[here], slope_hbm.at[here], slope_sems.at[step])

    def row_copy(step):
        here = rows_at(step)
        return pltpu.make_async_copy(out.at[here], out_hbm.at[here], row_sems.at[step])

    @unrolled(points // TILE)
    def _(step):
        pieces = []
        for row_tap in range(3):
            for col_tap in range(3):
                first = step * tile_rows + (row_tap // 2)
                held = even if row_tap == 1 else odd
                pieces.append(held[col_tap, pl.ds(first, tile_rows)].reshape(TILE, width))
        pre = f32_dot(jnp.concatenate(pieces, axis=1), weights[...]) + bias_ref[...]
        sigmoid = jax.nn.sigmoid(pre)
        here = rows_at(step)
        slope[here] = sigmoid * (1.0 + pre * (1.0 - sigmoid))
        latent[here] = (pre * sigmoid).astype(bf16)
        slope_copy(step).start()

    @unrolled(out.shape[0] // TILE)
    def _(step):
        here = rows_at(step)
        point = lax.broadcasted_iota(jnp.int32, (TILE, points), 1)
        pick = jnp.where(point == source_ref[here], 1.0, 0.0).astype(bf16)
        out[here] = f32_dot(pick, latent[...]).astype(bf16)
        row_copy(step).start()

    for copy in phase_copies:
        copy.wait()

    @pl.loop(0, points // TILE)
    def _(step):
        slope_copy(step).wait()

    @pl.loop(0, out.shape[0] // TILE)
    def _(step):
        row_copy(step).wait()


def flip_kernel(channels, even_ref, odd_ref, out_ref):
    number = pl.program_id(0)
    row_tap = number // 3
    col_tap = number % 3
    half_rows, half_cols, width = even_ref.shape[1:]

    def write(values):
        flipped = values.reshape(half_rows * half_cols, width).T
        line = lax.broadcasted_iota(jnp.int32, flipped.shape, 0)
        ones = (line == channels) & (number == 0)
        out_ref[0] = jnp.where(ones, 1.0, flipped.astype(jnp.float32)).astype(jnp.bfloat16)

    @pl.when(row_tap == 1)
    def _():
        write(even_ref[col_tap])

    @pl.when(row_tap != 1)
    def _():
        write(odd_ref[col_tap, pl.ds(row_tap // 2, half_rows)])


def edge_kernel(side, w_ref, flipped_ref, dst_ref, agg_ref, rows_hbm, *refs):
    outs = 2 if side else 1
    placed, (rows, *kept), (in_sems, out_sems) = refs[:outs], refs[outs : 2 * outs + 1], refs[2 * outs + 1 :]
    nodes = agg_ref.shape[0]
    tiles = in_sems.shape[0]
    tile = rows.shape[0] // tiles
    bf16 = jnp.bfloat16

    def load(step):
        here = rows_at(step, tile)
        return pltpu.make_async_copy(rows_hbm.at[here], rows.at[here], in_sems.at[step])

    def stores(step):
        here = rows_at(step, tile)
        return [
            pltpu.make_async_copy(kept[i].at[here], placed[i].at[here], out_sems.at[i, step])
            for i in range(outs)
        ]

    load(0).start()

    @unrolled(tiles)
    def _(step):
        here = rows_at(step, tile)
        node = lax.broadcasted_iota(jnp.int32, (nodes, tile), 0)
        pick = jnp.where(node == dst_ref[:, here], 1.0, 0.0).astype(bf16)
        grad_msg = inner_dot(pick, agg_ref[...])
        load(step).wait()

        @pl.when(step + 1 < tiles)
        def _():
            load(step + 1).start()

        pre = f32_dot(rows[here], w_ref[...])
        sigmoid = jax.nn.sigmoid(pre)
        grad_pre = (grad_msg * (sigmoid * (1.0 + pre * (1.0 - sigmoid)))).astype(bf16)
        if side:
            kept[0][here] = (pre * sigmoid).astype(bf16)
            kept[1][here] = grad_pre
        else:
            kept[0][here] = f32_dot(grad_pre, flipped_ref[...]).astype(bf16)
        for copy in stores(step):
            copy.start()

    for step in range(tiles):
        for copy in stores(step):
            copy.wait()


def quarter_of(spot, step):
    return lax.rem(spot + step + LINE, LINE)


def gradients_kernel(
    where_ref, source_ref, returned_hbm, slope_hbm, edge_hbm, node_hbm, patches_hbm,
    *refs,
):
    placed = (refs[:LINE], refs[LINE : 2 * LINE])
    (
        returned, slope, stemout, patches, smalls, out, before_sems, patch_sems, small_sems, out_sems,
    ) = refs[2 * LINE :]
    half_width = out.shape[3]
    depth = out.shape[2] // LINE
    points, width = stemout.shape
    slots = returned.shape[0]
    bf16 = jnp.bfloat16
    before = [
        pltpu.make_async_copy(returned_hbm, returned, before_sems.at[0]),
        pltpu.make_async_copy(slope_hbm, slope, before_sems.at[1]),
    ]
    patch_loads = [
        pltpu.make_async_copy(patches_hbm.at[tap], patches.at[tap], patch_sems.at[tap])
        for tap in range(TAPS)
    ]
    small_loads = [
        pltpu.make_async_copy(placed, smalls.at[number], small_sems.at[number])
        for number, placed in enumerate((edge_hbm, node_hbm))
    ]

    def stores(part):
        copies = []
        for slot in range(LINE):
            quarter = quarter_of(where_ref[3 - part], ORDER[slot])
            copies.append(
                pltpu.make_async_copy(out.at[part, :, pl.ds(pl.multiple_of(quarter * depth, depth), depth)], placed[part][slot], out_sems.at[part, slot])
            )
        return copies

    def finish(block, part, values):
        out[part, block] = values.astype(bf16)

    def columns(part):
        return pl.ds(pl.multiple_of(where_ref[1 - part] * half_width, half_width), half_width)

    for copy in before:
        copy.start()
    for copy in before:
        copy.wait()
    for copy in patch_loads + small_loads:
        copy.start()

    @unrolled(points // TILE)
    def _(tile):
        here = rows_at(tile)
        point = lax.broadcasted_iota(jnp.int32, (TILE, slots), 0) + tile * TILE
        pick = jnp.where(point == source_ref[...], 1.0, 0.0).astype(bf16)
        grad_latent = f32_dot(pick, returned[...])
        stemout[here] = (grad_latent * slope[here]).astype(bf16)

    for part in range(2):
        for tap in range(TAPS):
            if part == 0 and tap in (0, TAPS // 2):
                for copy in patch_loads[tap : TAPS // 2 if tap == 0 else TAPS]:
                    copy.wait()
            finish(tap, part, f32_dot(patches[tap], stemout[:, columns(part)]))
        for number in range(2):
            if part == 0:
                small_loads[number].wait()
            finish(TAPS + number, part, smalls[number, :, columns(part)])
        for copy in stores(part):
            copy.start()
    for part in range(2):
        for copy in stores(part):
            copy.wait()


def line_sum_kernel(kept_ref, received_ref, one_ref, two_ref, three_ref, out_ref):
    for piece in range(out_ref.shape[0]):
        here = (slice(None), pl.ds(piece // 2 * 16, 16), pl.ds(piece % 2 * 128, 128))
        total = kept_ref[here].astype(jnp.float32)
        for ref in (received_ref, one_ref, two_ref, three_ref):
            total = total + ref[here].astype(jnp.float32)
        out_ref[piece] = total.astype(out_ref.dtype)


def final_kernel(steps, where_ref, *refs):
    held = refs[: 2 * len(steps)]
    stem_hbm, bias_hbm, edge_hbm, node_hbm, blocks, last, bias, stem_sems, small_sems, bias_sems = refs[-10:]
    channels = stem_hbm.shape[1]
    depth, half_width = blocks.shape[2:]
    full = channels // depth
    spare = channels - full * depth
    finish = []
    for index, ref in enumerate(held):
        part = index % 2
        quarter = quarter_of(where_ref[2 + part], -steps[index // 2])
        half = where_ref[part]
        rows = pl.ds(pl.multiple_of(quarter * depth, depth), depth)
        columns = pl.ds(pl.multiple_of(half * half_width, half_width), half_width)
        for piece in range(ref.shape[0]):
            row, lane = piece // 2 * 16, piece % 2 * 128
            blocks[index, :, row : row + 16, lane : lane + 128] = ref[piece].astype(jnp.float32)
        whole_copy = pltpu.make_async_copy(
            blocks.at[index, pl.ds(0, TAPS)], stem_hbm.at[:, rows, columns], stem_sems.at[index]
        )
        last_copy = pltpu.make_async_copy(
            last.at[part], stem_hbm.at[:, pl.ds(full * depth, spare), columns], stem_sems.at[index]
        )
        bias_copy = pltpu.make_async_copy(bias.at[part], bias_hbm.at[:, columns], bias_sems.at[index])
        small_copies = [
            pltpu.make_async_copy(
                blocks.at[index, TAPS + number], placed.at[rows, columns], small_sems.at[index, number]
            )
            for number, placed in enumerate((edge_hbm, node_hbm))
        ]

        @pl.when(quarter < full)
        def _():
            whole_copy.start()

        @pl.when(quarter == full)
        def _():
            last[part] = blocks[index, :TAPS, :spare]
            bias[part] = blocks[index, 0, spare : spare + 1]
            last_copy.start()
            bias_copy.start()

        for copy in small_copies:
            copy.start()
        finish.append((quarter, whole_copy, last_copy, bias_copy, small_copies))
    for quarter, whole_copy, last_copy, bias_copy, small_copies in finish:
        @pl.when(quarter < full)
        def _():
            whole_copy.wait()

        @pl.when(quarter == full)
        def _():
            last_copy.wait()
            bias_copy.wait()

        for copy in small_copies:
            copy.wait()


def shards(
    grid_input, w_stem, b_stem, w_edge, w_node, src_index, dst_index, counts, mesh_cotangent
):
    rows_here, cols_here, channels = grid_input.shape
    width = w_edge.shape[0]
    bands = lax.axis_size("band")
    columns = lax.axis_size("chip") * 2
    chips = bands * lax.axis_size("chip")
    core = lax.axis_index("core")
    device_count = 2 * chips
    slot_count = src_index.shape[2]
    slots = device_count * slot_count
    half_rows = rows_here // 2
    half_cols = cols_here // 2
    points = half_rows * half_cols
    half_width = width // 2
    node_total = mesh_cotangent.shape[0]
    bf16, f32 = jnp.bfloat16, jnp.float32

    west = lax.ppermute(
        grid_input[:, -1:, :], ("chip", "core"), [(i, (i + 1) % columns) for i in range(columns)]
    )
    north = lax.ppermute(grid_input[-1:], "band", [(i, i + 1) for i in range(bands - 1)])
    corner = lax.ppermute(
        grid_input[-1:, -1:],
        EVERY,
        [
            (i * columns + j, (i + 1) * columns + (j + 1) % columns)
            for i in range(bands - 1)
            for j in range(columns)
        ],
    )
    flat_src = src_index.reshape(device_count, slot_count)
    slot_live = jnp.arange(slot_count, dtype=jnp.int32)[None, :] < counts.reshape(device_count, 1)
    source = jnp.where(slot_live, flat_src, -1)

    steps = slots // TILE
    even, odd, slope, outgoing = pl.pallas_call(
        stem_kernel,
        out_shape=(
            pltpu.HBM((3, half_rows, half_cols, width), bf16),
            pltpu.HBM((3, half_rows + 1, half_cols, width), bf16),
            pltpu.HBM((points, width), f32),
            pltpu.HBM((slots, width), bf16),
        ),
        in_specs=[whole()] * 7 + [whole(pltpu.HBM)] * 2,
        out_specs=(whole(pltpu.HBM),) * 4,
        scratch_shapes=[
            pltpu.VMEM((rows_here, cols_here, channels), bf16),
            pltpu.VMEM((TAPS, channels, width), bf16),
            pltpu.VMEM((TAPS * width, width), bf16),
            pltpu.VMEM((3, half_rows, half_cols, width), bf16),
            pltpu.VMEM((3, half_rows + 1, half_cols, width), bf16),
            pltpu.VMEM((points, width), bf16),
            pltpu.VMEM((points, width), f32),
            pltpu.VMEM((slots, width), bf16),
            pltpu.SemaphoreType.DMA((4,)),
            pltpu.SemaphoreType.DMA((TAPS,)),
            pltpu.SemaphoreType.DMA((2,)),
            pltpu.SemaphoreType.DMA((points // TILE,)),
            pltpu.SemaphoreType.DMA((steps,)),
        ],
        compiler_params=params(56),
        name="stem",
    )(
        west.reshape(half_rows, 2, 1, channels),
        north,
        corner,
        column_picker(4, cols_here),
        column_picker(1, cols_here),
        b_stem.reshape(1, width),
        source.reshape(slots, 1),
        grid_input,
        w_stem,
    )

    incoming = lax.all_to_all(
        outgoing.reshape(device_count, slot_count, width), EVERY, split_axis=0, concat_axis=0, tiled=True
    )
    arrived = incoming.reshape(slots, width)

    patches = pl.pallas_call(
        functools.partial(flip_kernel, channels),
        grid=(TAPS,),
        out_shape=pltpu.HBM((TAPS, width, points), bf16),
        in_specs=[
            pl.BlockSpec((3, half_rows, half_cols, width), lambda t: (0, 0, 0, 0)),
            pl.BlockSpec((3, half_rows + 1, half_cols, width), lambda t: (0, 0, 0, 0)),
        ],
        out_specs=pl.BlockSpec((1, width, points), lambda t: (t, 0, 0)),
        compiler_params=params(56),
        cost_estimate=cost(0, 16 * MIB),
        name="flip",
    )(even, odd)
    grad_agg = right_dot(mesh_cotangent, w_node).astype(bf16)
    dst_flat = dst_index.reshape(slots)

    dst_row = dst_flat.reshape(1, slots)
    w_flipped = w_edge.T

    def edge_call(side):
        outs = 2 if side else 1
        return pl.pallas_call(
            functools.partial(edge_kernel, side),
            out_shape=(pltpu.HBM((slots, width), bf16),) * outs,
            in_specs=[whole()] * 4 + [whole(pltpu.HBM)],
            out_specs=(whole(pltpu.HBM),) * outs,
            scratch_shapes=[pltpu.VMEM((slots, width), bf16)] * (1 + outs)
            + [pltpu.SemaphoreType.DMA((2,)), pltpu.SemaphoreType.DMA((outs, 2))],
            compiler_params=params(40),
            cost_estimate=cost(4 * slots * width * width, 8 * MIB),
            name="edge_side" if side else "edge_back",
        )(w_edge, w_flipped, dst_row, grad_agg, arrived)

    (back,) = edge_call(False)

    returned = lax.all_to_all(
        back.reshape(device_count, slot_count, width), EVERY, split_axis=0, concat_axis=0, tiled=True
    ).reshape(slots, width)

    messages, grad_pre = edge_call(True)
    node_ids = jnp.arange(node_total, dtype=jnp.int32)
    onehot = (node_ids[:, None] == dst_flat[None, :]).astype(bf16)
    aggregate = f32_dot(onehot, messages).astype(bf16)
    mesh_out = f32_dot(aggregate, w_node).astype(bf16)
    grad_node = inner_dot(aggregate, mesh_cotangent).astype(bf16)
    grad_edge = inner_dot(arrived, grad_pre).astype(bf16)
    mesh_out, grad_edge, grad_node = lax.optimization_barrier((mesh_out, grad_edge, grad_node))

    blocks = TAPS + 2
    band, chip = lax.axis_index("band"), lax.axis_index("chip")
    up = band // LINE
    where = jnp.where(
        core == 0, jnp.stack([core, 1 - core, chip, up]), jnp.stack([core, 1 - core, up, chip])
    )
    depth = width // LINE
    source_row = source.reshape(1, slots)
    quarter_shape = (blocks, depth, half_width)
    quarters = pl.pallas_call(
        gradients_kernel,
        out_shape=(jax.ShapeDtypeStruct(quarter_shape, bf16),) * (2 * LINE),
        in_specs=[whole(pltpu.SMEM), whole()] + [whole(pltpu.HBM)] * 5,
        out_specs=(whole(pl.ANY),) * (2 * LINE),
        scratch_shapes=[
            pltpu.VMEM((slots, width), bf16),
            pltpu.VMEM((points, width), f32),
            pltpu.VMEM((points, width), bf16),
            pltpu.VMEM((TAPS, width, points), bf16),
            pltpu.VMEM((2, width, width), bf16),
            pltpu.VMEM((2, blocks, width, half_width), bf16),
            pltpu.SemaphoreType.DMA((2,)),
            pltpu.SemaphoreType.DMA((TAPS,)),
            pltpu.SemaphoreType.DMA((2,)),
            pltpu.SemaphoreType.DMA((2, LINE)),
        ],
        compiler_params=params(51),
        name="gradients",
    )(where, source_row, returned, slope, grad_edge, grad_node, patches)

    sent, kept = quarters[:LINE], quarters[LINE:]
    steps_out = ORDER[:-1]
    received = [core_swap(array) for array in sent[:-1]]
    chip_sums = [
        (one.astype(f32) + other.astype(f32)).astype(bf16) for one, other in zip(kept, received)
    ]
    arrived_parts = [
        lax.ppermute(chip_sum, EVERY, line_pairs(step)) for step, chip_sum in zip(steps_out, chip_sums)
    ]
    sent_own, chip_sums[-1] = lax.optimization_barrier((sent[-1], chip_sums[-1]))
    received_own = core_swap(sent_own)
    part = (chips // LINE, blocks, 16, 128)
    line_sum = pl.pallas_call(
        line_sum_kernel,
        out_shape=jax.ShapeDtypeStruct(part, bf16),
        in_specs=[whole()] * 5,
        out_specs=whole(),
        compiler_params=params(16),
        name="line_sum",
    )(kept[-1], received_own, *arrived_parts)
    planes = plane_groups()
    pieces = lax.all_to_all(
        line_sum, EVERY, split_axis=0, concat_axis=0, tiled=True, axis_index_groups=planes
    )
    summed = jnp.sum(pieces.astype(f32), axis=0).astype(bf16)
    mine = lax.all_to_all(
        jnp.broadcast_to(summed[None], part), EVERY, split_axis=0, concat_axis=0, tiled=True,
        axis_index_groups=planes,
    )
    held = [lax.ppermute(mine, EVERY, line_pairs(step)) for step in steps_out]
    out_shape = (
        pltpu.HBM((TAPS, channels, width), f32),
        pltpu.HBM((1, width), f32),
        pltpu.HBM((width, width), f32),
        pltpu.HBM((width, width), f32),
    )

    def final(steps, pieces, before):
        count = len(pieces)
        return pl.pallas_call(
            functools.partial(final_kernel, steps),
            out_shape=out_shape,
            in_specs=[whole(pltpu.SMEM)] + [whole()] * count + [whole(pltpu.HBM)] * len(before),
            out_specs=(whole(pltpu.HBM),) * 4,
            scratch_shapes=[
                pltpu.VMEM((count, blocks, depth, half_width), f32),
                pltpu.VMEM((2, TAPS, channels % depth, half_width), f32),
                pltpu.VMEM((2, 1, half_width), f32),
                pltpu.SemaphoreType.DMA((count,)),
                pltpu.SemaphoreType.DMA((count, 2)),
                pltpu.SemaphoreType.DMA((count,)),
            ],
            input_output_aliases={1 + count + i: i for i in range(len(before))},
            compiler_params=params(26),
            cost_estimate=cost(0, 2 * MIB * count),
            name="final_own" if len(before) == 0 else "final_line",
        )(where, *pieces, *before)

    results = final((0,), [mine, core_swap(mine)], ())
    held[0], *results = lax.optimization_barrier((held[0], *results))
    others = [core_swap(held[0]), core_swap(held[1])]
    last, others[0] = lax.optimization_barrier((held[2], others[0]))
    others.append(core_swap(last))
    pieces = [array for pair in zip(held, others) for array in pair]
    results = final(steps_out, pieces, results)
    grad_stem, grad_bias, out_edge, out_node = results
    return (mesh_out, grad_stem, grad_bias.reshape(width), out_edge, out_node)


def solution(mesh):
    bands, columns = mesh.devices.shape
    fine = Mesh(mesh.devices.reshape(bands, columns // 2, 2), EVERY)
    in_specs = (
        P("band", ("chip", "core"), None),
        P(),
        P(),
        P(),
        P(),
        P(EVERY, None, None),
        P(EVERY, None, None),
        P(EVERY, None),
        P(EVERY, None),
    )
    out_specs = (P(EVERY, None), P(), P(), P(), P())
    return jax.shard_map(shards, mesh=fine, in_specs=in_specs, out_specs=out_specs, check_vma=False)
```

```python
import functools
import itertools

import jax
import jax.numpy as jnp
from jax import lax
from jax.experimental import pallas as pl
from jax.experimental.pallas import tpu as pltpu
from jax.sharding import Mesh, PartitionSpec as P

EVERY = ("band", "chip", "core")
TAPS = 9
LINE = 4
ORDER = (2, 1, 3, 0)
MIB = 1024 * 1024
TILE = 512


def f32_dot(first, second):
    return jnp.dot(first, second, preferred_element_type=jnp.float32)


def inner_dot(first, second):
    return lax.dot_general(
        first, second, (((0,), (0,)), ((), ())), preferred_element_type=jnp.float32
    )


def right_dot(first, second):
    return lax.dot_general(
        first, second, (((1,), (1,)), ((), ())), preferred_element_type=jnp.float32
    )


def core_swap(array):
    return lax.ppermute(array, "core", [(0, 1), (1, 0)])


def device_number(y, z, x, core):
    return ((y * LINE + z) * LINE + x) * 2 + core


def line_pairs(step):
    pairs = []
    for y, z, x in itertools.product(range(LINE), repeat=3):
        pairs.append((device_number(y, z, x, 0), device_number(y, z, (x + step) % LINE, 0)))
        pairs.append((device_number(y, z, x, 1), device_number((y + step) % LINE, z, x, 1)))
    return pairs


def plane_groups():
    planes = []
    for fixed in range(LINE):
        rest = list(itertools.product(range(LINE), repeat=2))
        planes.append([device_number(y, z, fixed, 0) for y, z in rest])
        planes.append([device_number(fixed, z, x, 1) for x, z in rest])
    return planes


def whole(memory=pltpu.VMEM):
    return pl.BlockSpec(memory_space=memory)


def params(mib):
    return pltpu.CompilerParams(vmem_limit_bytes=mib * MIB)


def cost(flops, moved):
    return pl.CostEstimate(flops=int(flops), bytes_accessed=int(moved), transcendentals=0)


def rows_at(number, size=TILE):
    return pl.ds(pl.multiple_of(number * size, size), size)


def unrolled(count):
    return pl.loop(0, count, unroll=True)


def stem_kernel(
    west_ref, north_ref, corner_ref, bias_ref, source_ref,
    grid_hbm, w_hbm, even_hbm, odd_hbm, slope_hbm, out_hbm,
    grid, wide, raw, weights, even, odd, latent, slope, out, in_sems, w_sems, out_sems, slope_sems, row_sems,
):
    rows, cols, channels = grid.shape
    half_rows, half_cols = rows // 2, cols // 2
    width = even.shape[-1]
    chunks = in_sems.shape[0]
    per_chunk = rows // chunks
    bf16 = jnp.bfloat16

    loads = [
        pltpu.make_async_copy(
            grid_hbm.at[rows_at(chunk, per_chunk)], grid.at[rows_at(chunk, per_chunk)], in_sems.at[chunk]
        )
        for chunk in range(chunks)
    ]
    w_loads = [
        pltpu.make_async_copy(w_hbm.at[tap], raw.at[tap], w_sems.at[tap]) for tap in range(TAPS)
    ]
    for copy in loads:
        copy.start()

    gap = channels // 16 * 16
    for tap in range(TAPS):
        weights[tap * width + gap : (tap + 1) * width] = jnp.zeros((width - gap, width), bf16)
    wide[...] = jnp.zeros_like(wide)
    edge = 8

    lanes = wide.shape[-1]

    def phases(slot, columns, west, target, line):
        columns, west = columns.astype(jnp.float32), west.astype(jnp.float32)
        for number in range(width // lanes):
            here = slice(number * lanes, min((number + 1) * lanes, channels))
            held = wide.at[slot, number]
            held[edge : edge + cols, : here.stop - here.start] = columns[:, here]
            held[edge - 1 : edge, : here.stop - here.start] = west[:, here]
            for tap in range(3):
                taken = wide[slot, number, pl.ds(edge - 1 + tap, half_cols, stride=2), :]
                target[tap, line, :, number * lanes : (number + 1) * lanes] = taken.astype(bf16)

    phases(0, north_ref[0], corner_ref[0], odd, 0)
    slots_wide = wide.shape[0]
    for chunk in range(chunks):
        loads[chunk].wait()
        if chunk == chunks - 2:
            for copy in w_loads:
                copy.start()

        @unrolled(per_chunk // slots_wide)
        def _(step):
            first = chunk * per_chunk + slots_wide * step
            pair = chunk * (per_chunk // 2) + (slots_wide // 2) * step
            for slot in range(slots_wide):
                target = odd if slot % 2 else even
                phases(
                    slot, grid[first + slot], west_ref[first + slot], target,
                    pair + slot // 2 + slot % 2,
                )

    phase_copies = [
        pltpu.make_async_copy(even, even_hbm, out_sems.at[0]),
        pltpu.make_async_copy(odd, odd_hbm, out_sems.at[1]),
    ]
    for tap in range(TAPS):
        w_loads[tap].wait()
        weights[tap * width : tap * width + channels] = raw[tap]
    for copy in phase_copies:
        copy.start()

    tile_rows = TILE // half_cols
    points = latent.shape[0]

    def slope_copy(step):
        here = rows_at(step)
        return pltpu.make_async_copy(slope.at[here], slope_hbm.at[here], slope_sems.at[step])

    def row_copy(step):
        here = rows_at(step)
        return pltpu.make_async_copy(out.at[here], out_hbm.at[here], row_sems.at[step])

    @unrolled(points // TILE)
    def _(step):
        pieces = []
        for row_tap in range(3):
            for col_tap in range(3):
                first = step * tile_rows + (row_tap // 2)
                held = even if row_tap == 1 else odd
                pieces.append(held[col_tap, pl.ds(first, tile_rows)].reshape(TILE, width))
        pre = f32_dot(jnp.concatenate(pieces, axis=1), weights[...]) + bias_ref[...]
        sigmoid = jax.nn.sigmoid(pre)
        here = rows_at(step)
        slope[here] = sigmoid * (1.0 + pre * (1.0 - sigmoid))
        latent[here] = (pre * sigmoid).astype(bf16)
        slope_copy(step).start()

    @unrolled(out.shape[0] // TILE)
    def _(step):
        here = rows_at(step)
        point = lax.broadcasted_iota(jnp.int32, (TILE, points), 1)
        pick = jnp.where(point == source_ref[here], 1.0, 0.0).astype(bf16)
        out[here] = f32_dot(pick, latent[...]).astype(bf16)
        row_copy(step).start()

    for copy in phase_copies:
        copy.wait()

    @pl.loop(0, points // TILE)
    def _(step):
        slope_copy(step).wait()

    @pl.loop(0, out.shape[0] // TILE)
    def _(step):
        row_copy(step).wait()


def flip_kernel(channels, even_ref, odd_ref, out_ref):
    number = pl.program_id(0)
    row_tap = number // 3
    col_tap = number % 3
    half_rows, half_cols, width = even_ref.shape[1:]

    def write(values):
        flipped = values.reshape(half_rows * half_cols, width).T
        line = lax.broadcasted_iota(jnp.int32, flipped.shape, 0)
        ones = (line == channels) & (number == 0)
        out_ref[0] = jnp.where(ones, 1.0, flipped.astype(jnp.float32)).astype(jnp.bfloat16)

    @pl.when(row_tap == 1)
    def _():
        write(even_ref[col_tap])

    @pl.when(row_tap != 1)
    def _():
        write(odd_ref[col_tap, pl.ds(row_tap // 2, half_rows)])


def edge_kernel(side, w_ref, dst_ref, agg_ref, rows_hbm, *refs):
    outs = 2 if side else 1
    placed, (rows, *kept) = refs[:outs], refs[outs : 2 * outs + 1]
    flipped_ref, in_sems, out_sems = refs[2 * outs + 1 :]
    nodes = agg_ref.shape[0]
    tiles = in_sems.shape[0]
    tile = rows.shape[0] // tiles
    bf16 = jnp.bfloat16

    def load(step):
        here = rows_at(step, tile)
        return pltpu.make_async_copy(rows_hbm.at[here], rows.at[here], in_sems.at[step])

    def stores(step):
        here = rows_at(step, tile)
        return [
            pltpu.make_async_copy(kept[i].at[here], placed[i].at[here], out_sems.at[i, step])
            for i in range(outs)
        ]

    load(0).start()
    if not side:
        flipped_ref[...] = w_ref[...].T

    @unrolled(tiles)
    def _(step):
        here = rows_at(step, tile)
        node = lax.broadcasted_iota(jnp.int32, (nodes, tile), 0)
        pick = jnp.where(node == dst_ref[:, here], 1.0, 0.0).astype(bf16)
        grad_msg = inner_dot(pick, agg_ref[...])
        load(step).wait()

        @pl.when(step + 1 < tiles)
        def _():
            load(step + 1).start()

        pre = f32_dot(rows[here], w_ref[...])
        sigmoid = jax.nn.sigmoid(pre)
        grad_pre = (grad_msg * (sigmoid * (1.0 + pre * (1.0 - sigmoid)))).astype(bf16)
        if side:
            kept[0][here] = (pre * sigmoid).astype(bf16)
            kept[1][here] = grad_pre
        else:
            kept[0][here] = f32_dot(grad_pre, flipped_ref[...]).astype(bf16)
        for copy in stores(step):
            copy.start()

    for step in range(tiles):
        for copy in stores(step):
            copy.wait()


def quarter_of(spot, step):
    return lax.rem(spot + step + LINE, LINE)


def gradients_kernel(
    where_ref, source_ref, returned_hbm, slope_hbm, edge_hbm, node_hbm, patches_hbm,
    *refs,
):
    placed = (refs[:LINE], refs[LINE : 2 * LINE])
    (
        returned, slope, stemout, patches, smalls, out, before_sems, patch_sems, small_sems, out_sems,
    ) = refs[2 * LINE :]
    half_width = out.shape[3]
    depth = out.shape[2] // LINE
    points, width = stemout.shape
    slots = returned.shape[0]
    bf16 = jnp.bfloat16
    before = [
        pltpu.make_async_copy(returned_hbm, returned, before_sems.at[0]),
        pltpu.make_async_copy(slope_hbm, slope, before_sems.at[1]),
    ]
    patch_loads = [
        pltpu.make_async_copy(patches_hbm.at[tap], patches.at[tap], patch_sems.at[tap])
        for tap in range(TAPS)
    ]
    small_loads = [
        pltpu.make_async_copy(placed, smalls.at[number], small_sems.at[number])
        for number, placed in enumerate((edge_hbm, node_hbm))
    ]

    def stores(part):
        copies = []
        for slot in range(LINE):
            quarter = quarter_of(where_ref[3 - part], ORDER[slot])
            copies.append(
                pltpu.make_async_copy(out.at[part, :, pl.ds(pl.multiple_of(quarter * depth, depth), depth)], placed[part][slot], out_sems.at[part, slot])
            )
        return copies

    def finish(block, part, values):
        out[part, block] = values.astype(bf16)

    def columns(part):
        return pl.ds(pl.multiple_of(where_ref[1 - part] * half_width, half_width), half_width)

    for copy in before:
        copy.start()
    for copy in before:
        copy.wait()
    for copy in patch_loads + small_loads:
        copy.start()

    @unrolled(points // TILE)
    def _(tile):
        here = rows_at(tile)
        point = lax.broadcasted_iota(jnp.int32, (TILE, slots), 0) + tile * TILE
        pick = jnp.where(point == source_ref[...], 1.0, 0.0).astype(bf16)
        grad_latent = f32_dot(pick, returned[...])
        stemout[here] = (grad_latent * slope[here]).astype(bf16)

    for part in range(2):
        for tap in range(TAPS):
            if part == 0 and tap in (0, TAPS // 2):
                for copy in patch_loads[tap : TAPS // 2 if tap == 0 else TAPS]:
                    copy.wait()
            finish(tap, part, f32_dot(patches[tap], stemout[:, columns(part)]))
        for number in range(2):
            if part == 0:
                small_loads[number].wait()
            finish(TAPS + number, part, smalls[number, :, columns(part)])
        for copy in stores(part):
            copy.start()
    for part in range(2):
        for copy in stores(part):
            copy.wait()


def line_sum_kernel(kept_ref, received_ref, one_ref, two_ref, three_ref, out_ref):
    for piece in range(out_ref.shape[0]):
        here = (slice(None), pl.ds(piece // 2 * 16, 16), pl.ds(piece % 2 * 128, 128))
        total = kept_ref[here].astype(jnp.float32)
        for ref in (received_ref, one_ref, two_ref, three_ref):
            total = total + ref[here].astype(jnp.float32)
        out_ref[piece] = total.astype(out_ref.dtype)


def final_kernel(steps, where_ref, *refs):
    held = refs[: 2 * len(steps)]
    stem_hbm, bias_hbm, edge_hbm, node_hbm, blocks, last, bias, stem_sems, small_sems, bias_sems = refs[-10:]
    channels = stem_hbm.shape[1]
    depth, half_width = blocks.shape[2:]
    full = channels // depth
    spare = channels - full * depth
    finish = []
    for index, ref in enumerate(held):
        part = index % 2
        quarter = quarter_of(where_ref[2 + part], -steps[index // 2])
        half = where_ref[part]
        rows = pl.ds(pl.multiple_of(quarter * depth, depth), depth)
        columns = pl.ds(pl.multiple_of(half * half_width, half_width), half_width)
        for piece in range(ref.shape[0]):
            row, lane = piece // 2 * 16, piece % 2 * 128
            blocks[index, :, row : row + 16, lane : lane + 128] = ref[piece].astype(jnp.float32)
        whole_copy = pltpu.make_async_copy(
            blocks.at[index, pl.ds(0, TAPS)], stem_hbm.at[:, rows, columns], stem_sems.at[index]
        )
        last_copy = pltpu.make_async_copy(
            last.at[part], stem_hbm.at[:, pl.ds(full * depth, spare), columns], stem_sems.at[index]
        )
        bias_copy = pltpu.make_async_copy(bias.at[part], bias_hbm.at[:, columns], bias_sems.at[index])
        small_copies = [
            pltpu.make_async_copy(
                blocks.at[index, TAPS + number], placed.at[rows, columns], small_sems.at[index, number]
            )
            for number, placed in enumerate((edge_hbm, node_hbm))
        ]

        @pl.when(quarter < full)
        def _():
            whole_copy.start()

        @pl.when(quarter == full)
        def _():
            last[part] = blocks[index, :TAPS, :spare]
            bias[part] = blocks[index, 0, spare : spare + 1]
            last_copy.start()
            bias_copy.start()

        for copy in small_copies:
            copy.start()
        finish.append((quarter, whole_copy, last_copy, bias_copy, small_copies))
    for quarter, whole_copy, last_copy, bias_copy, small_copies in finish:
        @pl.when(quarter < full)
        def _():
            whole_copy.wait()

        @pl.when(quarter == full)
        def _():
            last_copy.wait()
            bias_copy.wait()

        for copy in small_copies:
            copy.wait()


def shards(
    grid_input, w_stem, b_stem, w_edge, w_node, src_index, dst_index, counts, mesh_cotangent
):
    rows_here, cols_here, channels = grid_input.shape
    width = w_edge.shape[0]
    bands = lax.axis_size("band")
    columns = lax.axis_size("chip") * 2
    chips = bands * lax.axis_size("chip")
    core = lax.axis_index("core")
    device_count = 2 * chips
    slot_count = src_index.shape[2]
    slots = device_count * slot_count
    half_rows = rows_here // 2
    half_cols = cols_here // 2
    points = half_rows * half_cols
    half_width = width // 2
    node_total = mesh_cotangent.shape[0]
    bf16, f32 = jnp.bfloat16, jnp.float32

    west = lax.ppermute(
        grid_input[:, -1:, :], ("chip", "core"), [(i, (i + 1) % columns) for i in range(columns)]
    )
    north = lax.ppermute(grid_input[-1:], "band", [(i, i + 1) for i in range(bands - 1)])
    corner = lax.ppermute(
        grid_input[-1:, -1:],
        EVERY,
        [
            (i * columns + j, (i + 1) * columns + (j + 1) % columns)
            for i in range(bands - 1)
            for j in range(columns)
        ],
    )
    flat_src = src_index.reshape(device_count, slot_count)
    slot_live = jnp.arange(slot_count, dtype=jnp.int32)[None, :] < counts.reshape(device_count, 1)
    source = jnp.where(slot_live, flat_src, -1)

    steps = slots // TILE
    even, odd, slope, outgoing = pl.pallas_call(
        stem_kernel,
        out_shape=(
            pltpu.HBM((3, half_rows, half_cols, width), bf16),
            pltpu.HBM((3, half_rows + 1, half_cols, width), bf16),
            pltpu.HBM((points, width), f32),
            pltpu.HBM((slots, width), bf16),
        ),
        in_specs=[whole()] * 5 + [whole(pltpu.HBM)] * 2,
        out_specs=(whole(pltpu.HBM),) * 4,
        scratch_shapes=[
            pltpu.VMEM((rows_here, cols_here, channels), bf16),
            pltpu.VMEM((4, width // 128, cols_here + 16, 128), f32),
            pltpu.VMEM((TAPS, channels, width), bf16),
            pltpu.VMEM((TAPS * width, width), bf16),
            pltpu.VMEM((3, half_rows, half_cols, width), bf16),
            pltpu.VMEM((3, half_rows + 1, half_cols, width), bf16),
            pltpu.VMEM((points, width), bf16),
            pltpu.VMEM((points, width), f32),
            pltpu.VMEM((slots, width), bf16),
            pltpu.SemaphoreType.DMA((4,)),
            pltpu.SemaphoreType.DMA((TAPS,)),
            pltpu.SemaphoreType.DMA((2,)),
            pltpu.SemaphoreType.DMA((points // TILE,)),
            pltpu.SemaphoreType.DMA((steps,)),
        ],
        compiler_params=params(56),
        name="stem",
    )(
        west,
        north,
        corner,
        b_stem.reshape(1, width),
        source.reshape(slots, 1),
        grid_input,
        w_stem,
    )

    incoming = lax.all_to_all(
        outgoing.reshape(device_count, slot_count, width), EVERY, split_axis=0, concat_axis=0, tiled=True
    )
    arrived = incoming.reshape(slots, width)

    patches = pl.pallas_call(
        functools.partial(flip_kernel, channels),
        grid=(TAPS,),
        out_shape=pltpu.HBM((TAPS, width, points), bf16),
        in_specs=[
            pl.BlockSpec((3, half_rows, half_cols, width), lambda t: (0, 0, 0, 0)),
            pl.BlockSpec((3, half_rows + 1, half_cols, width), lambda t: (0, 0, 0, 0)),
        ],
        out_specs=pl.BlockSpec((1, width, points), lambda t: (t, 0, 0)),
        compiler_params=params(56),
        cost_estimate=cost(0, 16 * MIB),
        name="flip",
    )(even, odd)
    grad_agg = right_dot(mesh_cotangent, w_node).astype(bf16)
    dst_flat = dst_index.reshape(slots)

    dst_row = dst_flat.reshape(1, slots)

    def edge_call(side):
        outs = 2 if side else 1
        return pl.pallas_call(
            functools.partial(edge_kernel, side),
            out_shape=(pltpu.HBM((slots, width), bf16),) * outs,
            in_specs=[whole()] * 3 + [whole(pltpu.HBM)],
            out_specs=(whole(pltpu.HBM),) * outs,
            scratch_shapes=[pltpu.VMEM((slots, width), bf16)] * (1 + outs)
            + [pltpu.VMEM((width, width), bf16)]
            + [pltpu.SemaphoreType.DMA((2,)), pltpu.SemaphoreType.DMA((outs, 2))],
            compiler_params=params(40),
            cost_estimate=cost(4 * slots * width * width, 8 * MIB),
            name="edge_side" if side else "edge_back",
        )(w_edge, dst_row, grad_agg, arrived)

    (back,) = edge_call(False)

    returned = lax.all_to_all(
        back.reshape(device_count, slot_count, width), EVERY, split_axis=0, concat_axis=0, tiled=True
    ).reshape(slots, width)

    messages, grad_pre = edge_call(True)
    node_ids = jnp.arange(node_total, dtype=jnp.int32)
    onehot = (node_ids[:, None] == dst_flat[None, :]).astype(bf16)
    aggregate = f32_dot(onehot, messages).astype(bf16)
    mesh_out = f32_dot(aggregate, w_node).astype(bf16)
    grad_node = inner_dot(aggregate, mesh_cotangent).astype(bf16)
    grad_edge = inner_dot(arrived, grad_pre).astype(bf16)
    mesh_out, grad_edge, grad_node = lax.optimization_barrier((mesh_out, grad_edge, grad_node))

    blocks = TAPS + 2
    band, chip = lax.axis_index("band"), lax.axis_index("chip")
    up = band // LINE
    where = jnp.where(
        core == 0, jnp.stack([core, 1 - core, chip, up]), jnp.stack([core, 1 - core, up, chip])
    )
    depth = width // LINE
    source_row = source.reshape(1, slots)
    quarter_shape = (blocks, depth, half_width)
    quarters = pl.pallas_call(
        gradients_kernel,
        out_shape=(jax.ShapeDtypeStruct(quarter_shape, bf16),) * (2 * LINE),
        in_specs=[whole(pltpu.SMEM), whole()] + [whole(pltpu.HBM)] * 5,
        out_specs=(whole(pl.ANY),) * (2 * LINE),
        scratch_shapes=[
            pltpu.VMEM((slots, width), bf16),
            pltpu.VMEM((points, width), f32),
            pltpu.VMEM((points, width), bf16),
            pltpu.VMEM((TAPS, width, points), bf16),
            pltpu.VMEM((2, width, width), bf16),
            pltpu.VMEM((2, blocks, width, half_width), bf16),
            pltpu.SemaphoreType.DMA((2,)),
            pltpu.SemaphoreType.DMA((TAPS,)),
            pltpu.SemaphoreType.DMA((2,)),
            pltpu.SemaphoreType.DMA((2, LINE)),
        ],
        compiler_params=params(51),
        name="gradients",
    )(where, source_row, returned, slope, grad_edge, grad_node, patches)

    sent, kept = quarters[:LINE], quarters[LINE:]
    steps_out = ORDER[:-1]
    received = [core_swap(array) for array in sent[:-1]]
    chip_sums = [
        (one.astype(f32) + other.astype(f32)).astype(bf16) for one, other in zip(kept, received)
    ]
    arrived_parts = [
        lax.ppermute(chip_sum, EVERY, line_pairs(step)) for step, chip_sum in zip(steps_out, chip_sums)
    ]
    sent_own, chip_sums[-1] = lax.optimization_barrier((sent[-1], chip_sums[-1]))
    received_own = core_swap(sent_own)
    part = (chips // LINE, blocks, 16, 128)
    line_sum = pl.pallas_call(
        line_sum_kernel,
        out_shape=jax.ShapeDtypeStruct(part, bf16),
        in_specs=[whole()] * 5,
        out_specs=whole(),
        compiler_params=params(16),
        name="line_sum",
    )(kept[-1], received_own, *arrived_parts)
    planes = plane_groups()
    pieces = lax.all_to_all(
        line_sum, EVERY, split_axis=0, concat_axis=0, tiled=True, axis_index_groups=planes
    )
    summed = jnp.sum(pieces.astype(f32), axis=0).astype(bf16)
    mine = lax.all_to_all(
        jnp.broadcast_to(summed[None], part), EVERY, split_axis=0, concat_axis=0, tiled=True,
        axis_index_groups=planes,
    )
    held = [lax.ppermute(mine, EVERY, line_pairs(step)) for step in steps_out]
    out_shape = (
        pltpu.HBM((TAPS, channels, width), f32),
        pltpu.HBM((1, width), f32),
        pltpu.HBM((width, width), f32),
        pltpu.HBM((width, width), f32),
    )

    def final(steps, pieces, before):
        count = len(pieces)
        return pl.pallas_call(
            functools.partial(final_kernel, steps),
            out_shape=out_shape,
            in_specs=[whole(pltpu.SMEM)] + [whole()] * count + [whole(pltpu.HBM)] * len(before),
            out_specs=(whole(pltpu.HBM),) * 4,
            scratch_shapes=[
                pltpu.VMEM((count, blocks, depth, half_width), f32),
                pltpu.VMEM((2, TAPS, channels % depth, half_width), f32),
                pltpu.VMEM((2, 1, half_width), f32),
                pltpu.SemaphoreType.DMA((count,)),
                pltpu.SemaphoreType.DMA((count, 2)),
                pltpu.SemaphoreType.DMA((count,)),
            ],
            input_output_aliases={1 + count + i: i for i in range(len(before))},
            compiler_params=params(26),
            cost_estimate=cost(0, 2 * MIB * count),
            name="final_own" if len(before) == 0 else "final_line",
        )(where, *pieces, *before)

    results = final((0,), [mine, core_swap(mine)], ())
    held[0], *results = lax.optimization_barrier((held[0], *results))
    others = [core_swap(held[0]), core_swap(held[1])]
    last, others[0] = lax.optimization_barrier((held[2], others[0]))
    others.append(core_swap(last))
    pieces = [array for pair in zip(held, others) for array in pair]
    results = final(steps_out, pieces, results)
    grad_stem, grad_bias, out_edge, out_node = results
    return (mesh_out, grad_stem, grad_bias.reshape(width), out_edge, out_node)


def solution(mesh):
    bands, columns = mesh.devices.shape
    fine = Mesh(mesh.devices.reshape(bands, columns // 2, 2), EVERY)
    in_specs = (
        P("band", ("chip", "core"), None),
        P(),
        P(),
        P(),
        P(),
        P(EVERY, None, None),
        P(EVERY, None, None),
        P(EVERY, None),
        P(EVERY, None),
    )
    out_specs = (P(EVERY, None), P(), P(), P(), P())
    return jax.shard_map(shards, mesh=fine, in_specs=in_specs, out_specs=out_specs, check_vma=False)
```

```python
import functools
import itertools

import jax
import jax.numpy as jnp
from jax import lax
from jax.experimental import pallas as pl
from jax.experimental.pallas import tpu as pltpu
from jax.sharding import Mesh, PartitionSpec as P

EVERY = ("band", "chip", "core")
TAPS = 9
LINE = 4
ORDER = (1, 3, 2, 0)
MIB = 1024 * 1024
TILE = 512


def f32_dot(first, second):
    return jnp.dot(first, second, preferred_element_type=jnp.float32)


def inner_dot(first, second):
    return lax.dot_general(
        first, second, (((0,), (0,)), ((), ())), preferred_element_type=jnp.float32
    )


def right_dot(first, second):
    return lax.dot_general(
        first, second, (((1,), (1,)), ((), ())), preferred_element_type=jnp.float32
    )


def core_swap(array):
    return lax.ppermute(array, "core", [(0, 1), (1, 0)])


def device_number(y, z, x, core):
    return ((y * LINE + z) * LINE + x) * 2 + core


def line_pairs(step):
    pairs = []
    for y, z, x in itertools.product(range(LINE), repeat=3):
        pairs.append((device_number(y, z, x, 0), device_number(y, z, (x + step) % LINE, 0)))
        pairs.append((device_number(y, z, x, 1), device_number((y + step) % LINE, z, x, 1)))
    return pairs


def plane_groups():
    planes = []
    for fixed in range(LINE):
        rest = list(itertools.product(range(LINE), repeat=2))
        planes.append([device_number(y, z, fixed, 0) for y, z in rest])
        planes.append([device_number(fixed, z, x, 1) for x, z in rest])
    return planes


def whole(memory=pltpu.VMEM):
    return pl.BlockSpec(memory_space=memory)


def params(mib):
    return pltpu.CompilerParams(vmem_limit_bytes=mib * MIB)


def cost(flops, moved):
    return pl.CostEstimate(flops=int(flops), bytes_accessed=int(moved), transcendentals=0)


def rows_at(number, size=TILE):
    return pl.ds(pl.multiple_of(number * size, size), size)


def unrolled(count):
    return pl.loop(0, count, unroll=True)


def stem_kernel(
    west_ref, north_ref, corner_ref, bias_ref, source_ref,
    grid_hbm, w_hbm, even_hbm, odd_hbm, slope_hbm, out_hbm,
    grid, wide, raw, weights, even, odd, latent, slope, out, in_sems, w_sems, out_sems, slope_sems, row_sems,
):
    rows, cols, channels = grid.shape
    half_rows, half_cols = rows // 2, cols // 2
    width = even.shape[-1]
    chunks = in_sems.shape[0]
    per_chunk = rows // chunks
    bf16 = jnp.bfloat16

    loads = [
        pltpu.make_async_copy(
            grid_hbm.at[rows_at(chunk, per_chunk)], grid.at[rows_at(chunk, per_chunk)], in_sems.at[chunk]
        )
        for chunk in range(chunks)
    ]
    w_loads = [
        pltpu.make_async_copy(w_hbm.at[tap], raw.at[tap], w_sems.at[tap]) for tap in range(TAPS)
    ]
    for copy in loads:
        copy.start()

    gap = channels // 16 * 16
    for tap in range(TAPS):
        weights[tap * width + gap : (tap + 1) * width] = jnp.zeros((width - gap, width), bf16)
    wide[...] = jnp.zeros_like(wide)
    edge = 8

    lanes = wide.shape[-1]

    def phases(slot, columns, west, target, line):
        columns, west = columns.astype(jnp.float32), west.astype(jnp.float32)
        for number in range(width // lanes):
            here = slice(number * lanes, min((number + 1) * lanes, channels))
            held = wide.at[slot, number]
            held[edge : edge + cols, : here.stop - here.start] = columns[:, here]
            held[edge - 1 : edge, : here.stop - here.start] = west[:, here]
            for tap in range(3):
                taken = wide[slot, number, pl.ds(edge - 1 + tap, half_cols, stride=2), :]
                target[tap, line, :, number * lanes : (number + 1) * lanes] = taken.astype(bf16)

    phases(0, north_ref[0], corner_ref[0], odd, 0)
    slots_wide = wide.shape[0]
    for chunk in range(chunks):
        loads[chunk].wait()
        if chunk == chunks - 2:
            for copy in w_loads:
                copy.start()

        @unrolled(per_chunk // slots_wide)
        def _(step):
            first = chunk * per_chunk + slots_wide * step
            pair = chunk * (per_chunk // 2) + (slots_wide // 2) * step
            for slot in range(slots_wide):
                target = odd if slot % 2 else even
                phases(
                    slot, grid[first + slot], west_ref[first + slot], target,
                    pair + slot // 2 + slot % 2,
                )

    phase_copies = [
        pltpu.make_async_copy(even, even_hbm, out_sems.at[0]),
        pltpu.make_async_copy(odd, odd_hbm, out_sems.at[1]),
    ]
    for tap in range(TAPS):
        w_loads[tap].wait()
        weights[tap * width : tap * width + channels] = raw[tap]
    for copy in phase_copies:
        copy.start()

    tile_rows = TILE // half_cols
    points = latent.shape[0]

    def slope_copy(step):
        here = rows_at(step)
        return pltpu.make_async_copy(slope.at[here], slope_hbm.at[here], slope_sems.at[step])

    def row_copy(step):
        here = rows_at(step)
        return pltpu.make_async_copy(out.at[here], out_hbm.at[here], row_sems.at[step])

    @unrolled(points // TILE)
    def _(step):
        pieces = []
        for row_tap in range(3):
            for col_tap in range(3):
                first = step * tile_rows + (row_tap // 2)
                held = even if row_tap == 1 else odd
                pieces.append(held[col_tap, pl.ds(first, tile_rows)].reshape(TILE, width))
        pre = f32_dot(jnp.concatenate(pieces, axis=1), weights[...]) + bias_ref[...]
        sigmoid = jax.nn.sigmoid(pre)
        here = rows_at(step)
        slope[here] = sigmoid * (1.0 + pre * (1.0 - sigmoid))
        latent[here] = (pre * sigmoid).astype(bf16)
        slope_copy(step).start()

    @unrolled(out.shape[0] // TILE)
    def _(step):
        here = rows_at(step)
        point = lax.broadcasted_iota(jnp.int32, (TILE, points), 1)
        pick = jnp.where(point == source_ref[here], 1.0, 0.0).astype(bf16)
        out[here] = f32_dot(pick, latent[...]).astype(bf16)
        row_copy(step).start()

    for copy in phase_copies:
        copy.wait()

    @pl.loop(0, points // TILE)
    def _(step):
        slope_copy(step).wait()

    @pl.loop(0, out.shape[0] // TILE)
    def _(step):
        row_copy(step).wait()


def flip_kernel(channels, even_ref, odd_ref, out_ref):
    number = pl.program_id(0)
    row_tap = number // 3
    col_tap = number % 3
    half_rows, half_cols, width = even_ref.shape[1:]

    def write(values):
        flipped = values.reshape(half_rows * half_cols, width).T
        line = lax.broadcasted_iota(jnp.int32, flipped.shape, 0)
        ones = (line == channels) & (number == 0)
        out_ref[0] = jnp.where(ones, 1.0, flipped.astype(jnp.float32)).astype(jnp.bfloat16)

    @pl.when(row_tap == 1)
    def _():
        write(even_ref[col_tap])

    @pl.when(row_tap != 1)
    def _():
        write(odd_ref[col_tap, pl.ds(row_tap // 2, half_rows)])


def edge_kernel(side, w_ref, dst_ref, agg_ref, rows_hbm, *refs):
    outs = 2 if side else 1
    placed, (rows, *kept) = refs[:outs], refs[outs : 2 * outs + 1]
    flipped_ref, in_sems, out_sems = refs[2 * outs + 1 :]
    nodes = agg_ref.shape[0]
    tiles = in_sems.shape[0]
    tile = rows.shape[0] // tiles
    bf16 = jnp.bfloat16

    def load(step):
        here = rows_at(step, tile)
        return pltpu.make_async_copy(rows_hbm.at[here], rows.at[here], in_sems.at[step])

    def stores(step):
        here = rows_at(step, tile)
        return [
            pltpu.make_async_copy(kept[i].at[here], placed[i].at[here], out_sems.at[i, step])
            for i in range(outs)
        ]

    load(0).start()
    if not side:
        flipped_ref[...] = w_ref[...].T

    @unrolled(tiles)
    def _(step):
        here = rows_at(step, tile)
        node = lax.broadcasted_iota(jnp.int32, (nodes, tile), 0)
        pick = jnp.where(node == dst_ref[:, here], 1.0, 0.0).astype(bf16)
        grad_msg = inner_dot(pick, agg_ref[...])
        load(step).wait()

        @pl.when(step + 1 < tiles)
        def _():
            load(step + 1).start()

        pre = f32_dot(rows[here], w_ref[...])
        sigmoid = jax.nn.sigmoid(pre)
        grad_pre = (grad_msg * (sigmoid * (1.0 + pre * (1.0 - sigmoid)))).astype(bf16)
        if side:
            kept[0][here] = (pre * sigmoid).astype(bf16)
            kept[1][here] = grad_pre
        else:
            kept[0][here] = f32_dot(grad_pre, flipped_ref[...]).astype(bf16)
        for copy in stores(step):
            copy.start()

    for step in range(tiles):
        for copy in stores(step):
            copy.wait()


def quarter_of(spot, step):
    return lax.rem(spot + step + LINE, LINE)


def gradients_kernel(
    where_ref, source_ref, returned_hbm, slope_hbm, edge_hbm, node_hbm, patches_hbm,
    *refs,
):
    placed = (refs[:LINE], refs[LINE : 2 * LINE])
    (
        returned, slope, stemout, patches, smalls, out, before_sems, patch_sems, small_sems, out_sems,
    ) = refs[2 * LINE :]
    half_width = out.shape[3]
    depth = out.shape[2] // LINE
    points, width = stemout.shape
    slots = returned.shape[0]
    bf16 = jnp.bfloat16
    before = [
        pltpu.make_async_copy(returned_hbm, returned, before_sems.at[0]),
        pltpu.make_async_copy(slope_hbm, slope, before_sems.at[1]),
    ]
    patch_loads = [
        pltpu.make_async_copy(patches_hbm.at[tap], patches.at[tap], patch_sems.at[tap])
        for tap in range(TAPS)
    ]
    small_loads = [
        pltpu.make_async_copy(placed, smalls.at[number], small_sems.at[number])
        for number, placed in enumerate((edge_hbm, node_hbm))
    ]

    def stores(part):
        copies = []
        for slot in range(LINE):
            quarter = quarter_of(where_ref[3 - part], ORDER[slot])
            copies.append(
                pltpu.make_async_copy(out.at[part, :, pl.ds(pl.multiple_of(quarter * depth, depth), depth)], placed[part][slot], out_sems.at[part, slot])
            )
        return copies

    def finish(block, part, values):
        out[part, block] = values.astype(bf16)

    def columns(part):
        return pl.ds(pl.multiple_of(where_ref[1 - part] * half_width, half_width), half_width)

    for copy in before:
        copy.start()
    for copy in before:
        copy.wait()
    for copy in patch_loads + small_loads:
        copy.start()

    @unrolled(points // TILE)
    def _(tile):
        here = rows_at(tile)
        point = lax.broadcasted_iota(jnp.int32, (TILE, slots), 0) + tile * TILE
        pick = jnp.where(point == source_ref[...], 1.0, 0.0).astype(bf16)
        grad_latent = f32_dot(pick, returned[...])
        stemout[here] = (grad_latent * slope[here]).astype(bf16)

    for part in range(2):
        for tap in range(TAPS):
            if part == 0 and tap in (0, TAPS // 2):
                for copy in patch_loads[tap : TAPS // 2 if tap == 0 else TAPS]:
                    copy.wait()
            finish(tap, part, f32_dot(patches[tap], stemout[:, columns(part)]))
        for number in range(2):
            if part == 0:
                small_loads[number].wait()
            finish(TAPS + number, part, smalls[number, :, columns(part)])
        for copy in stores(part):
            copy.start()
    for part in range(2):
        for copy in stores(part):
            copy.wait()


def line_sum_kernel(kept_ref, received_ref, one_ref, two_ref, three_ref, out_ref):
    for piece in range(out_ref.shape[0]):
        here = (slice(None), pl.ds(piece // 2 * 16, 16), pl.ds(piece % 2 * 128, 128))
        total = kept_ref[here].astype(jnp.float32)
        for ref in (received_ref, one_ref, two_ref, three_ref):
            total = total + ref[here].astype(jnp.float32)
        out_ref[piece] = total.astype(out_ref.dtype)


def final_kernel(steps, where_ref, *refs):
    held = refs[: 2 * len(steps)]
    stem_hbm, bias_hbm, edge_hbm, node_hbm, blocks, last, bias, stem_sems, small_sems, bias_sems = refs[-10:]
    channels = stem_hbm.shape[1]
    depth, half_width = blocks.shape[2:]
    full = channels // depth
    spare = channels - full * depth
    finish = []
    for index, ref in enumerate(held):
        part = index % 2
        quarter = quarter_of(where_ref[2 + part], -steps[index // 2])
        half = where_ref[part]
        rows = pl.ds(pl.multiple_of(quarter * depth, depth), depth)
        columns = pl.ds(pl.multiple_of(half * half_width, half_width), half_width)
        for piece in range(ref.shape[0]):
            row, lane = piece // 2 * 16, piece % 2 * 128
            blocks[index, :, row : row + 16, lane : lane + 128] = ref[piece].astype(jnp.float32)
        whole_copy = pltpu.make_async_copy(
            blocks.at[index, pl.ds(0, TAPS)], stem_hbm.at[:, rows, columns], stem_sems.at[index]
        )
        last_copy = pltpu.make_async_copy(
            last.at[part], stem_hbm.at[:, pl.ds(full * depth, spare), columns], stem_sems.at[index]
        )
        bias_copy = pltpu.make_async_copy(bias.at[part], bias_hbm.at[:, columns], bias_sems.at[index])
        small_copies = [
            pltpu.make_async_copy(
                blocks.at[index, TAPS + number], placed.at[rows, columns], small_sems.at[index, number]
            )
            for number, placed in enumerate((edge_hbm, node_hbm))
        ]

        @pl.when(quarter < full)
        def _():
            whole_copy.start()

        @pl.when(quarter == full)
        def _():
            last[part] = blocks[index, :TAPS, :spare]
            bias[part] = blocks[index, 0, spare : spare + 1]
            last_copy.start()
            bias_copy.start()

        for copy in small_copies:
            copy.start()
        finish.append((quarter, whole_copy, last_copy, bias_copy, small_copies))
    for quarter, whole_copy, last_copy, bias_copy, small_copies in finish:
        @pl.when(quarter < full)
        def _():
            whole_copy.wait()

        @pl.when(quarter == full)
        def _():
            last_copy.wait()
            bias_copy.wait()

        for copy in small_copies:
            copy.wait()


def shards(
    grid_input, w_stem, b_stem, w_edge, w_node, src_index, dst_index, counts, mesh_cotangent
):
    rows_here, cols_here, channels = grid_input.shape
    width = w_edge.shape[0]
    bands = lax.axis_size("band")
    columns = lax.axis_size("chip") * 2
    chips = bands * lax.axis_size("chip")
    core = lax.axis_index("core")
    device_count = 2 * chips
    slot_count = src_index.shape[2]
    slots = device_count * slot_count
    half_rows = rows_here // 2
    half_cols = cols_here // 2
    points = half_rows * half_cols
    half_width = width // 2
    node_total = mesh_cotangent.shape[0]
    bf16, f32 = jnp.bfloat16, jnp.float32

    west = lax.ppermute(
        grid_input[:, -1:, :], ("chip", "core"), [(i, (i + 1) % columns) for i in range(columns)]
    )
    north = lax.ppermute(grid_input[-1:], "band", [(i, i + 1) for i in range(bands - 1)])
    corner = lax.ppermute(
        grid_input[-1:, -1:],
        EVERY,
        [
            (i * columns + j, (i + 1) * columns + (j + 1) % columns)
            for i in range(bands - 1)
            for j in range(columns)
        ],
    )
    flat_src = src_index.reshape(device_count, slot_count)
    slot_live = jnp.arange(slot_count, dtype=jnp.int32)[None, :] < counts.reshape(device_count, 1)
    source = jnp.where(slot_live, flat_src, -1)

    steps = slots // TILE
    even, odd, slope, outgoing = pl.pallas_call(
        stem_kernel,
        out_shape=(
            pltpu.HBM((3, half_rows, half_cols, width), bf16),
            pltpu.HBM((3, half_rows + 1, half_cols, width), bf16),
            pltpu.HBM((points, width), f32),
            pltpu.HBM((slots, width), bf16),
        ),
        in_specs=[whole()] * 5 + [whole(pltpu.HBM)] * 2,
        out_specs=(whole(pltpu.HBM),) * 4,
        scratch_shapes=[
            pltpu.VMEM((rows_here, cols_here, channels), bf16),
            pltpu.VMEM((4, width // 128, cols_here + 16, 128), f32),
            pltpu.VMEM((TAPS, channels, width), bf16),
            pltpu.VMEM((TAPS * width, width), bf16),
            pltpu.VMEM((3, half_rows, half_cols, width), bf16),
            pltpu.VMEM((3, half_rows + 1, half_cols, width), bf16),
            pltpu.VMEM((points, width), bf16),
            pltpu.VMEM((points, width), f32),
            pltpu.VMEM((slots, width), bf16),
            pltpu.SemaphoreType.DMA((4,)),
            pltpu.SemaphoreType.DMA((TAPS,)),
            pltpu.SemaphoreType.DMA((2,)),
            pltpu.SemaphoreType.DMA((points // TILE,)),
            pltpu.SemaphoreType.DMA((steps,)),
        ],
        compiler_params=params(54),
        name="stem",
    )(
        west,
        north,
        corner,
        b_stem.reshape(1, width),
        source.reshape(slots, 1),
        grid_input,
        w_stem,
    )

    incoming = lax.all_to_all(
        outgoing.reshape(device_count, slot_count, width), EVERY, split_axis=0, concat_axis=0, tiled=True
    )
    arrived = incoming.reshape(slots, width)

    patches = pl.pallas_call(
        functools.partial(flip_kernel, channels),
        grid=(TAPS,),
        out_shape=pltpu.HBM((TAPS, width, points), bf16),
        in_specs=[
            pl.BlockSpec((3, half_rows, half_cols, width), lambda t: (0, 0, 0, 0)),
            pl.BlockSpec((3, half_rows + 1, half_cols, width), lambda t: (0, 0, 0, 0)),
        ],
        out_specs=pl.BlockSpec((1, width, points), lambda t: (t, 0, 0)),
        compiler_params=params(56),
        cost_estimate=cost(0, 16 * MIB),
        name="flip",
    )(even, odd)
    grad_agg = right_dot(mesh_cotangent, w_node).astype(bf16)
    dst_flat = dst_index.reshape(slots)

    dst_row = dst_flat.reshape(1, slots)

    def edge_call(side):
        outs = 2 if side else 1
        return pl.pallas_call(
            functools.partial(edge_kernel, side),
            out_shape=(pltpu.HBM((slots, width), bf16),) * outs,
            in_specs=[whole()] * 3 + [whole(pltpu.HBM)],
            out_specs=(whole(pltpu.HBM),) * outs,
            scratch_shapes=[pltpu.VMEM((slots, width), bf16)] * (1 + outs)
            + [pltpu.VMEM((width, width), bf16)]
            + [pltpu.SemaphoreType.DMA((2,)), pltpu.SemaphoreType.DMA((outs, 2))],
            compiler_params=params(40),
            cost_estimate=cost(4 * slots * width * width, 8 * MIB),
            name="edge_side" if side else "edge_back",
        )(w_edge, dst_row, grad_agg, arrived)

    (back,) = edge_call(False)

    returned = lax.all_to_all(
        back.reshape(device_count, slot_count, width), EVERY, split_axis=0, concat_axis=0, tiled=True
    ).reshape(slots, width)

    messages, grad_pre = edge_call(True)
    node_ids = jnp.arange(node_total, dtype=jnp.int32)
    onehot = (node_ids[:, None] == dst_flat[None, :]).astype(bf16)
    aggregate = f32_dot(onehot, messages).astype(bf16)
    mesh_out = f32_dot(aggregate, w_node).astype(bf16)
    grad_node = inner_dot(aggregate, mesh_cotangent).astype(bf16)
    grad_edge = inner_dot(arrived, grad_pre).astype(bf16)
    mesh_out, grad_edge, grad_node = lax.optimization_barrier((mesh_out, grad_edge, grad_node))

    blocks = TAPS + 2
    band, chip = lax.axis_index("band"), lax.axis_index("chip")
    up = band // LINE
    where = jnp.where(
        core == 0, jnp.stack([core, 1 - core, chip, up]), jnp.stack([core, 1 - core, up, chip])
    )
    depth = width // LINE
    source_row = source.reshape(1, slots)
    quarter_shape = (blocks, depth, half_width)
    quarters = pl.pallas_call(
        gradients_kernel,
        out_shape=(jax.ShapeDtypeStruct(quarter_shape, bf16),) * (2 * LINE),
        in_specs=[whole(pltpu.SMEM), whole()] + [whole(pltpu.HBM)] * 5,
        out_specs=(whole(pl.ANY),) * (2 * LINE),
        scratch_shapes=[
            pltpu.VMEM((slots, width), bf16),
            pltpu.VMEM((points, width), f32),
            pltpu.VMEM((points, width), bf16),
            pltpu.VMEM((TAPS, width, points), bf16),
            pltpu.VMEM((2, width, width), bf16),
            pltpu.VMEM((2, blocks, width, half_width), bf16),
            pltpu.SemaphoreType.DMA((2,)),
            pltpu.SemaphoreType.DMA((TAPS,)),
            pltpu.SemaphoreType.DMA((2,)),
            pltpu.SemaphoreType.DMA((2, LINE)),
        ],
        compiler_params=params(51),
        name="gradients",
    )(where, source_row, returned, slope, grad_edge, grad_node, patches)

    sent, kept = quarters[:LINE], quarters[LINE:]
    steps_out = ORDER[:-1]
    received = [core_swap(array) for array in sent[:-1]]
    chip_sums = [
        (one.astype(f32) + other.astype(f32)).astype(bf16) for one, other in zip(kept, received)
    ]
    arrived_parts = [
        lax.ppermute(chip_sum, EVERY, line_pairs(step)) for step, chip_sum in zip(steps_out, chip_sums)
    ]
    sent_own, chip_sums[-1] = lax.optimization_barrier((sent[-1], chip_sums[-1]))
    received_own = core_swap(sent_own)
    part = (chips // LINE, blocks, 16, 128)
    line_sum = pl.pallas_call(
        line_sum_kernel,
        out_shape=jax.ShapeDtypeStruct(part, bf16),
        in_specs=[whole()] * 5,
        out_specs=whole(),
        compiler_params=params(16),
        name="line_sum",
    )(kept[-1], received_own, *arrived_parts)
    planes = plane_groups()
    pieces = lax.all_to_all(
        line_sum, EVERY, split_axis=0, concat_axis=0, tiled=True, axis_index_groups=planes
    )
    summed = jnp.sum(pieces.astype(f32), axis=0).astype(bf16)
    mine = lax.all_to_all(
        jnp.broadcast_to(summed[None], part), EVERY, split_axis=0, concat_axis=0, tiled=True,
        axis_index_groups=planes,
    )
    steps_out = (2, 3, 1)
    held = [lax.ppermute(mine, EVERY, line_pairs(step)) for step in steps_out]
    out_shape = (
        pltpu.HBM((TAPS, channels, width), f32),
        pltpu.HBM((1, width), f32),
        pltpu.HBM((width, width), f32),
        pltpu.HBM((width, width), f32),
    )

    def final(steps, pieces, before):
        count = len(pieces)
        return pl.pallas_call(
            functools.partial(final_kernel, steps),
            out_shape=out_shape,
            in_specs=[whole(pltpu.SMEM)] + [whole()] * count + [whole(pltpu.HBM)] * len(before),
            out_specs=(whole(pltpu.HBM),) * 4,
            scratch_shapes=[
                pltpu.VMEM((count, blocks, depth, half_width), f32),
                pltpu.VMEM((2, TAPS, channels % depth, half_width), f32),
                pltpu.VMEM((2, 1, half_width), f32),
                pltpu.SemaphoreType.DMA((count,)),
                pltpu.SemaphoreType.DMA((count, 2)),
                pltpu.SemaphoreType.DMA((count,)),
            ],
            input_output_aliases={1 + count + i: i for i in range(len(before))},
            compiler_params=params(26),
            cost_estimate=cost(0, 2 * MIB * count),
            name="final_own" if len(before) == 0 else "final_line",
        )(where, *pieces, *before)

    results = final((0,), [mine, core_swap(mine)], ())
    held[0], *results = lax.optimization_barrier((held[0], *results))
    others = [core_swap(held[0]), core_swap(held[1])]
    last, others[0] = lax.optimization_barrier((held[2], others[0]))
    others.append(core_swap(last))
    pieces = [array for pair in zip(held, others) for array in pair]
    results = final(steps_out, pieces, results)
    grad_stem, grad_bias, out_edge, out_node = results
    return (mesh_out, grad_stem, grad_bias.reshape(width), out_edge, out_node)


def solution(mesh):
    bands, columns = mesh.devices.shape
    fine = Mesh(mesh.devices.reshape(bands, columns // 2, 2), EVERY)
    in_specs = (
        P("band", ("chip", "core"), None),
        P(),
        P(),
        P(),
        P(),
        P(EVERY, None, None),
        P(EVERY, None, None),
        P(EVERY, None),
        P(EVERY, None),
    )
    out_specs = (P(EVERY, None), P(), P(), P(), P())
    return jax.shard_map(shards, mesh=fine, in_specs=in_specs, out_specs=out_specs, check_vma=False)
```

```python
import functools
import itertools

import jax
import jax.numpy as jnp
from jax import lax
from jax.experimental import pallas as pl
from jax.experimental.pallas import tpu as pltpu
from jax.sharding import Mesh, PartitionSpec as P

EVERY = ("band", "chip", "core")
TAPS = 9
LINE = 4
ORDER = (1, 3, 2, 0)
MIB = 1024 * 1024
TILE = 512


def f32_dot(first, second):
    return jnp.dot(first, second, preferred_element_type=jnp.float32)


def inner_dot(first, second):
    return lax.dot_general(
        first, second, (((0,), (0,)), ((), ())), preferred_element_type=jnp.float32
    )


def right_dot(first, second):
    return lax.dot_general(
        first, second, (((1,), (1,)), ((), ())), preferred_element_type=jnp.float32
    )


def core_swap(array):
    return lax.ppermute(array, "core", [(0, 1), (1, 0)])


def device_number(y, z, x, core):
    return ((y * LINE + z) * LINE + x) * 2 + core


def line_pairs(step):
    pairs = []
    for y, z, x in itertools.product(range(LINE), repeat=3):
        pairs.append((device_number(y, z, x, 0), device_number(y, z, (x + step) % LINE, 0)))
        pairs.append((device_number(y, z, x, 1), device_number((y + step) % LINE, z, x, 1)))
    return pairs


def plane_groups():
    planes = []
    for fixed in range(LINE):
        rest = list(itertools.product(range(LINE), repeat=2))
        planes.append([device_number(y, z, fixed, 0) for y, z in rest])
        planes.append([device_number(fixed, z, x, 1) for x, z in rest])
    return planes


def whole(memory=pltpu.VMEM):
    return pl.BlockSpec(memory_space=memory)


def params(mib):
    return pltpu.CompilerParams(vmem_limit_bytes=mib * MIB)


def cost(flops, moved):
    return pl.CostEstimate(flops=int(flops), bytes_accessed=int(moved), transcendentals=0)


def rows_at(number, size=TILE):
    return pl.ds(pl.multiple_of(number * size, size), size)


def unrolled(count):
    return pl.loop(0, count, unroll=True)


def stem_kernel(
    west_ref, north_ref, corner_ref, bias_ref, source_ref,
    grid_hbm, w_hbm, even_hbm, odd_hbm, slope_hbm, out_hbm,
    grid, wide, raw, weights, even, odd, latent, slope, out, in_sems, w_sems, out_sems, slope_sems, row_sems,
):
    rows, cols, channels = grid.shape
    half_rows, half_cols = rows // 2, cols // 2
    width = even.shape[-1]
    chunks = in_sems.shape[0]
    per_chunk = rows // chunks
    bf16 = jnp.bfloat16

    loads = [
        pltpu.make_async_copy(
            grid_hbm.at[rows_at(chunk, per_chunk)], grid.at[rows_at(chunk, per_chunk)], in_sems.at[chunk]
        )
        for chunk in range(chunks)
    ]
    w_loads = [
        pltpu.make_async_copy(w_hbm.at[tap], raw.at[tap], w_sems.at[tap]) for tap in range(TAPS)
    ]
    for copy in loads:
        copy.start()

    gap = channels // 16 * 16
    for tap in range(TAPS):
        weights[tap * width + gap : (tap + 1) * width] = jnp.zeros((width - gap, width), bf16)
    wide[...] = jnp.zeros_like(wide)
    edge = 8

    lanes = wide.shape[-1]

    def phases(slot, columns, west, target, line):
        columns, west = columns.astype(jnp.float32), west.astype(jnp.float32)
        for number in range(width // lanes):
            here = slice(number * lanes, min((number + 1) * lanes, channels))
            held = wide.at[slot, number]
            held[edge : edge + cols, : here.stop - here.start] = columns[:, here]
            held[edge - 1 : edge, : here.stop - here.start] = west[:, here]
            for tap in range(3):
                taken = wide[slot, number, pl.ds(edge - 1 + tap, half_cols, stride=2), :]
                target[tap, line, :, number * lanes : (number + 1) * lanes] = taken.astype(bf16)

    phases(0, north_ref[0], corner_ref[0], odd, 0)
    slots_wide = wide.shape[0]
    for chunk in range(chunks):
        loads[chunk].wait()
        if chunk == chunks - 2:
            for copy in w_loads:
                copy.start()

        @unrolled(per_chunk // slots_wide)
        def _(step):
            first = chunk * per_chunk + slots_wide * step
            pair = chunk * (per_chunk // 2) + (slots_wide // 2) * step
            for slot in range(slots_wide):
                target = odd if slot % 2 else even
                phases(
                    slot, grid[first + slot], west_ref[first + slot], target,
                    pair + slot // 2 + slot % 2,
                )

    phase_copies = [
        pltpu.make_async_copy(even, even_hbm, out_sems.at[0]),
        pltpu.make_async_copy(odd, odd_hbm, out_sems.at[1]),
    ]
    for tap in range(TAPS):
        w_loads[tap].wait()
        weights[tap * width : tap * width + channels] = raw[tap]
    for copy in phase_copies:
        copy.start()

    tile_rows = TILE // half_cols
    points = latent.shape[0]

    def slope_copy(step):
        here = rows_at(step)
        return pltpu.make_async_copy(slope.at[here], slope_hbm.at[here], slope_sems.at[step])

    def row_copy(step):
        here = rows_at(step)
        return pltpu.make_async_copy(out.at[here], out_hbm.at[here], row_sems.at[step])

    @unrolled(points // TILE)
    def _(step):
        pieces = []
        for row_tap in range(3):
            for col_tap in range(3):
                first = step * tile_rows + (row_tap // 2)
                held = even if row_tap == 1 else odd
                pieces.append(held[col_tap, pl.ds(first, tile_rows)].reshape(TILE, width))
        pre = f32_dot(jnp.concatenate(pieces, axis=1), weights[...]) + bias_ref[...]
        sigmoid = jax.nn.sigmoid(pre)
        here = rows_at(step)
        slope[here] = sigmoid * (1.0 + pre * (1.0 - sigmoid))
        latent[here] = (pre * sigmoid).astype(bf16)
        slope_copy(step).start()

    @unrolled(out.shape[0] // TILE)
    def _(step):
        here = rows_at(step)
        point = lax.broadcasted_iota(jnp.int32, (TILE, points), 1)
        pick = jnp.where(point == source_ref[here], 1.0, 0.0).astype(bf16)
        out[here] = f32_dot(pick, latent[...]).astype(bf16)
        row_copy(step).start()

    for copy in phase_copies:
        copy.wait()

    @pl.loop(0, points // TILE)
    def _(step):
        slope_copy(step).wait()

    @pl.loop(0, out.shape[0] // TILE)
    def _(step):
        row_copy(step).wait()


def flip_kernel(channels, even_ref, odd_ref, out_ref):
    number = pl.program_id(0)
    row_tap = number // 3
    col_tap = number % 3
    half_rows, half_cols, width = even_ref.shape[1:]

    def write(values):
        flipped = values.reshape(half_rows * half_cols, width).T
        line = lax.broadcasted_iota(jnp.int32, flipped.shape, 0)
        ones = (line == channels) & (number == 0)
        out_ref[0] = jnp.where(ones, 1.0, flipped.astype(jnp.float32)).astype(jnp.bfloat16)

    @pl.when(row_tap == 1)
    def _():
        write(even_ref[col_tap])

    @pl.when(row_tap != 1)
    def _():
        write(odd_ref[col_tap, pl.ds(row_tap // 2, half_rows)])


def edge_kernel(side, w_ref, dst_ref, agg_ref, rows_hbm, *refs):
    outs = 2 if side else 1
    placed, (rows, *kept) = refs[:outs], refs[outs : 2 * outs + 1]
    flipped_ref, in_sems, out_sems = refs[2 * outs + 1 :]
    nodes = agg_ref.shape[0]
    tiles = in_sems.shape[0]
    tile = rows.shape[0] // tiles
    bf16 = jnp.bfloat16

    def load(step):
        here = rows_at(step, tile)
        return pltpu.make_async_copy(rows_hbm.at[here], rows.at[here], in_sems.at[step])

    def stores(step):
        here = rows_at(step, tile)
        return [
            pltpu.make_async_copy(kept[i].at[here], placed[i].at[here], out_sems.at[i, step])
            for i in range(outs)
        ]

    load(0).start()
    if not side:
        flipped_ref[...] = w_ref[...].T

    @unrolled(tiles)
    def _(step):
        here = rows_at(step, tile)
        node = lax.broadcasted_iota(jnp.int32, (nodes, tile), 0)
        pick = jnp.where(node == dst_ref[:, here], 1.0, 0.0).astype(bf16)
        grad_msg = inner_dot(pick, agg_ref[...])
        load(step).wait()

        @pl.when(step + 1 < tiles)
        def _():
            load(step + 1).start()

        pre = f32_dot(rows[here], w_ref[...])
        sigmoid = jax.nn.sigmoid(pre)
        grad_pre = (grad_msg * (sigmoid * (1.0 + pre * (1.0 - sigmoid)))).astype(bf16)
        if side:
            kept[0][here] = (pre * sigmoid).astype(bf16)
            kept[1][here] = grad_pre
        else:
            kept[0][here] = f32_dot(grad_pre, flipped_ref[...]).astype(bf16)
        for copy in stores(step):
            copy.start()

    for step in range(tiles):
        for copy in stores(step):
            copy.wait()


def quarter_of(spot, step):
    return lax.rem(spot + step + LINE, LINE)


def gradients_kernel(
    where_ref, source_ref, returned_hbm, slope_hbm, edge_hbm, node_hbm, patches_hbm,
    *refs,
):
    placed = (refs[:LINE], refs[LINE : 2 * LINE])
    (
        returned, slope, stemout, patches, smalls, out, before_sems, patch_sems, small_sems, out_sems,
    ) = refs[2 * LINE :]
    half_width = out.shape[3]
    depth = out.shape[2] // LINE
    points, width = stemout.shape
    slots = returned.shape[0]
    bf16 = jnp.bfloat16
    before = [
        pltpu.make_async_copy(returned_hbm, returned, before_sems.at[0]),
        pltpu.make_async_copy(slope_hbm, slope, before_sems.at[1]),
    ]
    patch_loads = [
        pltpu.make_async_copy(patches_hbm.at[tap], patches.at[tap], patch_sems.at[tap])
        for tap in range(TAPS)
    ]
    small_loads = [
        pltpu.make_async_copy(placed, smalls.at[number], small_sems.at[number])
        for number, placed in enumerate((edge_hbm, node_hbm))
    ]

    def stores(part):
        copies = []
        for slot in range(LINE):
            quarter = quarter_of(where_ref[3 - part], ORDER[slot])
            copies.append(
                pltpu.make_async_copy(out.at[part, :, pl.ds(pl.multiple_of(quarter * depth, depth), depth)], placed[part][slot], out_sems.at[part, slot])
            )
        return copies

    def finish(block, part, values):
        out[part, block] = values.astype(bf16)

    def columns(part):
        return pl.ds(pl.multiple_of(where_ref[1 - part] * half_width, half_width), half_width)

    for copy in before:
        copy.start()
    for copy in before:
        copy.wait()
    for copy in patch_loads + small_loads:
        copy.start()

    @unrolled(points // TILE)
    def _(tile):
        here = rows_at(tile)
        point = lax.broadcasted_iota(jnp.int32, (TILE, slots), 0) + tile * TILE
        pick = jnp.where(point == source_ref[...], 1.0, 0.0).astype(bf16)
        grad_latent = f32_dot(pick, returned[...])
        stemout[here] = (grad_latent * slope[here]).astype(bf16)

    for part in range(2):
        for tap in range(TAPS):
            if part == 0 and tap in (0, TAPS // 2):
                for copy in patch_loads[tap : TAPS // 2 if tap == 0 else TAPS]:
                    copy.wait()
            finish(tap, part, f32_dot(patches[tap], stemout[:, columns(part)]))
        for number in range(2):
            if part == 0:
                small_loads[number].wait()
            finish(TAPS + number, part, smalls[number, :, columns(part)])
        for copy in stores(part):
            copy.start()
    for part in range(2):
        for copy in stores(part):
            copy.wait()


def line_sum_kernel(kept_ref, received_ref, one_ref, two_ref, three_ref, out_ref):
    for piece in range(out_ref.shape[0]):
        here = (slice(None), pl.ds(piece // 2 * 16, 16), pl.ds(piece % 2 * 128, 128))
        total = kept_ref[here].astype(jnp.float32)
        for ref in (received_ref, one_ref, two_ref, three_ref):
            total = total + ref[here].astype(jnp.float32)
        out_ref[piece] = total.astype(out_ref.dtype)


def final_kernel(steps, where_ref, *refs):
    held = refs[: 2 * len(steps)]
    stem_hbm, bias_hbm, edge_hbm, node_hbm, blocks, last, bias, stem_sems, small_sems, bias_sems = refs[-10:]
    channels = stem_hbm.shape[1]
    depth, half_width = blocks.shape[2:]
    full = channels // depth
    spare = channels - full * depth
    finish = []
    for index, ref in enumerate(held):
        part = index % 2
        quarter = quarter_of(where_ref[2 + part], -steps[index // 2])
        half = where_ref[part]
        rows = pl.ds(pl.multiple_of(quarter * depth, depth), depth)
        columns = pl.ds(pl.multiple_of(half * half_width, half_width), half_width)
        for piece in range(ref.shape[0]):
            row, lane = piece // 2 * 16, piece % 2 * 128
            blocks[index, :, row : row + 16, lane : lane + 128] = ref[piece].astype(jnp.float32)
        whole_copy = pltpu.make_async_copy(
            blocks.at[index, pl.ds(0, TAPS)], stem_hbm.at[:, rows, columns], stem_sems.at[index]
        )
        last_copy = pltpu.make_async_copy(
            last.at[part], stem_hbm.at[:, pl.ds(full * depth, spare), columns], stem_sems.at[index]
        )
        bias_copy = pltpu.make_async_copy(bias.at[part], bias_hbm.at[:, columns], bias_sems.at[index])
        small_copies = [
            pltpu.make_async_copy(
                blocks.at[index, TAPS + number], placed.at[rows, columns], small_sems.at[index, number]
            )
            for number, placed in enumerate((edge_hbm, node_hbm))
        ]

        @pl.when(quarter < full)
        def _():
            whole_copy.start()

        @pl.when(quarter == full)
        def _():
            last[part] = blocks[index, :TAPS, :spare]
            bias[part] = blocks[index, 0, spare : spare + 1]
            last_copy.start()
            bias_copy.start()

        for copy in small_copies:
            copy.start()
        finish.append((quarter, whole_copy, last_copy, bias_copy, small_copies))
    for quarter, whole_copy, last_copy, bias_copy, small_copies in finish:
        @pl.when(quarter < full)
        def _():
            whole_copy.wait()

        @pl.when(quarter == full)
        def _():
            last_copy.wait()
            bias_copy.wait()

        for copy in small_copies:
            copy.wait()


def shards(
    grid_input, w_stem, b_stem, w_edge, w_node, src_index, dst_index, counts, mesh_cotangent
):
    rows_here, cols_here, channels = grid_input.shape
    width = w_edge.shape[0]
    bands = lax.axis_size("band")
    columns = lax.axis_size("chip") * 2
    chips = bands * lax.axis_size("chip")
    core = lax.axis_index("core")
    device_count = 2 * chips
    slot_count = src_index.shape[2]
    slots = device_count * slot_count
    half_rows = rows_here // 2
    half_cols = cols_here // 2
    points = half_rows * half_cols
    half_width = width // 2
    node_total = mesh_cotangent.shape[0]
    bf16, f32 = jnp.bfloat16, jnp.float32

    west = lax.ppermute(
        grid_input[:, -1:, :], ("chip", "core"), [(i, (i + 1) % columns) for i in range(columns)]
    )
    north = lax.ppermute(grid_input[-1:], "band", [(i, i + 1) for i in range(bands - 1)])
    corner = lax.ppermute(
        grid_input[-1:, -1:],
        EVERY,
        [
            (i * columns + j, (i + 1) * columns + (j + 1) % columns)
            for i in range(bands - 1)
            for j in range(columns)
        ],
    )
    flat_src = src_index.reshape(device_count, slot_count)
    slot_live = jnp.arange(slot_count, dtype=jnp.int32)[None, :] < counts.reshape(device_count, 1)
    source = jnp.where(slot_live, flat_src, -1)

    steps = slots // TILE
    even, odd, slope, outgoing = pl.pallas_call(
        stem_kernel,
        out_shape=(
            pltpu.HBM((3, half_rows, half_cols, width), bf16),
            pltpu.HBM((3, half_rows + 1, half_cols, width), bf16),
            pltpu.HBM((points, width), f32),
            pltpu.HBM((slots, width), bf16),
        ),
        in_specs=[whole()] * 5 + [whole(pltpu.HBM)] * 2,
        out_specs=(whole(pltpu.HBM),) * 4,
        scratch_shapes=[
            pltpu.VMEM((rows_here, cols_here, channels), bf16),
            pltpu.VMEM((4, width // 128, cols_here + 16, 128), f32),
            pltpu.VMEM((TAPS, channels, width), bf16),
            pltpu.VMEM((TAPS * width, width), bf16),
            pltpu.VMEM((3, half_rows, half_cols, width), bf16),
            pltpu.VMEM((3, half_rows + 1, half_cols, width), bf16),
            pltpu.VMEM((points, width), bf16),
            pltpu.VMEM((points, width), f32),
            pltpu.VMEM((slots, width), bf16),
            pltpu.SemaphoreType.DMA((4,)),
            pltpu.SemaphoreType.DMA((TAPS,)),
            pltpu.SemaphoreType.DMA((2,)),
            pltpu.SemaphoreType.DMA((points // TILE,)),
            pltpu.SemaphoreType.DMA((steps,)),
        ],
        compiler_params=params(54),
        name="stem",
    )(
        west,
        north,
        corner,
        b_stem.reshape(1, width),
        source.reshape(slots, 1),
        grid_input,
        w_stem,
    )

    incoming = lax.all_to_all(
        outgoing.reshape(device_count, slot_count, width), EVERY, split_axis=0, concat_axis=0, tiled=True
    )
    arrived = incoming.reshape(slots, width)

    patches = pl.pallas_call(
        functools.partial(flip_kernel, channels),
        grid=(TAPS,),
        out_shape=pltpu.HBM((TAPS, width, points), bf16),
        in_specs=[
            pl.BlockSpec((3, half_rows, half_cols, width), lambda t: (0, 0, 0, 0)),
            pl.BlockSpec((3, half_rows + 1, half_cols, width), lambda t: (0, 0, 0, 0)),
        ],
        out_specs=pl.BlockSpec((1, width, points), lambda t: (t, 0, 0)),
        compiler_params=params(56),
        cost_estimate=cost(0, 16 * MIB),
        name="flip",
    )(even, odd)
    grad_agg = right_dot(mesh_cotangent, w_node).astype(bf16)
    dst_flat = dst_index.reshape(slots)

    dst_row = dst_flat.reshape(1, slots)

    def edge_call(side):
        outs = 2 if side else 1
        return pl.pallas_call(
            functools.partial(edge_kernel, side),
            out_shape=(pltpu.HBM((slots, width), bf16),) * outs,
            in_specs=[whole()] * 3 + [whole(pltpu.HBM)],
            out_specs=(whole(pltpu.HBM),) * outs,
            scratch_shapes=[pltpu.VMEM((slots, width), bf16)] * (1 + outs)
            + [pltpu.VMEM((width, width), bf16)]
            + [pltpu.SemaphoreType.DMA((2,)), pltpu.SemaphoreType.DMA((outs, 2))],
            compiler_params=params(40),
            cost_estimate=cost(4 * slots * width * width, 8 * MIB),
            name="edge_side" if side else "edge_back",
        )(w_edge, dst_row, grad_agg, arrived)

    (back,) = edge_call(False)

    returned = lax.all_to_all(
        back.reshape(device_count, slot_count, width), EVERY, split_axis=0, concat_axis=0, tiled=True
    ).reshape(slots, width)

    messages, grad_pre = edge_call(True)
    node_ids = jnp.arange(node_total, dtype=jnp.int32)
    onehot = (node_ids[:, None] == dst_flat[None, :]).astype(bf16)
    aggregate = f32_dot(onehot, messages).astype(bf16)
    mesh_out = f32_dot(aggregate, w_node).astype(bf16)
    grad_node = inner_dot(aggregate, mesh_cotangent).astype(bf16)
    grad_edge = inner_dot(arrived, grad_pre).astype(bf16)
    mesh_out, grad_edge, grad_node = lax.optimization_barrier((mesh_out, grad_edge, grad_node))

    blocks = TAPS + 2
    band, chip = lax.axis_index("band"), lax.axis_index("chip")
    up = band // LINE
    where = jnp.where(
        core == 0, jnp.stack([core, 1 - core, chip, up]), jnp.stack([core, 1 - core, up, chip])
    )
    depth = width // LINE
    source_row = source.reshape(1, slots)
    quarter_shape = (blocks, depth, half_width)
    quarters = pl.pallas_call(
        gradients_kernel,
        out_shape=(jax.ShapeDtypeStruct(quarter_shape, bf16),) * (2 * LINE),
        in_specs=[whole(pltpu.SMEM), whole()] + [whole(pltpu.HBM)] * 5,
        out_specs=(whole(pl.ANY),) * (2 * LINE),
        scratch_shapes=[
            pltpu.VMEM((slots, width), bf16),
            pltpu.VMEM((points, width), f32),
            pltpu.VMEM((points, width), bf16),
            pltpu.VMEM((TAPS, width, points), bf16),
            pltpu.VMEM((2, width, width), bf16),
            pltpu.VMEM((2, blocks, width, half_width), bf16),
            pltpu.SemaphoreType.DMA((2,)),
            pltpu.SemaphoreType.DMA((TAPS,)),
            pltpu.SemaphoreType.DMA((2,)),
            pltpu.SemaphoreType.DMA((2, LINE)),
        ],
        compiler_params=params(49),
        name="gradients",
    )(where, source_row, returned, slope, grad_edge, grad_node, patches)

    sent, kept = quarters[:LINE], quarters[LINE:]
    steps_out = ORDER[:-1]
    received = [core_swap(array) for array in sent[:-1]]
    chip_sums = [
        (one.astype(f32) + other.astype(f32)).astype(bf16) for one, other in zip(kept, received)
    ]
    arrived_parts = [
        lax.ppermute(chip_sum, EVERY, line_pairs(step)) for step, chip_sum in zip(steps_out, chip_sums)
    ]
    sent_own, chip_sums[-1] = lax.optimization_barrier((sent[-1], chip_sums[-1]))
    received_own = core_swap(sent_own)
    part = (chips // LINE, blocks, 16, 128)
    line_sum = pl.pallas_call(
        line_sum_kernel,
        out_shape=jax.ShapeDtypeStruct(part, bf16),
        in_specs=[whole()] * 5,
        out_specs=whole(),
        compiler_params=params(16),
        name="line_sum",
    )(kept[-1], received_own, *arrived_parts)
    planes = plane_groups()
    pieces = lax.all_to_all(
        line_sum, EVERY, split_axis=0, concat_axis=0, tiled=True, axis_index_groups=planes
    )
    summed = jnp.sum(pieces.astype(f32), axis=0).astype(bf16)
    mine = lax.all_to_all(
        jnp.broadcast_to(summed[None], part), EVERY, split_axis=0, concat_axis=0, tiled=True,
        axis_index_groups=planes,
    )
    steps_out = (2, 3, 1)
    held = [lax.ppermute(mine, EVERY, line_pairs(step)) for step in steps_out]
    out_shape = (
        pltpu.HBM((TAPS, channels, width), f32),
        pltpu.HBM((1, width), f32),
        pltpu.HBM((width, width), f32),
        pltpu.HBM((width, width), f32),
    )

    def final(steps, pieces, before):
        count = len(pieces)
        return pl.pallas_call(
            functools.partial(final_kernel, steps),
            out_shape=out_shape,
            in_specs=[whole(pltpu.SMEM)] + [whole()] * count + [whole(pltpu.HBM)] * len(before),
            out_specs=(whole(pltpu.HBM),) * 4,
            scratch_shapes=[
                pltpu.VMEM((count, blocks, depth, half_width), f32),
                pltpu.VMEM((2, TAPS, channels % depth, half_width), f32),
                pltpu.VMEM((2, 1, half_width), f32),
                pltpu.SemaphoreType.DMA((count,)),
                pltpu.SemaphoreType.DMA((count, 2)),
                pltpu.SemaphoreType.DMA((count,)),
            ],
            input_output_aliases={1 + count + i: i for i in range(len(before))},
            compiler_params=params(26),
            cost_estimate=cost(0, 2 * MIB * count),
            name="final_own" if len(before) == 0 else "final_line",
        )(where, *pieces, *before)

    results = final((0,), [mine, core_swap(mine)], ())
    held[0], *results = lax.optimization_barrier((held[0], *results))
    others = [core_swap(held[0]), core_swap(held[1])]
    last, others[0] = lax.optimization_barrier((held[2], others[0]))
    others.append(core_swap(last))
    pieces = [array for pair in zip(held, others) for array in pair]
    results = final(steps_out, pieces, results)
    grad_stem, grad_bias, out_edge, out_node = results
    return (mesh_out, grad_stem, grad_bias.reshape(width), out_edge, out_node)


def solution(mesh):
    bands, columns = mesh.devices.shape
    fine = Mesh(mesh.devices.reshape(bands, columns // 2, 2), EVERY)
    in_specs = (
        P("band", ("chip", "core"), None),
        P(),
        P(),
        P(),
        P(),
        P(EVERY, None, None),
        P(EVERY, None, None),
        P(EVERY, None),
        P(EVERY, None),
    )
    out_specs = (P(EVERY, None), P(), P(), P(), P())
    return jax.shard_map(shards, mesh=fine, in_specs=in_specs, out_specs=out_specs, check_vma=False)
```
